32 devices in a mesh: dp: 2 (over y), fsdp: 16 (over z, x, core).
Axes of the slice: x: 2, y: 2, z: 4, core: 2. Of those that a mesh axis runs over, the one named last changes fastest.
Arguments:
- inputs: bfloat16 [2, 2048, 2048], P('dp', 'fsdp'), may hold values from -6 to 6
- weight: bfloat16 [2048, 6144], P('fsdp', 'dp'), may hold values from -0.125 to 0.125
- gain: float32 [2048], replicated, may hold values from 0.5 to 1.5
- shift: float32 [2048], replicated, may hold values from -1.5 to 1.5
- forget_vec: float32 [2048], replicated, may hold values from -0.8 to 0.8
- reset_vec: float32 [2048], replicated, may hold values from -0.8 to 0.8
- forget_bias: float32 [2048], replicated, may hold values from 3 to 10
- reset_bias: float32 [2048], replicated, may hold values from 0 to 3
- initial: float32 [2, 2048], P('dp'), may hold values from -5 to 5
- resets: int32 [2, 2048], P('dp', 'fsdp'), may hold values from 0 to 1, as said below
- grad_out: bfloat16 [2, 2048, 2048], P('dp', 'fsdp'), may hold values from -6 to 6
Outputs:
- hidden: bfloat16 [2, 2048, 2048], P('dp', 'fsdp')
- grad_inputs: bfloat16 [2, 2048, 2048], P('dp', 'fsdp')
- final_state: float32 [2, 2048], P('dp', 'fsdp')
- grad_weight: float32 [2048, 6144], P('fsdp', 'dp')
- grad_forget_vec: float32 [2048], replicated
- grad_reset_vec: float32 [2048], replicated
- grad_forget_bias: float32 [2048], replicated
- grad_reset_bias: float32 [2048], replicated
- grad_gain: float32 [2048], replicated
- grad_shift: float32 [2048], replicated
The draws below stay inside these ranges and needn't reach their ends.
Inputs may be any that keep to these rules, and one draw needn't show every extreme that they name: `resets`: A 1 marks the first token of a sentence; position 0 of every row is 0. The first 1 of a row lies at position 641 to 768, and exactly at 768 in some row. The last 1 of a row lies at position 1857 or later. After a row's first 1, two consecutive sentence starts lie 128 // 2 to 191 tokens apart.
All inputs are finite; a program needn't handle non-finite values.
Results may differ from the reference program's by a relative error of at most 0.011.
Values may be sent and summed in bfloat16 or wider, within the bound.
No kernel may reach another device: no remote copies, remote signals or barrier semaphores. Data moves between devices by JAX's collectives and lax.ppermute only.
A program may use at most 192 MiB of HBM per device.

```python
import jax
import jax.numpy as jnp
from jax import lax

D = 2048
PROJ = 6144
ROW_LEN = 2048
SENT = 128
LEAD = 768
ROWS = 2


def draw_resets(key, part):
    key = jax.random.fold_in(key, 17)
    first_key, second_key, third_key = jax.random.split(key, 3)
    halfway = SENT // 2
    number = ROW_LEN // halfway + 2
    spacing = jax.random.randint(first_key, (ROWS, number), halfway, SENT + halfway)
    opening = jax.random.randint(second_key, (ROWS, 1), LEAD - SENT + 1, LEAD + 1)
    chosen = jax.random.randint(third_key, (1, 1), 0, ROWS)
    row_ids = jnp.arange(ROWS, dtype=jnp.int32)[:, None]
    opening = jnp.where(row_ids == chosen, LEAD, opening)
    preceding = jnp.concatenate([jnp.zeros((ROWS, 1), jnp.int32), jnp.cumsum(spacing, axis=1)[:, :-1]], axis=1)
    starting = opening + preceding
    positions = jnp.arange(ROW_LEN, dtype=jnp.int32)
    marked = jnp.any(starting[:, :, None] == positions[None, None, :], axis=1)
    return marked.astype(jnp.int32)


def draw_forget_bias(key, part):
    key = jax.random.fold_in(key, 29)
    pick_key, fast_key, slow_key = jax.random.split(key, 3)
    share = jax.random.uniform(pick_key, (D,), jnp.float32)
    fast = jax.random.uniform(fast_key, (D,), jnp.float32, 3.0, 5.0)
    slow = jax.random.uniform(slow_key, (D,), jnp.float32, 7.0, 10.0)
    return jnp.where(share < 0.5, fast, slow)


def draw_grad_out(key, part):
    key = jax.random.fold_in(key, 41)
    lasting_key, noise_key = jax.random.split(key, 2)
    lasting = 0.9 * jax.random.normal(lasting_key, (ROWS, 1, D), jnp.float32)
    noise = 0.5 * jax.random.normal(noise_key, (ROWS, ROW_LEN, D), jnp.float32)
    return jnp.clip(lasting + noise, -6.0, 6.0).astype(jnp.bfloat16)


def shard_levels(key, extent, cuts, smallest, high):
    def one(axis_at, shards_of):
        steps = jax.random.uniform(jax.random.fold_in(jax.random.fold_in(key, 6), axis_at), (shards_of,), jnp.float32, smallest / len(cuts), high / len(cuts))
        return jnp.repeat(jnp.exp(steps), extent[axis_at] // shards_of).reshape((-1,) + (1,) * (len(extent) - axis_at - 1))

    loudness = one(*cuts[0])
    for cut in cuts[1:]:
        loudness = loudness * one(*cut)
    return loudness


def scatter_about(rng, shape, scale, reach, cuts=(), kind=jnp.bfloat16):
    result = jax.random.normal(rng, shape, jnp.float32) * scale
    if len(cuts) > 0:
        result = shard_levels(rng, shape, cuts, -0.22, 0.18) * result
    return jnp.clip(result, min=-reach, max=reach).astype(kind)


def setup_inputs(seed: int = 0) -> dict:
    streams_of = jax.random.split(jax.random.key(seed), 12)
    inputs = scatter_about(streams_of[0], (ROWS, ROW_LEN, D), 1.0, 6.0, ((0, 2), (1, 16)))
    weight = scatter_about(streams_of[1], (D, PROJ), D ** -0.5, 0.125, ((0, 16), (1, 2)))
    gain = jnp.clip(1.0 + 0.1 * jax.random.normal(streams_of[2], (D,), jnp.float32), 0.5, 1.5)
    shift = scatter_about(streams_of[3], (D,), 0.3, 1.5, (), jnp.float32)
    forget_vec = jnp.clip(jax.random.uniform(streams_of[4], (D,), jnp.float32, -0.8, 0.8), -0.8, 0.8)
    reset_vec = jnp.clip(jax.random.uniform(streams_of[5], (D,), jnp.float32, -0.8, 0.8), -0.8, 0.8)
    forget_bias = draw_forget_bias(jax.random.fold_in(streams_of[11], 71), 0)
    reset_bias = jnp.clip(jax.random.uniform(streams_of[7], (D,), jnp.float32, 0.0, 3.0), 0.0, 3.0)
    initial = scatter_about(streams_of[8], (ROWS, D), 1.0, 5.0, ((0, 2),), jnp.float32)
    resets = draw_resets(jax.random.fold_in(streams_of[11], 71), 0)
    grad_out = draw_grad_out(jax.random.fold_in(streams_of[11], 71), 0)
    return dict(inputs=inputs, weight=weight, gain=gain, shift=shift, forget_vec=forget_vec, reset_vec=reset_vec, forget_bias=forget_bias, reset_bias=reset_bias, initial=initial, resets=resets, grad_out=grad_out)


epsilon = 1e-05

@jax.custom_vjp
def low(v):
    return lax.optimization_barrier(v.astype(jnp.bfloat16)).astype(jnp.float32)

@jax.custom_vjp
def low_back(v):
    return v

def low_keep(v):
    return (low(v), None)

def low_pass(kept, grad):
    return (grad,)

def back_keep(v):
    return (v, None)

def back_low(kept, grad):
    return (low(grad),)
low.defvjp(low_keep, low_pass)
low_back.defvjp(back_keep, back_low)

def layer_norm(values, gain_vec, shift_vec):
    average = lax.optimization_barrier(jnp.mean(values, axis=-1, keepdims=True))
    centred = values - average
    variance = lax.optimization_barrier(jnp.mean(centred * centred, axis=-1, keepdims=True))
    return centred * lax.rsqrt(variance + epsilon) * gain_vec + shift_vec

def recurrence(begin_state, candidate, forget_in, reset_in, highway, keeping, forget_vec, reset_vec, forget_bias, reset_bias):

    def advance(cell_prev, sliced):
        cand_now, forget_now, reset_now, input_now, keep_now = sliced
        previous = cell_prev * keep_now
        forget_gate = jax.nn.sigmoid(forget_now + forget_vec * previous + forget_bias)
        cell_now = forget_gate * previous + (1.0 - forget_gate) * cand_now
        reset_gate = jax.nn.sigmoid(reset_now + reset_vec * previous + reset_bias)
        output = reset_gate * cell_now + (1.0 - reset_gate) * input_now
        return (cell_now, output)
    last_cell, outputs = lax.scan(advance, begin_state, (candidate, forget_in, reset_in, highway, keeping))
    return (outputs, last_cell)

def forward(inputs, weight, gain, shift, forget_vec, reset_vec, forget_bias, reset_bias, initial, keeping):
    features = inputs.shape[-1]
    normed = low(layer_norm(inputs, gain, shift))
    projected = low_back(jnp.einsum('gtd,de->gte', normed, weight, precision=lax.Precision.HIGHEST))
    timed = jnp.transpose(projected, (1, 0, 2))
    highway = jnp.transpose(inputs, (1, 0, 2))
    keep_timed = jnp.transpose(keeping, (1, 0))[:, :, None]
    outputs, last_cell = recurrence(initial, timed[:, :, :features], timed[:, :, features:2 * features], timed[:, :, 2 * features:], highway, keep_timed, forget_vec, reset_vec, forget_bias, reset_bias)
    return (jnp.transpose(outputs, (1, 0, 2)), last_cell)

def reference(inputs, weight, gain, shift, forget_vec, reset_vec, forget_bias, reset_bias, initial, resets, grad_out):
    per_group = 2
    groups = ROWS // per_group
    weight_full = weight.astype(jnp.float32)
    keep_all = (1 - resets).astype(jnp.float32)

    def one_group(totals, position):
        offset = (position * per_group).astype(jnp.int32)
        rows_in = lax.dynamic_slice_in_dim(inputs, offset, per_group, 0).astype(jnp.float32)
        grad_rows = lax.dynamic_slice_in_dim(grad_out, offset, per_group, 0).astype(jnp.float32)
        start_rows = lax.dynamic_slice_in_dim(initial, offset, per_group, 0)
        keep_rows = lax.dynamic_slice_in_dim(keep_all, offset, per_group, 0)

        def run(values, weights, gain_vec, shift_vec, forget_v, reset_v, forget_b, reset_b):
            return forward(values, weights, gain_vec, shift_vec, forget_v, reset_v, forget_b, reset_b, start_rows, keep_rows)
        outputs, pull, last_cell = jax.vjp(run, rows_in, weight_full, gain, shift, forget_vec, reset_vec, forget_bias, reset_bias, has_aux=True)
        grads = pull(grad_rows)
        totals = tuple((total + piece for total, piece in zip(totals, grads[1:])))
        return (totals, (outputs.astype(jnp.bfloat16), grads[0].astype(jnp.bfloat16), last_cell))
    vector_zero = jnp.zeros((D,), jnp.float32)
    starting = (jnp.zeros((D, 3 * D), jnp.float32), vector_zero, vector_zero, vector_zero, vector_zero, vector_zero, vector_zero)
    totals, (outputs, grad_in, finals) = lax.scan(one_group, starting, jnp.arange(groups, dtype=jnp.int32))
    hidden = outputs.reshape(ROWS, ROW_LEN, D)
    grad_inputs = grad_in.reshape(ROWS, ROW_LEN, D)
    final_state = finals.reshape(ROWS, D)
    grad_weight, grad_gain, grad_shift, grad_forget_vec, grad_reset_vec, grad_forget_bias, grad_reset_bias = totals
    return (hidden, grad_inputs, final_state, grad_weight, grad_forget_vec, grad_reset_vec, grad_forget_bias, grad_reset_bias, grad_gain, grad_shift)
```

```python
import functools
import math

import jax
import jax.numpy as jnp
from jax import lax
from jax.experimental import pallas as pl
from jax.experimental.pallas import tpu as pltpu
from jax.sharding import PartitionSpec as P

SENT = 128
LEAD = 768
EPSILON = 1e-05
LANES = 128
BLOCK = 128
SPACED = 136
TAIL = 256
UNROLL = 8
f32 = jnp.float32
bf16 = jnp.bfloat16
VMEM = 48 << 20


def spaced(token):
    return token + (SPACED - BLOCK) * (token // BLOCK)


def tiles_of(ref, count):
    return [ref[:, LANES * i : LANES * (i + 1)] for i in range(count)]


def project_kernel(x_ref, w_ref, gain_ref, shift_ref, fb_ref, rb_ref, normed_ref, mean_ref, inv_ref, c_ref, yf_ref, yr_ref):
    x = x_ref[0].astype(f32)
    mean = jnp.mean(x, axis=-1, keepdims=True)
    centred = x - mean
    inv = lax.rsqrt(jnp.mean(centred * centred, axis=-1, keepdims=True) + EPSILON)
    normed = (centred * inv * gain_ref[...] + shift_ref[...]).astype(bf16)
    normed_ref[0] = normed
    mean_ref[0] = mean
    inv_ref[0] = inv
    p = jnp.dot(normed, w_ref[...], preferred_element_type=f32)
    tiles = c_ref.shape[1]
    width = tiles * LANES
    for i in range(tiles):
        at = slice(LANES * i, LANES * (i + 1))
        c_ref[0, i, :BLOCK, :] = p[:, LANES * i : LANES * (i + 1)]
        yf_ref[0, i, :BLOCK, :] = 0.5 * (p[:, width + LANES * i : width + LANES * (i + 1)] + fb_ref[:, at])
        yr_ref[0, i, :BLOCK, :] = 0.5 * (p[:, 2 * width + LANES * i : 2 * width + LANES * (i + 1)] + rb_ref[:, at])


def project(x_all, weight, gain, shift, fb, rb):
    rows, tokens, features = x_all.shape
    width = weight.shape[1] // 3
    tiles = width // LANES
    blocks = tokens // BLOCK
    whole = lambda r, k: (0, 0)
    padded = jax.ShapeDtypeStruct((rows, tiles, blocks * SPACED, LANES), f32)
    padded_spec = pl.BlockSpec((1, tiles, SPACED, LANES), lambda r, k: (r, 0, k, 0))
    column = jax.ShapeDtypeStruct((rows, tokens, 1), f32)
    column_spec = pl.BlockSpec((1, BLOCK, 1), lambda r, k: (r, k, 0))
    return pl.pallas_call(
        project_kernel,
        grid=(rows, blocks),
        in_specs=[
            pl.BlockSpec((1, BLOCK, features), lambda r, k: (r, k, 0)),
            pl.BlockSpec((features, 3 * width), whole),
            pl.BlockSpec((1, features), whole),
            pl.BlockSpec((1, features), whole),
            pl.BlockSpec((1, width), whole),
            pl.BlockSpec((1, width), whole),
        ],
        out_specs=[
            pl.BlockSpec((1, BLOCK, features), lambda r, k: (r, k, 0)),
            column_spec,
            column_spec,
            padded_spec,
            padded_spec,
            padded_spec,
        ],
        out_shape=[jax.ShapeDtypeStruct(x_all.shape, bf16), column, column, padded, padded, padded],
        compiler_params=pltpu.CompilerParams(vmem_limit_bytes=VMEM),
        name="project",
    )(x_all, weight, gain, shift, fb, rb)


def chain_step(refs, hfv, carried, row, next_row, store):
    yf_ref, c_ref, kb_ref, prev_ref = refs
    keep = kb_ref[0, next_row, :]
    out = []
    for i, (y, prev) in enumerate(carried):
        tau = jnp.tanh(y)
        half = 0.5 * c_ref[0, i, row, :]
        mid, gap = 0.5 * prev + half, 0.5 * prev - half
        if store:
            prev_ref[0, i, row, :] = prev
        reach = hfv[i] * keep
        out.append(((yf_ref[0, i, next_row, :] + reach * mid) + (reach * gap) * tau, (keep * mid) + (keep * gap) * tau))
    return out


def begin(refs, hfv, cells, row):
    yf_ref, _, kb_ref, _ = refs
    keep = kb_ref[0, row, :]
    out = []
    for i, cell in enumerate(cells):
        prev = keep * cell
        out.append((yf_ref[0, i, row, :] + hfv[i] * prev, prev))
    return out


def rows_of(token):
    return pl.ds(spaced(token), 1)


def run_chain(refs, hfv, carried, first, count, last):
    def body(j, now):
        for u in range(UNROLL):
            token = first + j * UNROLL + u
            now = chain_step(refs, hfv, now, rows_of(token), rows_of(jnp.minimum(token + 1, last)), True)
        return now

    return lax.fori_loop(0, count // UNROLL, body, carried)


def blocks_kernel(yf_ref, c_ref, kb_ref, hfv_ref, init_ref, seg_ref, lead_ref, end_ref, lead_end_ref, *, early):
    tiles = yf_ref.shape[1]
    blocks = yf_ref.shape[2] // SPACED
    hfv = tiles_of(hfv_ref, tiles)
    seg_refs = (yf_ref, c_ref, kb_ref, seg_ref)
    lead_refs = (yf_ref, c_ref, kb_ref, lead_ref)

    def strided(step):
        return pl.ds(step, blocks, stride=SPACED)

    def seg_step(cells, step, store):
        row = strided(step)
        keep = kb_ref[0, row, :]
        out = []
        for i, cell in enumerate(cells):
            prev = keep * cell
            tau = jnp.tanh(yf_ref[0, i, row, :] + (hfv[i] * keep) * cell)
            half = 0.5 * c_ref[0, i, row, :]
            if store:
                seg_ref[0, i, row, :] = prev
            out.append((0.5 * prev + half) + (0.5 * prev - half) * tau)
        return out

    def run(cells, lead, first, token, count, store):
        def body(j, carried):
            cells, lead = carried
            for u in range(UNROLL):
                at = j * UNROLL + u
                cells = seg_step(cells, first + at, store)
                lead = chain_step(lead_refs, hfv, lead, rows_of(token + at), rows_of(token + at + 1), True)
            return cells, lead

        return lax.fori_loop(0, count // UNROLL, body, (cells, lead))

    def moved(cells):
        return [jnp.concatenate([jnp.zeros((1, LANES), f32), cell[:-1]], axis=0) for cell in cells]

    cells = [jnp.zeros((blocks, LANES), f32) for _ in range(tiles)]
    lead = begin(lead_refs, hfv, tiles_of(init_ref.at[0], tiles), pl.ds(0, 1))
    cells, lead = run(cells, lead, BLOCK - early, 0, early, False)
    cells, lead = run(moved(cells), lead, 0, early, BLOCK, False)
    cells, lead = run(moved(cells), lead, 0, early + BLOCK, BLOCK, True)
    for i in range(tiles):
        end_ref[0, :, LANES * i : LANES * (i + 1)] = cells[i][-1:]
        lead_end_ref[0, :, LANES * i : LANES * (i + 1)] = lead[i][1]


def blocks_forward(yf, c, kb, hfv, init, early):
    rows, tiles, length, _ = yf.shape
    covered = early + 2 * BLOCK
    padded_spec = pl.BlockSpec((1, tiles, length, LANES), lambda r: (r, 0, 0, 0))
    state_spec = pl.BlockSpec((1, 1, tiles * LANES), lambda r: (r, 0, 0))
    state = jax.ShapeDtypeStruct((rows, 1, tiles * LANES), f32)
    return pl.pallas_call(
        functools.partial(blocks_kernel, early=early),
        grid=(rows,),
        in_specs=[
            padded_spec,
            padded_spec,
            pl.BlockSpec((1, length, LANES), lambda r: (r, 0, 0)),
            pl.BlockSpec((1, tiles * LANES), lambda r: (0, 0)),
            state_spec,
        ],
        out_specs=[
            padded_spec,
            pl.BlockSpec((1, tiles, spaced(covered), LANES), lambda r: (r, 0, 0, 0)),
            state_spec,
            state_spec,
        ],
        out_shape=[
            jax.ShapeDtypeStruct(yf.shape, f32),
            jax.ShapeDtypeStruct((rows, tiles, spaced(covered), LANES), f32),
            state,
            state,
        ],
        compiler_params=pltpu.CompilerParams(vmem_limit_bytes=VMEM),
        name="blocks_forward",
    )(yf, c, kb, hfv, init)


def lead_kernel(first_ref, yf_ref, c_ref, kb_ref, hfv_ref, start_ref, lead_ref, prev_ref, prev_out_ref, *, covered, count):
    tiles = yf_ref.shape[1]
    hfv = tiles_of(hfv_ref, tiles)
    refs = (yf_ref, c_ref, kb_ref, prev_out_ref)
    for i in range(tiles):
        prev_out_ref[0, i] = prev_ref[0, i]
        prev_out_ref[0, i, : spaced(covered), :] = lead_ref[0, i]
    first = first_ref[0]
    row = rows_of(first)
    carried = []
    for i, prev in enumerate(tiles_of(start_ref.at[0], tiles)):
        carried.append((yf_ref[0, i, row, :] + hfv[i] * prev, prev))
    run_chain(refs, hfv, carried, first, count, covered + count)


def lead_forward(first, yf, c, kb, hfv, start, lead, prev, covered, count):
    rows, tiles, length, _ = yf.shape
    padded_spec = pl.BlockSpec((1, tiles, length, LANES), lambda r, _: (r, 0, 0, 0))
    return pl.pallas_call(
        functools.partial(lead_kernel, covered=covered, count=count),
        grid_spec=pltpu.PrefetchScalarGridSpec(
            num_scalar_prefetch=1,
            grid=(rows,),
            in_specs=[
                padded_spec,
                padded_spec,
                pl.BlockSpec((1, length, LANES), lambda r, _: (r, 0, 0)),
                pl.BlockSpec((1, tiles * LANES), lambda r, _: (0, 0)),
                pl.BlockSpec((1, 1, tiles * LANES), lambda r, _: (r, 0, 0)),
                pl.BlockSpec((1, tiles, lead.shape[2], LANES), lambda r, _: (r, 0, 0, 0)),
                padded_spec,
            ],
            out_specs=padded_spec,
        ),
        out_shape=jax.ShapeDtypeStruct(yf.shape, f32),
        compiler_params=pltpu.CompilerParams(vmem_limit_bytes=VMEM),
        name="lead_forward",
    )(first, yf, c, kb, hfv, start, lead, prev)


def gates(prev, c, yf, yr, hfv, hrv):
    tau_f = jnp.tanh(yf + hfv * prev)
    tau_r = jnp.tanh(yr + hrv * prev)
    return 0.5 + 0.5 * tau_f, 0.5 - 0.5 * tau_f, 0.5 + 0.5 * tau_r, 0.5 - 0.5 * tau_r


def backward_kernel(
    yf_ref, c_ref, yr_ref, kb_ref, prev_ref, x_ref, g_ref, hfv_ref, hrv_ref, carry_ref,
    gp_ref, hidden_ref, high_ref, sums_ref, final_ref, back_ref,
    a_ref, b_ref, gg_ref, e_ref, omf_ref, dr_ref, d_ref, *, first_block, summed_blocks,
):
    tiles = yf_ref.shape[1]
    blocks = yf_ref.shape[2] // SPACED - first_block
    hfv, hrv = tiles_of(hfv_ref, tiles), tiles_of(hrv_ref, tiles)

    @pl.loop(0, blocks)
    def _(k):
        at = pl.ds(pl.multiple_of((k + first_block) * SPACED, 8), BLOCK)
        out = pl.ds(pl.multiple_of(k * BLOCK, BLOCK), BLOCK)
        token = pl.ds(pl.multiple_of((k + first_block) * BLOCK, BLOCK), BLOCK)
        keep = kb_ref[0, at, :]
        for i in range(tiles):
            prev, c = prev_ref[0, i, at, :], c_ref[0, i, at, :]
            f, omf, gate, omg = gates(prev, c, yf_ref[0, i, at, :], yr_ref[0, i, at, :], hfv[i], hrv[i])
            cell = f * prev + omf * c
            x, g = x_ref[0, i, token, :].astype(f32), g_ref[0, i, token, :].astype(f32)
            hidden_ref[0, i, out, :] = (gate * cell + omg * x).astype(bf16)
            high_ref[0, i, out, :] = (g * omg).astype(bf16)
            gg = g * gate
            dr = gg * omg * (cell - x)
            e = (prev - c) * f * omf
            slope = f + e * (2.0 * hfv[i])
            a_ref[i, out, :] = keep * slope
            b_ref[i, out, :] = keep * (slope * gg + dr * (2.0 * hrv[i]))
            gg_ref[i, out, :] = gg
            e_ref[i, out, :] = e
            omf_ref[i, out, :] = omf
            dr_ref[i, out, :] = dr
            final_ref[0, :, LANES * i : LANES * (i + 1)] = cell[-1:]

    def body(j, carried):
        base = pl.multiple_of((blocks * BLOCK) - UNROLL * (j + 1), UNROLL)
        for u in reversed(range(UNROLL)):
            now = []
            for i, d in enumerate(carried):
                row = pl.ds(base + u, 1)
                d_ref[i, row, :] = d
                now.append(a_ref[i, row, :] * d + b_ref[i, row, :])
            carried = now
        return carried

    carried = lax.fori_loop(0, blocks * BLOCK // UNROLL, body, tiles_of(carry_ref.at[0], tiles))
    for i in range(tiles):
        back_ref[0, :, LANES * i : LANES * (i + 1)] = carried[i]

    sums_ref[...] = jnp.zeros_like(sums_ref)

    @pl.loop(0, summed_blocks)
    def _(k):
        at = pl.ds(pl.multiple_of((k + first_block) * SPACED, 8), BLOCK)
        out = pl.ds(pl.multiple_of(k * BLOCK, BLOCK), BLOCK)
        for i in range(tiles):
            prev = prev_ref[0, i, at, :]
            u = d_ref[i, out, :] + gg_ref[i, out, :]
            df, dr = u * e_ref[i, out, :], dr_ref[i, out, :]
            for m, value in enumerate((u * omf_ref[i, out, :], df, dr)):
                lane = LANES * (m * tiles + i)
                gp_ref[0, out, lane : lane + LANES] = value.astype(bf16)
            for m, value in enumerate((df * prev, dr * prev, df, dr)):
                lane = slice(LANES * i, LANES * (i + 1))
                sums_ref[0, m : m + 1, lane] += jnp.sum(value, axis=0, keepdims=True)


def backward(yf, c, yr, kb, prev, x_own, g_own, hfv, hrv, carry, first_block, summed_blocks):
    rows, tiles, length, _ = yf.shape
    tokens = (length // SPACED - first_block) * BLOCK
    width = tiles * LANES
    padded_spec = pl.BlockSpec((1, tiles, length, LANES), lambda r: (r, 0, 0, 0))
    own_spec = pl.BlockSpec((1, tiles, x_own.shape[2], LANES), lambda r: (r, 0, 0, 0))
    out_spec = pl.BlockSpec((1, tiles, tokens, LANES), lambda r: (r, 0, 0, 0))
    vector_spec = pl.BlockSpec((1, width), lambda r: (0, 0))
    state_spec = pl.BlockSpec((1, 1, width), lambda r: (r, 0, 0))
    state = jax.ShapeDtypeStruct((rows, 1, width), f32)
    own = jax.ShapeDtypeStruct((rows, tiles, tokens, LANES), bf16)
    return pl.pallas_call(
        functools.partial(backward_kernel, first_block=first_block, summed_blocks=summed_blocks),
        grid=(rows,),
        in_specs=[
            padded_spec, padded_spec, padded_spec,
            pl.BlockSpec((1, length, LANES), lambda r: (r, 0, 0)),
            padded_spec, own_spec, own_spec, vector_spec, vector_spec, state_spec,
        ],
        out_specs=[
            pl.BlockSpec((1, summed_blocks * BLOCK, 3 * width), lambda r: (r, 0, 0)),
            out_spec,
            out_spec,
            pl.BlockSpec((1, 8, width), lambda r: (r, 0, 0)),
            state_spec,
            state_spec,
        ],
        out_shape=[
            jax.ShapeDtypeStruct((rows, summed_blocks * BLOCK, 3 * width), bf16),
            own,
            own,
            jax.ShapeDtypeStruct((rows, 8, width), f32),
            state,
            state,
        ],
        scratch_shapes=[pltpu.VMEM((tiles, tokens, LANES), f32)] * 7,
        compiler_params=pltpu.CompilerParams(vmem_limit_bytes=VMEM),
        name="backward",
    )(yf, c, yr, kb, prev, x_own, g_own, hfv, hrv, carry)


def norm_back_kernel(x_ref, mean_ref, inv_ref, gp_ref, w_ref, gain_ref, out_ref, sums_ref):
    gn = lax.dot_general(gp_ref[0], w_ref[...], (((1,), (1,)), ((), ())), preferred_element_type=f32)
    inv = inv_ref[0]
    unit = (x_ref[0].astype(f32) - mean_ref[0]) * inv
    gu = gn * gain_ref[...]
    first = jnp.mean(gu, axis=-1, keepdims=True)
    second = jnp.mean(gu * unit, axis=-1, keepdims=True)
    out_ref[0] = (inv * (gu - first - unit * second)).astype(bf16)

    @pl.when((pl.program_id(0) == 0) & (pl.program_id(1) == 0))
    def _():
        sums_ref[...] = jnp.zeros_like(sums_ref)

    sums_ref[0:1, :] += jnp.sum(gn * unit, axis=0, keepdims=True)
    sums_ref[1:2, :] += jnp.sum(gn, axis=0, keepdims=True)


def norm_back(x_all, mean, inv, gp, weight, gain):
    rows, tokens, features = x_all.shape
    width3 = weight.shape[1]
    whole = lambda r, k: (0, 0)
    tile = pl.BlockSpec((1, BLOCK, features), lambda r, k: (r, k, 0))
    column = pl.BlockSpec((1, BLOCK, 1), lambda r, k: (r, k, 0))
    return pl.pallas_call(
        norm_back_kernel,
        grid=(rows, tokens // BLOCK),
        in_specs=[
            tile,
            column,
            column,
            pl.BlockSpec((1, BLOCK, width3), lambda r, k: (r, k, 0)),
            pl.BlockSpec((features, width3), whole),
            pl.BlockSpec((1, features), whole),
        ],
        out_specs=[tile, pl.BlockSpec((8, features), whole)],
        out_shape=[jax.ShapeDtypeStruct(x_all.shape, bf16), jax.ShapeDtypeStruct((8, features), f32)],
        compiler_params=pltpu.CompilerParams(vmem_limit_bytes=VMEM),
        name="norm_back",
    )(x_all, mean, inv, gp, weight, gain)


def local(inputs, weight, gain, shift, forget_vec, reset_vec, forget_bias, reset_bias, initial, resets, grad_out):
    rows, block_len, features = inputs.shape
    row_block, columns_here = weight.shape
    sections = lax.axis_size("fsdp")
    ranks = lax.axis_size("dp")
    group = sections // 2
    tokens = group * block_len
    index = lax.axis_index("fsdp")
    half, place = index // group, index % group
    first_half = half == 0
    groups = [list(range(group)), list(range(group, sections))]
    chunk = math.gcd(features, columns_here)
    chunks, piece = features // chunk, chunk // group
    width = chunks * piece
    tiles = width // LANES
    parts = columns_here // chunk
    early = 64

    def across(value):
        return lax.ppermute(value, "fsdp", [(j, (j + group) % sections) for j in range(sections)])

    def own(vector):
        return lax.dynamic_index_in_dim(vector.reshape(-1, chunks, group, piece), place, 2, False).reshape(-1, width)

    def to_tiles(value):
        return value.reshape(rows, tokens, tiles, LANES).swapaxes(1, 2)

    def to_owners(value):
        cut = value.reshape(rows, block_len, chunks, group, piece).transpose(3, 0, 1, 2, 4)
        got = lax.all_to_all(cut, "fsdp", 0, 0, tiled=True, axis_index_groups=groups)
        return to_tiles(got.transpose(1, 0, 2, 3, 4).reshape(rows, tokens, width))

    all_resets = resets
    step = 1
    while step < group:
        other = lax.ppermute(all_resets, "fsdp", [(j, j ^ step) for j in range(sections)])
        low = (index // step) % 2 == 0
        all_resets = jnp.concatenate([jnp.where(low, all_resets, other), jnp.where(low, other, all_resets)], axis=1)
        step *= 2
    keep = (1 - all_resets).astype(f32).reshape(rows, tokens // BLOCK, BLOCK)
    keep = jnp.pad(keep, ((0, 0), (0, 0), (0, SPACED - BLOCK))).reshape(rows, -1, 1)
    kb = jnp.broadcast_to(keep, (rows, keep.shape[1], LANES))

    x_all = lax.all_gather(inputs, "fsdp", axis=1, tiled=True, axis_index_groups=groups)

    cut = weight.reshape(row_block, parts, group, piece).transpose(2, 0, 1, 3).reshape(group, row_block, parts * piece)
    mine = lax.all_to_all(cut, "fsdp", 0, 0, tiled=True, axis_index_groups=groups).reshape(group * row_block, parts * piece)
    theirs = across(mine)

    def beside(value):
        return lax.all_gather(value, "dp", axis=1, tiled=True) if ranks != 2 else both(value)

    def both(value):
        other = lax.ppermute(value, "dp", [(0, 1), (1, 0)])
        low = lax.axis_index("dp") == 0
        return jnp.concatenate([jnp.where(low, value, other), jnp.where(low, other, value)], axis=1)

    mine, theirs = beside(mine), beside(theirs)
    own_weight = jnp.concatenate([jnp.where(first_half, mine, theirs), jnp.where(first_half, theirs, mine)], axis=0)

    g_own = to_owners(grad_out)
    x_own = to_tiles(own(x_all.reshape(rows * tokens, features)).reshape(rows, tokens, width))
    hfv, hrv, fb, rb = 0.5 * own(forget_vec), 0.5 * own(reset_vec), own(forget_bias), own(reset_bias)
    gain_row, shift_row = gain[None], shift[None]
    normed, mean, inv, c, yf, yr = project(x_all, own_weight, gain_row, shift_row, fb, rb)

    init = own(initial)[:, None, :]
    prev, lead, end, lead_prev = blocks_forward(yf, c, kb, hfv, init, early)
    arrived = across(end)
    covered = early + 2 * BLOCK
    first = jnp.where(first_half, covered, 0).astype(jnp.int32)[None]
    keep_first = kb[:, 0:1, 0:1]
    start = jnp.where(first_half, lead_prev, keep_first * arrived)
    prev = lead_forward(first, yf, c, kb, hfv, start, lead, prev, covered, LEAD - covered)

    zero = jnp.zeros((rows, 1, width), f32)
    blocks = tokens // BLOCK
    tail = TAIL // BLOCK
    gp, hidden_own, high_own, sums, final, back = backward(
        yf, c, yr, kb, prev, x_own, g_own, hfv, hrv, zero, 0, blocks - tail
    )
    carry = jnp.where(first_half, across(back), 0.0)
    gp_tail, _, _, sums_tail, _, _ = backward(
        yf, c, yr, kb, prev, x_own, g_own, hfv, hrv, carry, blocks - tail, tail
    )
    gp = jnp.concatenate([gp, gp_tail], axis=1)
    sums = jnp.sum(sums[:, :4] + sums_tail[:, :4], axis=0)

    flat = lambda value: value.reshape(rows * tokens, -1)
    contract_first = (((0,), (0,)), ((), ()))
    grad_own = lax.dot_general(flat(normed), flat(gp), contract_first, preferred_element_type=f32).astype(bf16)
    if ranks == 2:
        low = lax.axis_index("dp") == 0
        left, right = grad_own[:, : parts * piece], grad_own[:, parts * piece :]
        sent = lax.ppermute(jnp.where(low, right, left), "dp", [(0, 1), (1, 0)])
        grad_half = (jnp.where(low, left, right).astype(f32) + sent.astype(f32)).astype(bf16)
    else:
        grad_half = lax.psum_scatter(grad_own, "dp", scatter_dimension=1, tiled=True)
    cut_rows = group * row_block
    upper, lower = grad_half[:cut_rows], grad_half[cut_rows:]
    sent = across(jnp.where(first_half, lower, upper))
    grad_part = (jnp.where(first_half, upper, lower).astype(f32) + sent.astype(f32)).astype(bf16)
    got = lax.all_to_all(
        grad_part.reshape(group, row_block, parts * piece), "fsdp", 0, 0, tiled=True, axis_index_groups=groups
    )
    grad_weight = (
        got.reshape(group, row_block, parts, piece).transpose(1, 2, 0, 3).reshape(row_block, columns_here).astype(f32)
    )

    part, norm_sums = norm_back(x_all, mean, inv, gp, own_weight, gain_row)
    high = high_own.swapaxes(1, 2).reshape(rows, tokens, chunks, 1, piece)
    mask = (jnp.arange(group) == place)[:, None]
    part = part.reshape(rows, tokens, chunks, group, piece)
    part = (part.astype(f32) + jnp.where(mask, high.astype(f32), 0.0)).astype(bf16).reshape(rows, tokens, features)
    grad_inputs = lax.psum_scatter(part, "fsdp", scatter_dimension=1, tiled=True, axis_index_groups=groups)

    cut = hidden_own.swapaxes(1, 2).reshape(rows, group, block_len, width).swapaxes(0, 1)
    got = lax.all_to_all(cut, "fsdp", 0, 0, tiled=True, axis_index_groups=groups)
    hidden = (
        got.reshape(group, rows, block_len, chunks, piece).transpose(1, 2, 3, 0, 4).reshape(rows, block_len, features)
    )

    own_width = features // sections
    if piece == own_width and chunks == 2:
        final = final[:, 0]
        low_part = lax.ppermute(final[:, :piece], "fsdp", [(j + group, j) for j in range(group)])
        final_state = jnp.where(first_half, low_part, final[:, piece:])
    else:
        whole = jnp.where(mask, final.reshape(rows, chunks, 1, piece), 0.0).reshape(rows, features)
        whole = lax.psum(jnp.where(first_half, 0.0, whole), "fsdp")
        final_state = lax.dynamic_slice_in_dim(whole, index * own_width, own_width, 1)

    spread = jnp.where(mask, sums.reshape(4, chunks, 1, piece), 0.0).reshape(4, features)
    totals = lax.psum(jnp.concatenate([spread, norm_sums[:2]], axis=0), ("dp", "fsdp"))
    return (hidden, grad_inputs, final_state, grad_weight, *[totals[i] for i in range(6)])


def solution(mesh):
    in_specs = (
        P("dp", "fsdp", None), P("fsdp", "dp"), P(), P(), P(), P(), P(), P(),
        P("dp", None), P("dp", "fsdp"), P("dp", "fsdp", None),
    )
    out_specs = (
        P("dp", "fsdp", None), P("dp", "fsdp", None), P("dp", "fsdp"), P("fsdp", "dp"), P(), P(), P(), P(), P(), P(),
    )
    return jax.shard_map(local, mesh=mesh, in_specs=in_specs, out_specs=out_specs, check_vma=False)
```

```python
import functools
import math

import jax
import jax.numpy as jnp
from jax import lax
from jax.experimental import pallas as pl
from jax.experimental.pallas import tpu as pltpu
from jax.sharding import PartitionSpec as P

SENT = 128
LEAD = 768
REACH = 192
EPSILON = 1e-05
LANES = 128
BLOCK = 128
SPACED = 136
EARLY = REACH - BLOCK
COVERED = EARLY + 2 * BLOCK
STATS = 16
UNROLL = 8
f32 = jnp.float32
bf16 = jnp.bfloat16


def spaced(token):
    return token + (SPACED - BLOCK) * (token // BLOCK)


def tiles_of(ref, count):
    return [ref[:, LANES * i : LANES * (i + 1)] for i in range(count)]


def call(kernel, out_shape, operands, scalars=(), waits=(), scratch=(), mebibytes=14, name=None):
    in_vmem, in_smem = pl.BlockSpec(memory_space=pltpu.VMEM), pl.BlockSpec(memory_space=pltpu.SMEM)
    before = len(scalars) + len(operands)

    def body(*refs):
        kernel(*refs[:before], *refs[before + len(waits) :])

    return pl.pallas_call(
        body,
        in_specs=[in_smem] * len(scalars) + [in_vmem] * len(operands) + [pl.BlockSpec(memory_space=pl.ANY)] * len(waits),
        out_specs=[in_vmem] * len(out_shape),
        out_shape=[jax.ShapeDtypeStruct(*shape) for shape in out_shape],
        scratch_shapes=[pltpu.VMEM(*shape) for shape in scratch],
        compiler_params=pltpu.CompilerParams(vmem_limit_bytes=mebibytes << 20),
        name=name,
    )(*scalars, *operands, *waits)


def fence(value, waits):
    return pl.pallas_call(
        lambda *refs: None,
        in_specs=[pl.BlockSpec(memory_space=pl.ANY)] * (1 + len(waits)),
        out_specs=pl.BlockSpec(memory_space=pl.ANY),
        out_shape=jax.ShapeDtypeStruct(value.shape, value.dtype),
        input_output_aliases={0: 0},
        name="fence",
    )(value, *waits)


def deal_kernel(in_ref, out_ref, *, chunks):
    group = out_ref.shape[0]
    for q in range(group):
        for c in range(chunks):
            lane = (c * group + q) * LANES
            out_ref[q, :, LANES * c : LANES * (c + 1)] = in_ref[:, lane : lane + LANES]


def deal(value, group, waits=()):
    n, features = value.shape
    kernel = functools.partial(deal_kernel, chunks=features // group // LANES)
    return call(kernel, [((group, n, features // group), value.dtype)], (value,), waits=waits, name="deal")[0]


def collect_kernel(*refs):
    *in_refs, out_ref = refs
    row = 0
    for ref in in_refs:
        group, n, width = ref.shape
        for q in range(group):
            for c in range(width // LANES):
                lane = (c * group + q) * LANES
                value = ref[q, :, LANES * c : LANES * (c + 1)]
                out_ref[row : row + n, lane : lane + LANES] = value.astype(out_ref.dtype)
        row += n


def collect(pieces, dtype, waits=()):
    group, _, width = pieces[0].shape
    shape = (sum(value.shape[1] for value in pieces), group * width)
    return call(collect_kernel, [(shape, dtype)], pieces, waits=waits, name="collect")[0]


def add_kernel(a_ref, b_ref, out_ref):
    out_ref[...] = (a_ref[...].astype(f32) + b_ref[...].astype(f32)).astype(out_ref.dtype)


def added(a, b, waits=()):
    return call(add_kernel, [(a.shape, a.dtype)], (a, b), waits=waits, name="added")[0]


def blocks_of(refs):
    return [ref.at[i] for ref in refs for i in range(ref.shape[0])]


def halve_kernel(*refs):
    *in_refs, first_stays, first_goes, second_stays, second_goes = refs
    n = len(in_refs) // 4
    parts = [blocks_of(in_refs[n * i : n * (i + 1)]) for i in range(4)]
    outs = (blocks_of((first_stays, first_goes)), blocks_of((second_stays, second_goes)))
    for kept, got, out in zip(parts[:2], parts[2:], outs):
        for kept_ref, got_ref, out_ref in zip(kept, got, out):
            out_ref[...] = (kept_ref[...].astype(f32) + got_ref[...].astype(f32)).astype(bf16)


def halve(kept, got, waits=()):
    n = sum(value.shape[0] for value in kept) // 4
    out = call(halve_kernel, [((n, *kept[0].shape[1:]), bf16)] * 4, (*kept, *got), waits=waits, name="halve")
    return out[0::2], out[1::2]


def merge_kernel(own_ref, got_ref, away_ref, out_ref):
    value = own_ref[...].astype(f32) + got_ref[...].astype(f32) + away_ref[...].astype(f32)
    out_ref[...] = value.astype(bf16)


def merge(own, got, away, waits=()):
    return call(merge_kernel, [(own.shape, bf16)], (own, got, away), waits=waits, name="merge")[0]


def finish_kernel(where_ref, *refs):
    *in_refs, out_ref = refs
    width = in_refs[0].shape[-1]
    for part in range(2):
        kept_ref, got_ref = in_refs[part], in_refs[2 + part]
        lane = pl.ds(pl.multiple_of((where_ref[0] ^ part) * width, LANES), width)
        out_ref[:, :, lane] = (kept_ref[0].astype(f32) + got_ref[0].astype(f32)).astype(bf16)


def finish(where, kept, got, waits=()):
    _, rows, block, width = kept[0].shape
    return call(finish_kernel, [((rows, block, 2 * width), bf16)], (*kept, *got), (where,), waits, name="finish")[0]


def stats_kernel(where_ref, x_ref, keep_ref, first_ref, second_ref):
    total, block, features = x_ref.shape
    half_width = features // 2

    def row(column):
        return jnp.transpose(jnp.broadcast_to(column, (block, LANES)))[0:1, :]

    for r in range(total):
        for part, ref in enumerate((first_ref, second_ref)):
            lane = pl.multiple_of((where_ref[0] ^ part) * half_width, LANES)
            ref[0, r, :block, :] = x_ref[r, :, pl.ds(lane, half_width)]
        x = x_ref[r].astype(f32)
        mean = jnp.sum(x, axis=-1, keepdims=True) * (1.0 / features)
        centred = x - mean
        inv = lax.rsqrt(jnp.sum(centred * centred, axis=-1, keepdims=True) * (1.0 / features) + EPSILON)
        rows = [keep_ref[r]]
        for value in (row(mean), row(inv)):
            for _ in range(3):
                upper = value.astype(bf16).astype(f32)
                rows.append(upper)
                value = value - upper
        rows = jnp.concatenate(rows + [jnp.zeros_like(rows[0])] * (STATS - len(rows)), axis=0)
        if block < LANES:
            rows = jnp.concatenate([rows, jnp.zeros((STATS, LANES - block), f32)], axis=1)
        first_ref[0, r, block:, :LANES] = rows.astype(bf16)
        first_ref[0, r, block:, LANES:] = jnp.zeros((STATS, half_width - LANES), bf16)


def stats(where, inputs, keep, waits):
    rows, block, features = inputs.shape
    out_shape = [((1, rows, block + STATS, features // 2), bf16), ((1, rows, block, features // 2), bf16)]
    return call(stats_kernel, out_shape, (inputs, keep), (where,), waits, name="stats")


def norm_kernel(where_ref, gain_ref, shift_ref, *refs, orders):
    block_refs, (normed_ref, stats_ref, keep_ref, *own_refs) = refs[:4], refs[4:]
    half_width = block_refs[0].shape[-1]
    total, block = block_refs[1].shape[1:3]
    per_block = BLOCK // block

    def device(r, first_ref, d, second_ref, e, bits):
        q = where_ref[3] ^ bits
        at = pl.ds(pl.multiple_of(q * block, block), block)
        spaced_at = pl.ds(pl.multiple_of(q // per_block * SPACED + q % per_block * block, 8), block)
        rows = first_ref[d, r, block:, :block].astype(f32)

        def column(*of):
            row = functools.reduce(jnp.add, [rows[k : k + 1, :] for k in of])
            return jnp.transpose(jnp.broadcast_to(row, (LANES, block)))

        keep_ref[r, spaced_at, :] = column(0)
        mean, inv = column(1, 2, 3), column(4, 5, 6)
        stats_ref[r, 0, at, :] = mean
        stats_ref[r, 1, at, :] = inv
        for part, x_ref, at_d in ((0, first_ref, d), (1, second_ref, e)):
            for j in range(half_width // LANES):
                x = x_ref[at_d, r, :block, LANES * j : LANES * (j + 1)].astype(f32)
                out = slice(part * half_width + j * LANES, part * half_width + (j + 1) * LANES)
                normed_ref[r, at, out] = ((x - mean) * inv * gain_ref[:, out] + shift_ref[:, out]).astype(bf16)
            for ref in own_refs:
                lane = pl.ds(pl.multiple_of(where_ref[3] * LANES, LANES), LANES)
                ref[r, where_ref[0] ^ part, at, :] = x_ref[at_d, r, :block, lane]

    for r in range(total):
        for odd in range(2):
            for d, bits in enumerate(orders[0]):
                e = orders[1].index(bits)
                device(r, block_refs[2 * odd], d, block_refs[2 * odd + 1], e, bits | odd)


def norm(where, blocks, gain, shift, orders, aligned):
    count, rows, block, half_width = blocks[1].shape
    tokens = 2 * count * block
    out_shape = [
        ((rows, tokens, 2 * half_width), bf16),
        ((rows, 2, tokens, LANES), f32),
        ((rows, tokens // BLOCK * SPACED, LANES), f32),
    ]
    if aligned:
        out_shape.append(((rows, 2, tokens, LANES), bf16))
    return call(functools.partial(norm_kernel, orders=orders), out_shape, (gain, shift, *blocks), (where,), name="norm")


def weight_into(w_ref, parts):
    if len(parts) == 1:
        w_ref[...] = parts[0][...]
        return
    row = 0
    for own, other in zip(parts[0::2], parts[1::2]):
        rows, columns = own.shape
        w_ref[row : row + rows, :columns] = own[...]
        w_ref[row : row + rows, columns:] = other[...]
        row += rows


def slot_of(where_ref, s, slots):
    return lax.rem(where_ref[4] + s, slots)


def project_kernel(where_ref, normed_ref, rows_ref, *refs):
    *parts, sum_ref, vectors_ref, w_ref = refs
    weight_into(w_ref, parts)
    depth = w_ref.shape[0]
    total, slots = sum_ref.shape[:2]
    step = 2 * BLOCK
    vectors_ref[...] = jnp.dot(rows_ref[:, :depth], w_ref[...], preferred_element_type=f32)
    for r in range(total):

        @pl.loop(0, normed_ref.shape[1] // step)
        def _(j):
            at = pl.ds(pl.multiple_of(j * step, step), step)
            p = jnp.dot(normed_ref[r, at, :depth], w_ref[...], preferred_element_type=f32)
            for s in range(slots):
                sum_ref[r, s, at, :] = p[:, LANES * s : LANES * (s + 1)]


def project(where, normed, vector_rows, parts, depth, slots):
    rows, tokens, _ = normed.shape
    out_shape = [
        ((rows, slots, tokens, LANES), f32), ((vector_rows.shape[0], slots * LANES), f32), ((depth, slots * LANES), bf16),
    ]
    return call(project_kernel, out_shape, (normed, vector_rows, *parts), (where,), name="project")


def blocks_kernel(where_ref, normed_ref, rows_ref, sum_ref, some_ref, bias_ref, keep_ref, hfv_ref, init_ref, *refs):
    *parts, p_ref, seg_ref, lead_ref, end_ref, lead_end_ref, vectors_ref, w_ref = refs
    weight_into(w_ref, parts)
    depth = w_ref.shape[0]
    total, slots = p_ref.shape[:2]
    tiles = slots // 3
    step = 2 * BLOCK
    features = normed_ref.shape[2]
    by_column = some_ref[...] + jnp.dot(rows_ref[:, features - depth :], w_ref[...], preferred_element_type=f32)
    for s in range(slots):
        slot = slot_of(where_ref, s, slots)
        lanes = slice(LANES * s, LANES * (s + 1))
        vectors_ref[slot, 0:1, :] = jnp.sum(by_column[0:3, lanes], axis=0, keepdims=True)
        vectors_ref[slot, 1:2, :] = jnp.sum(by_column[3:6, lanes], axis=0, keepdims=True) + bias_ref[slot]
    for r in range(total):

        @pl.loop(0, normed_ref.shape[1] // step)
        def _(j):
            at = pl.ds(pl.multiple_of(j * step, step), step)
            p = jnp.dot(normed_ref[r, at, features - depth :], w_ref[...], preferred_element_type=f32)
            for s in range(slots):
                slot = slot_of(where_ref, s, slots)
                scale = jnp.where(slot < tiles, 1.0, 0.5)
                value = scale * (p[:, LANES * s : LANES * (s + 1)] + sum_ref[r, s, at, :] + bias_ref[slot])
                for k in range(2):
                    to = pl.ds(pl.multiple_of((2 * j + k) * SPACED, 8), BLOCK)
                    p_ref[r, slot, to, :] = value[BLOCK * k : BLOCK * (k + 1)]

        row_blocks(
            p_ref.at[r], keep_ref.at[r], hfv_ref, init_ref.at[r], seg_ref.at[r], lead_ref.at[r], end_ref.at[r],
            lead_end_ref.at[r],
        )


def blocks_forward(where, normed, vector_rows, some, some_vectors, bias, keep, hfv, init, parts, depth):
    rows, tokens, _ = normed.shape
    slots = bias.shape[0]
    tiles = slots // 3
    state = ((rows, 1, tiles * LANES), f32)
    length = tokens // BLOCK * SPACED
    out_shape = [
        ((rows, slots, length, LANES), f32), ((rows, tiles, length, LANES), f32),
        ((rows, tiles, spaced(COVERED), LANES), f32), state, state, ((slots, 2, LANES), f32), ((depth, slots * LANES), bf16),
    ]
    return call(
        blocks_kernel, out_shape, (normed, vector_rows, some, some_vectors, bias, keep, hfv, init, *parts), (where,),
        name="blocks_forward",
    )


def chain_step(p_ref, kb_ref, prev_ref, hfv, carried, row, next_row):
    tiles = len(hfv)
    keep = kb_ref[next_row, :]
    out = []
    for i, (y, prev) in enumerate(carried):
        tau = jnp.tanh(y)
        half = 0.5 * p_ref[i, row, :]
        mid, gap = 0.5 * prev + half, 0.5 * prev - half
        prev_ref[i, row, :] = prev
        reach = hfv[i] * keep
        out.append(
            ((p_ref[tiles + i, next_row, :] + reach * mid) + (reach * gap) * tau, (keep * mid) + (keep * gap) * tau)
        )
    return out


def begin(p_ref, hfv, previous, row):
    return [(p_ref[len(hfv) + i, row, :] + hfv[i] * prev, prev) for i, prev in enumerate(previous)]


def rows_of(token):
    return pl.ds(spaced(token), 1)


def run_chain(p_ref, kb_ref, prev_ref, hfv, carried, first, count):
    def body(j, now):
        for u in range(UNROLL):
            token = first + j * UNROLL + u
            now = chain_step(p_ref, kb_ref, prev_ref, hfv, now, rows_of(token), rows_of(token + 1))
        return now

    return lax.fori_loop(0, count // UNROLL, body, carried)


def row_blocks(p_ref, kb_ref, hfv_ref, init_ref, seg_ref, lead_ref, end_ref, lead_end_ref):
    tiles = seg_ref.shape[0]
    blocks = p_ref.shape[1] // SPACED
    hfv = tiles_of(hfv_ref, tiles)

    def seg_step(cells, step, store):
        row = pl.ds(step, blocks, stride=SPACED)
        keep = kb_ref[row, :]
        out = []
        for i, cell in enumerate(cells):
            prev = keep * cell
            tau = jnp.tanh(p_ref[tiles + i, row, :] + (hfv[i] * keep) * cell)
            half = 0.5 * p_ref[i, row, :]
            if store:
                seg_ref[i, row, :] = prev
            out.append((0.5 * prev + half) + (0.5 * prev - half) * tau)
        return out

    def run(cells, lead, first, token, count, store):
        def body(j, carried):
            cells, lead = carried
            for u in range(UNROLL):
                at = j * UNROLL + u
                cells = seg_step(cells, first + at, store)
                lead = chain_step(p_ref, kb_ref, lead_ref, hfv, lead, rows_of(token + at), rows_of(token + at + 1))
            return cells, lead

        return lax.fori_loop(0, count // UNROLL, body, (cells, lead))

    def moved(cells):
        return [jnp.concatenate([jnp.zeros((1, LANES), f32), cell[:-1]], axis=0) for cell in cells]

    cells = [jnp.zeros((blocks, LANES), f32) for _ in range(tiles)]
    lead = begin(p_ref, hfv, [kb_ref[0:1, :] * v for v in tiles_of(init_ref, tiles)], pl.ds(0, 1))
    cells, lead = run(cells, lead, BLOCK - EARLY, 0, EARLY, False)
    cells, lead = run(moved(cells), lead, 0, EARLY, BLOCK, False)
    cells, lead = run(moved(cells), lead, 0, EARLY + BLOCK, BLOCK, True)
    for i in range(tiles):
        end_ref[:, LANES * i : LANES * (i + 1)] = cells[i][-1:]
        lead_end_ref[:, LANES * i : LANES * (i + 1)] = lead[i][1]


def lead_kernel(p_ref, keep_ref, hfv_ref, start_ref, early_ref, lead_ref):
    rows, tiles = lead_ref.shape[:2]
    hfv = tiles_of(hfv_ref, tiles)
    lead_ref[:, :, : spaced(COVERED), :] = early_ref[...]
    for r in range(rows):
        carried = begin(p_ref.at[r], hfv, tiles_of(start_ref.at[r], tiles), rows_of(COVERED))
        run_chain(p_ref.at[r], keep_ref.at[r], lead_ref.at[r], hfv, carried, COVERED, LEAD - COVERED)


def lead_forward(p, keep, hfv, start, early):
    rows, tiles = early.shape[:2]
    out_shape = [((rows, tiles, spaced(LEAD), LANES), f32)]
    return call(lead_kernel, out_shape, (p, keep, hfv, start, early), name="lead_forward")[0]


def token_terms(prev, c, yf, yr, x, g, keep, hfv, hrv):
    tau_f = jnp.tanh(yf + hfv * prev)
    tau_r = jnp.tanh(yr + hrv * prev)
    f, omf, gate, omg = 0.5 + 0.5 * tau_f, 0.5 - 0.5 * tau_f, 0.5 + 0.5 * tau_r, 0.5 - 0.5 * tau_r
    cell = f * prev + omf * c
    gg = g * gate
    dr = gg * omg * (cell - x)
    e = (prev - c) * f * omf
    slope = f + e * (2.0 * hfv)
    return dict(
        cell=cell, hidden=gate * cell + omg * x, high=g * omg, gg=gg, dr=dr, e=e, omf=omf,
        a=keep * slope, b=keep * (slope * gg + dr * (2.0 * hrv)),
    )


def block_terms(p_ref, keep_ref, prev_ref, x_ref, g_ref, hfv, hrv, r, k, i):
    tiles = len(hfv)
    at = pl.ds(pl.multiple_of(k * SPACED, 8), BLOCK)
    devices = BLOCK // g_ref.shape[2]
    lanes = slice(LANES * i, LANES * (i + 1))
    g = jnp.concatenate([g_ref[k * devices + n, r, :, lanes].astype(f32) for n in range(devices)], axis=0)
    x = x_ref[r, i, pl.ds(pl.multiple_of(k * BLOCK, BLOCK), BLOCK), :].astype(f32)
    c, yf, yr = (p_ref[r, m * tiles + i, at, :] for m in range(3))
    return token_terms(prev_ref[i, at, :], c, yf, yr, x, g, keep_ref[r, at, :], hfv[i], hrv[i])


def run_back(a_ref, b_ref, d_ref, carried, count):
    def body(j, carried):
        base = pl.multiple_of(count - UNROLL * (j + 1), UNROLL)
        for u in reversed(range(UNROLL)):
            row = pl.ds(base + u, 1)
            now = []
            for i, d in enumerate(carried):
                if d_ref is not None:
                    d_ref[i, row, :] = d
                now.append(a_ref[i, row, :] * d + b_ref[i, row, :])
            carried = now
        return carried

    return lax.fori_loop(0, count // UNROLL, body, carried)


def entry_kernel(
    p_ref, keep_ref, seg_ref, x_ref, g_ref, hfv_ref, hrv_ref, start_ref, first_ref, back_ref, prev_ref, a_ref, b_ref
):
    rows, slots = p_ref.shape[:2]
    tiles = slots // 3
    hfv, hrv = tiles_of(hfv_ref, tiles), tiles_of(hrv_ref, tiles)
    blocks = -(-REACH // BLOCK)
    for r in range(rows):
        prev_ref[...] = seg_ref[r, :, : blocks * SPACED, :]
        start = [keep_ref[r, 0:1, :] * v for v in tiles_of(start_ref.at[r], tiles)]
        run_chain(p_ref.at[r], keep_ref.at[r], prev_ref, hfv, begin(p_ref.at[r], hfv, start, pl.ds(0, 1)), 0, REACH)
        first_ref[r] = prev_ref[:, : spaced(REACH), :]
        for k in range(blocks):
            for i in range(tiles):
                t = block_terms(p_ref, keep_ref, prev_ref, x_ref, g_ref, hfv, hrv, r, k, i)
                a_ref[i, BLOCK * k : BLOCK * (k + 1), :] = t["a"]
                b_ref[i, BLOCK * k : BLOCK * (k + 1), :] = t["b"]
        carried = run_back(a_ref, b_ref, None, [jnp.zeros((1, LANES), f32)] * tiles, blocks * BLOCK)
        for i in range(tiles):
            back_ref[r, :, LANES * i : LANES * (i + 1)] = carried[i]


def entry(p, keep, seg, x_own, g_own, hfv, hrv, start, waits):
    rows, slots, _, _ = p.shape
    tiles = slots // 3
    blocks = -(-REACH // BLOCK)
    length, count = blocks * SPACED, blocks * BLOCK
    return call(
        entry_kernel,
        [((rows, tiles, spaced(REACH), LANES), f32), ((rows, 1, tiles * LANES), f32)],
        (p, keep, seg, x_own, g_own, hfv, hrv, start),
        waits=waits,
        scratch=[((tiles, length, LANES), f32)] + [((tiles, count, LANES), f32)] * 2,
        name="entry",
    )


def backward_kernel(
    where_ref, p_ref, keep_ref, seg_ref, lead_ref, first_ref, x_ref, g_ref, hfv_ref, hrv_ref, carry_ref, vectors_ref,
    gp_ref, hidden_ref, high_ref, sums_ref, final_ref, means_ref,
    prev_ref, a_ref, b_ref, gg_ref, e_ref, omf_ref, dr_ref, d_ref,
):
    rows, slots = p_ref.shape[:2]
    tiles = slots // 3
    blocks = p_ref.shape[2] // SPACED
    hfv, hrv = tiles_of(hfv_ref, tiles), tiles_of(hrv_ref, tiles)
    devices, block = BLOCK // g_ref.shape[2], g_ref.shape[2]
    sums_ref[...] = jnp.zeros_like(sums_ref)
    for r in range(rows):
        prev_ref[...] = seg_ref[r]

        @pl.when(where_ref[0] == 0)
        def _():
            prev_ref[:, : spaced(LEAD), :] = lead_ref[r]

        @pl.when(where_ref[0] != 0)
        def _():
            prev_ref[:, : spaced(REACH), :] = first_ref[r]

        @pl.loop(0, blocks)
        def _(k):
            out = pl.ds(pl.multiple_of(k * BLOCK, BLOCK), BLOCK)
            for i in range(tiles):
                t = block_terms(p_ref, keep_ref, prev_ref, x_ref, g_ref, hfv, hrv, r, k, i)
                lanes = slice(LANES * i, LANES * (i + 1))
                for n in range(devices):
                    hidden_ref[k * devices + n, r, :, lanes] = t["hidden"][n * block : (n + 1) * block].astype(bf16)
                high_ref[r, i, out, :] = t["high"].astype(bf16)
                for ref, name in zip((a_ref, b_ref, gg_ref, e_ref, omf_ref, dr_ref), "a b gg e omf dr".split()):
                    ref[i, out, :] = t[name]
                final_ref[r, :, lanes] = t["cell"][-1:]

        run_back(a_ref, b_ref, d_ref, tiles_of(carry_ref.at[r], tiles), blocks * BLOCK)

        @pl.loop(0, blocks)
        def _(k):
            at = pl.ds(pl.multiple_of(k * SPACED, 8), BLOCK)
            out = pl.ds(pl.multiple_of(k * BLOCK, BLOCK), BLOCK)
            first, second = jnp.zeros((BLOCK, LANES), f32), jnp.zeros((BLOCK, LANES), f32)
            for i in range(tiles):
                prev = prev_ref[i, at, :]
                u = d_ref[i, out, :] + gg_ref[i, out, :]
                df, dr = u * e_ref[i, out, :], dr_ref[i, out, :]
                dc = u * omf_ref[i, out, :]
                for m, value in enumerate((dc, df, dr)):
                    slot = m * tiles + i
                    lane = lax.rem(slot + slots - where_ref[4], slots) * LANES
                    gp_ref[r, out, pl.ds(pl.multiple_of(lane, LANES), LANES)] = value.astype(bf16)
                    first += value * vectors_ref[slot, 0:1, :]
                    second += value * ((1.0 if m == 0 else 2.0) * p_ref[r, slot, at, :] - vectors_ref[slot, 1:2, :])
                lanes = slice(LANES * i, LANES * (i + 1))
                for m, value in enumerate((df * prev, dr * prev, df, dr)):
                    sums_ref[m : m + 1, lanes] += jnp.sum(value, axis=0, keepdims=True)
                for m, value in enumerate((dc, df, dr)):
                    lane = lax.rem(m * tiles + i + slots - where_ref[4], slots) * LANES
                    at_lane = pl.ds(pl.multiple_of(lane, LANES), LANES)
                    sums_ref[7:8, at_lane] += jnp.sum(value, axis=0, keepdims=True)
            means_ref[r, 0, out, :] = first
            means_ref[r, 1, out, :] = second


def backward(where, p, keep, seg, lead, first, x_own, g_own, hfv, hrv, carry, vectors):
    rows, slots, length, _ = p.shape
    tiles = slots // 3
    tokens = length // SPACED * BLOCK
    width = tiles * LANES
    return call(
        backward_kernel,
        [
            ((rows, tokens, 3 * width), bf16),
            (g_own.shape, bf16),
            ((rows, tiles, tokens, LANES), bf16),
            ((8, 3 * width), f32),
            ((rows, 1, width), f32),
            ((rows, 2, tokens, LANES), f32),
        ],
        (p, keep, seg, lead, first, x_own, g_own, hfv, hrv, carry, vectors),
        (where,),
        scratch=[((tiles, length, LANES), f32)] + [((tiles, tokens, LANES), f32)] * 7,
        name="backward",
    )


def weight_back_kernel(normed_ref, gp_ref, sums_ref, *refs, part, group, cuts):
    count = sum(len(rows) for rows in cuts)
    w_refs, (by_feature_ref, *out_refs) = refs[: len(refs) - count - 1], refs[len(refs) - count - 1 :]
    total, _, features = normed_ref.shape
    row_block = features // 2 // group
    columns = out_refs[0].shape[2]
    span = 2 * LANES
    devices = span // row_block
    lane_tiles = gp_ref.shape[2] // LANES
    for k in range(group // devices):
        lane = slice(part * (features // 2) + k * span, part * (features // 2) + (k + 1) * span)
        p = sum(
            lax.dot_general(normed_ref[r, :, lane], gp_ref[r], (((0,), (0,)), ((), ())), preferred_element_type=f32)
            for r in range(total)
        )
        first = w_refs[0].shape[0]
        w = [w_refs[0][lane.start : min(lane.stop, first), :]] if lane.start < first else []
        if lane.stop > first:
            w.append(w_refs[1][max(lane.start - first, 0) : lane.stop - first, :])
        w = jnp.concatenate(w).astype(f32)
        for m, value in enumerate((p * w, w * sums_ref[7:8, :])):
            value = functools.reduce(jnp.add, [value[:, LANES * j : LANES * (j + 1)] for j in range(lane_tiles)])
            by_feature_ref[m : m + 1, k * span : (k + 1) * span] = jnp.sum(jnp.transpose(value), axis=0, keepdims=True)
        p = p.astype(bf16)
        outs = iter(out_refs)
        for split, rows in enumerate(cuts):
            start = 0
            for step in rows:
                out_ref = next(outs)
                for n in range(devices):
                    row = n * row_block + start
                    out_ref[k * devices + n] = p[row : row + step, split * columns : (split + 1) * columns]
                start += step


def weight_back(normed, gp, sums, weights, part, group, cuts, waits):
    features = normed.shape[2]
    columns = gp.shape[2] // len(cuts)
    kernel = functools.partial(weight_back_kernel, part=part, group=group, cuts=cuts)
    out_shape = [((2, features // 2), f32)] + [((group, step, columns), bf16) for rows in cuts for step in rows]
    return call(kernel, out_shape, (normed, gp, sums, *weights), waits=waits, name="weight_back")


def norm_back_kernel(where_ref, first_ref, second_ref, stats_ref, means_ref, gp_ref, gain_ref, *refs, orders, odd, with_high):
    *w_refs, high_ref, a_low, a_high, b_low, b_high, some_ref, gn_ref = refs
    half_count, total, block, half_width = a_low.shape
    out_refs = ((a_low, a_high), (b_low, b_high))
    features = 2 * half_width
    together = gn_ref.shape[0] // block
    for r in range(total):
        for d in range(0, len(orders[0]), together):
            tokens = []
            for n in range(together):
                place = where_ref[3] ^ (orders[0][d + n] | odd)
                tokens.append(pl.ds(pl.multiple_of(place * block, 16), block))
                some_ref[n * block : (n + 1) * block, :] = gp_ref[r, tokens[n], :]
            lane = 0
            for w_ref in w_refs:
                rows = w_ref.shape[0]
                gn_ref[:, lane : lane + rows] = lax.dot_general(
                    some_ref[...], w_ref[...], (((1,), (1,)), ((), ())), preferred_element_type=f32
                )
                lane += rows
            for n in range(together):
                mean, inv = stats_ref[r, 0, tokens[n], :], stats_ref[r, 1, tokens[n], :]
                first, second = (
                    jnp.sum(means_ref[r, m, tokens[n], :], axis=-1, keepdims=True) * (1.0 / features) for m in range(2)
                )
                slope = inv * inv * second
                rest = inv * first - slope * mean
                for part, x_ref in enumerate((first_ref, second_ref)):
                    at_d = orders[part].index(orders[0][d + n])
                    for j in range(half_width // LANES):
                        at = slice(part * half_width + LANES * j, part * half_width + LANES * (j + 1))
                        lanes = slice(LANES * j, LANES * (j + 1))
                        value = inv * (gn_ref[n * block : (n + 1) * block, at] * gain_ref[:, at])
                        value -= slope * x_ref[at_d, r, :block, lanes].astype(f32) + rest
                        if with_high:
                            add = high_ref[r, where_ref[0] ^ part, tokens[n], :].astype(f32)
                            value += jnp.where(where_ref[3] == j, add, 0.0)
                        out_refs[part][at_d // half_count][at_d % half_count, r, :, lanes] = value.astype(bf16)


def norm_back(where, first, second, orders, odd, stats, means, gp, weights, gain, high, with_high, waits):
    count, rows, block, half_width = second.shape
    together = 2 * LANES // block
    return call(
        functools.partial(norm_back_kernel, orders=orders, odd=odd, with_high=with_high),
        [((count // 2, *second.shape[1:]), bf16)] * 4,
        (first, second, stats, means, gp, gain, *weights, high), (where,), waits,
        scratch=[((together * block, gp.shape[2]), bf16), ((together * block, 2 * half_width), f32)],
        name="norm_back",
    )


def totals_kernel(where_ref, sums_ref, own_ref, other_ref, gain_ref, shift_ref, out_ref, *, chunk):
    half_width = own_ref.shape[1]
    out_ref[...] = jnp.zeros_like(out_ref)
    for i in range(2):
        lane = pl.ds(pl.multiple_of(i * chunk + where_ref[3] * LANES, LANES), LANES)
        out_ref[0:4, lane] = sums_ref[0:4, LANES * i : LANES * (i + 1)]
    for part, ref in enumerate((own_ref, other_ref)):
        lane = pl.ds(pl.multiple_of((where_ref[0] ^ part) * half_width, LANES), half_width)
        at = slice(part * half_width, (part + 1) * half_width)
        out_ref[4:5, lane] = (ref[0:1, :] - shift_ref[:, at] * ref[1:2, :]) / gain_ref[:, at]
        out_ref[5:6, lane] = ref[1:2, :]


def bf16_parts(row):
    rows = []
    for _ in range(3):
        upper = lax.reduce_precision(row, 8, 7)
        rows.append(upper.astype(bf16))
        row = row - upper
    return rows


def local(inputs, weight, gain, shift, forget_vec, reset_vec, forget_bias, reset_bias, initial, resets, grad_out):
    rows, block_len, features = inputs.shape
    row_block, columns_here = weight.shape
    sections = lax.axis_size("fsdp")
    ranks = lax.axis_size("dp")
    group = sections // 2
    tokens = group * block_len
    index = lax.axis_index("fsdp")
    half, place = index // group, index % group
    rank = lax.axis_index("dp")
    first_half = half == 0
    groups = [list(range(group)), list(range(group, sections))]
    chunk = math.gcd(features, columns_here)
    chunks, piece = features // chunk, chunk // group
    width = chunks * piece
    tiles = width // LANES
    slots = 3 * tiles
    parts = columns_here // chunk
    columns = parts * piece
    aligned = piece == LANES and chunks == 2
    paired = ranks == 2 and aligned
    turn = rank * (columns // LANES) if paired else jnp.zeros_like(rank)
    where = jnp.stack([half, rank, index % 2, place, turn]).astype(jnp.int32)
    bits = [1 << b for b in range(1, group.bit_length() - 1)]
    ways = (bits[::-1], bits)
    orders = []
    for way in ways:
        order = [0]
        for bit in way:
            order += [d | bit for d in order]
        orders.append(order)

    def across(value):
        return lax.ppermute(value, "fsdp", [(j, (j + group) % sections) for j in range(sections)])

    def flipped(value, bit):
        return lax.ppermute(value, "fsdp", [(j, j ^ bit) for j in range(sections)])

    def swapped(value):
        return lax.ppermute(value, "dp", [(0, 1), (1, 0)])

    def shared(value):
        return lax.all_to_all(value, "fsdp", 0, 0, tiled=True, axis_index_groups=groups)

    def own(vector):
        return lax.dynamic_index_in_dim(vector.reshape(-1, chunks, group, piece), place, 2, False).reshape(-1, width)

    def halves_turned(vector):
        low, high = vector[..., : features // 2], vector[..., features // 2 :]
        return jnp.concatenate([jnp.where(first_half, low, high), jnp.where(first_half, high, low)], axis=-1)

    def dealt(value, waits=()):
        if aligned:
            return deal(value, group, waits)
        n, wide = value.shape
        return value.reshape(n, wide // chunk, group, piece).transpose(2, 0, 1, 3).reshape(group, n, wide // group)

    def collected(pieces, dtype, waits=()):
        if aligned:
            return collect(pieces, dtype, waits)
        wide = pieces[0].shape[2]
        back = lambda v: v.reshape(group, -1, wide // piece, piece).transpose(1, 2, 0, 3).reshape(-1, wide * group)
        return jnp.concatenate([back(v) for v in pieces]).astype(dtype)

    mine = shared(dealt(weight)).reshape(-1, columns)
    early_rows = (group - 1) * row_block
    theirs = [across(mine[:early_rows]), across(mine[early_rows:])]
    early_rows += features // 2
    near = list(stats(where, inputs, (1 - resets).astype(f32)[:, None, :], (mine,)))
    for way in zip(*ways):
        near = [jnp.concatenate([value, flipped(value, bit)]) for value, bit in zip(near, way)]
    blocks = [*near, *(flipped(value, 1) for value in near)]
    if paired:
        beside = swapped(mine)
        theirs_beside = []
        for i in range(2):
            theirs[i] = fence(theirs[i], (beside, *theirs_beside[-1:]))
            theirs_beside.append(swapped(theirs[i]))
        early, late = [mine, beside, theirs[0], theirs_beside[0]], [theirs[1], theirs_beside[1]]
    else:
        whole = [lax.all_gather(v, "dp", axis=1, tiled=True) for v in (mine, jnp.concatenate(theirs))]
        whole = jnp.concatenate(whole, axis=0)
        early, late = [whole[:early_rows]], [whole[early_rows:]]
    g_own = shared(dealt(grad_out.reshape(-1, features), (theirs[0],)).reshape(group, rows, block_len, width))

    hfv, hrv = 0.5 * own(forget_vec), 0.5 * own(reset_vec)
    bias = jnp.concatenate([jnp.zeros((1, width), f32), own(forget_bias), own(reset_bias)]).reshape(-1, 1, LANES)
    gain_row, shift_row = halves_turned(gain)[None], halves_turned(shift)[None]
    vector_rows = [*bf16_parts(gain_row), *bf16_parts(shift_row)]
    vector_rows = jnp.pad(jnp.concatenate(vector_rows), ((0, 10), (0, 0)))
    normed, token_stats, keep, *x_own = norm(where, blocks, gain_row, shift_row, orders, aligned)
    if aligned:
        x_own = x_own[0]
    else:
        at = lambda part, d: blocks[2 * (d % 2) + part][orders[part].index(d & ~1)][:, :block_len]
        by_place = jnp.stack([jnp.concatenate([at(0, d), at(1, d)], axis=-1) for d in range(group)])
        in_order = halves_turned(by_place[place ^ jnp.arange(group)]).swapaxes(0, 1).reshape(rows * tokens, features)
        x_own = own(in_order).reshape(rows, tokens, tiles, LANES).swapaxes(1, 2)
    some, some_vectors, early_weight = project(where, normed, vector_rows, early, early_rows, slots)
    p, seg, lead, end, lead_end, vectors, late_weight = blocks_forward(
        where, normed, vector_rows, some, some_vectors, bias, keep, hfv, own(initial)[:, None, :], late,
        features - early_rows,
    )
    weights = (early_weight, late_weight)
    start = across(end)
    lead = lead_forward(p, keep, hfv, lead_end, lead)
    first, back = entry(p, keep, seg, x_own, g_own, hfv, hrv, start, ())
    carry = jnp.where(first_half, across(back), 0.0)
    gp, hidden_own, high_own, sums, final, means = backward(
        where, p, keep, seg, lead, first, x_own, g_own, hfv, hrv, carry, vectors
    )

    mask = (jnp.arange(group) == place)[:, None]

    def norm_part(odd, waits):
        out = norm_back(
            where, *blocks[2 * odd : 2 * odd + 2], orders, odd, token_stats, means, gp, weights, gain_row, high_own, aligned,
            waits,
        )
        if aligned:
            return out
        spread = high_own.swapaxes(1, 2).reshape(rows, group, block_len, chunks, 1, piece).swapaxes(0, 1)
        spread = jnp.where(mask, spread.astype(f32), 0.0).reshape(group, rows, block_len, features)
        spread = halves_turned(spread)[place ^ jnp.arange(group)]
        halves = (spread[..., : features // 2], spread[..., features // 2 :])
        add = [add[d | odd] for add, order in zip(halves, orders) for d in order]
        n = group // 4
        return [(v.astype(f32) + jnp.stack(add[i * n : (i + 1) * n])).astype(bf16) for i, v in enumerate(out)]

    pieces = 1
    cuts = [(row_block // pieces,) * pieces] * (2 if paired else 1)
    by_feature_other, *away = weight_back(normed, gp, sums, weights, 1, group, cuts, ())
    away_got = [swapped(value) for value in away[pieces:]]
    sent = norm_part(1, (by_feature_other,))
    got = [flipped(value, 1) for value in sent]
    by_feature_own, *here = weight_back(normed, gp, sums, weights, 0, group, cuts, sent[:1])
    kept = norm_part(0, (by_feature_own,))
    kept, sent = halve(kept, got, kept[:1])
    bit_pairs = list(zip(*(w[::-1] for w in ways)))
    got = [flipped(value, bit) for value, bit in zip(sent, bit_pairs.pop(0))]
    hidden_got = shared(fence(hidden_own, kept[:1]))
    if paired:
        away = [added(a, b, kept[:1]) for a, b in zip(away, away_got)]
        here_got = [swapped(fence(value, away)) for value in here[pieces:]]
    else:
        away, here = ([lax.psum_scatter(x, "dp", scatter_dimension=2, tiled=True) for x in v] for v in (away, here))
    z_got = [across(value) for value in away]

    hidden = collected([hidden_got.reshape(group, -1, width)], bf16).reshape(rows, block_len, features)
    for way in bit_pairs:
        kept, sent = halve(kept, got, (hidden,))
        got = [flipped(value, bit) for value, bit in zip(sent, way)]
    grad_inputs = finish(where, kept, got)

    if aligned:
        totals = call(
            functools.partial(totals_kernel, chunk=chunk), [((8, features), f32)],
            (sums, by_feature_own, by_feature_other, gain_row, shift_row), (where,), kept[:1], name="totals",
        )[0]
    else:
        spread = jnp.where(mask, sums[:4, :width].reshape(4, chunks, 1, piece), 0.0).reshape(4, features)
        product, shift_sum = jnp.concatenate([by_feature_own, by_feature_other], axis=1)
        gain_sum = (product - shift_row[0] * shift_sum) / gain_row[0]
        totals = jnp.concatenate([spread, halves_turned(jnp.stack([gain_sum, shift_sum]))], axis=0)
    for bit in [1 << b for b in range(group.bit_length() - 1)]:
        totals = added(totals, flipped(totals, bit))
    waits = (grad_inputs, totals)
    grad_weight = []
    for i in range(pieces):
        value = merge(here[i], here_got[i], z_got[i], waits) if paired else added(here[i], z_got[i], waits)
        grad_weight.append(shared(value))
    grad_weight = collected(grad_weight, f32)
    totals = added(totals, swapped(totals)) if ranks == 2 else lax.psum(totals, "dp")
    totals = added(totals, across(totals))

    own_width = features // sections
    if piece == own_width and chunks == 2:
        final = final[:, 0]
        low_part = lax.ppermute(final[:, :piece], "fsdp", [(j + group, j) for j in range(group)])
        final_state = jnp.where(first_half, low_part, final[:, piece:])
    else:
        spread = jnp.where(mask, final.reshape(rows, chunks, 1, piece), 0.0).reshape(rows, features)
        spread = lax.psum(jnp.where(first_half, 0.0, spread), "fsdp")
        final_state = lax.dynamic_slice_in_dim(spread, index * own_width, own_width, 1)

    return (hidden, grad_inputs, final_state, grad_weight, *[totals[i] for i in range(6)])


def solution(mesh):
    in_specs = (
        P("dp", "fsdp", None), P("fsdp", "dp"), P(), P(), P(), P(), P(), P(),
        P("dp", None), P("dp", "fsdp"), P("dp", "fsdp", None),
    )
    out_specs = (
        P("dp", "fsdp", None), P("dp", "fsdp", None), P("dp", "fsdp"), P("fsdp", "dp"), P(), P(), P(), P(), P(), P(),
    )
    return jax.shard_map(local, mesh=mesh, in_specs=in_specs, out_specs=out_specs, check_vma=False)
```

```python
import functools
import math

import jax
import jax.numpy as jnp
from jax import lax
from jax.experimental import pallas as pl
from jax.experimental.pallas import tpu as pltpu
from jax.sharding import PartitionSpec as P

SENT = 128
LEAD = 768
REACH = 192
EPSILON = 1e-05
LANES = 128
BLOCK = 128
SPACED = 136
EARLY = REACH - BLOCK
COVERED = EARLY + 2 * BLOCK
STATS = 16
UNROLL = 8
f32 = jnp.float32
bf16 = jnp.bfloat16


def spaced(token):
    return token + (SPACED - BLOCK) * (token // BLOCK)


def tiles_of(ref, count):
    return [ref[:, LANES * i : LANES * (i + 1)] for i in range(count)]


def call(kernel, out_shape, operands, scalars=(), waits=(), scratch=(), mebibytes=14, name=None):
    in_vmem, in_smem = pl.BlockSpec(memory_space=pltpu.VMEM), pl.BlockSpec(memory_space=pltpu.SMEM)
    before = len(scalars) + len(operands)

    def body(*refs):
        kernel(*refs[:before], *refs[before + len(waits) :])

    return pl.pallas_call(
        body,
        in_specs=[in_smem] * len(scalars) + [in_vmem] * len(operands) + [pl.BlockSpec(memory_space=pl.ANY)] * len(waits),
        out_specs=[in_vmem] * len(out_shape),
        out_shape=[jax.ShapeDtypeStruct(*shape) for shape in out_shape],
        scratch_shapes=[pltpu.VMEM(*shape) for shape in scratch],
        compiler_params=pltpu.CompilerParams(vmem_limit_bytes=mebibytes << 20),
        name=name,
    )(*scalars, *operands, *waits)


def fence(value, waits):
    return pl.pallas_call(
        lambda *refs: None,
        in_specs=[pl.BlockSpec(memory_space=pl.ANY)] * (1 + len(waits)),
        out_specs=pl.BlockSpec(memory_space=pl.ANY),
        out_shape=jax.ShapeDtypeStruct(value.shape, value.dtype),
        input_output_aliases={0: 0},
        name="fence",
    )(value, *waits)


def deal_kernel(in_ref, out_ref, *, chunks):
    group = out_ref.shape[0]
    for q in range(group):
        for c in range(chunks):
            lane = (c * group + q) * LANES
            out_ref[q, :, LANES * c : LANES * (c + 1)] = in_ref[:, lane : lane + LANES]


def deal(value, group, waits=()):
    n, features = value.shape
    kernel = functools.partial(deal_kernel, chunks=features // group // LANES)
    return call(kernel, [((group, n, features // group), value.dtype)], (value,), waits=waits, name="deal")[0]


def collect_kernel(*refs):
    *in_refs, out_ref = refs
    row = 0
    for ref in in_refs:
        group, n, width = ref.shape
        for q in range(group):
            for c in range(width // LANES):
                lane = (c * group + q) * LANES
                value = ref[q, :, LANES * c : LANES * (c + 1)]
                out_ref[row : row + n, lane : lane + LANES] = value.astype(out_ref.dtype)
        row += n


def collect(pieces, dtype, waits=()):
    group, _, width = pieces[0].shape
    shape = (sum(value.shape[1] for value in pieces), group * width)
    return call(collect_kernel, [(shape, dtype)], pieces, waits=waits, name="collect")[0]


def add_kernel(a_ref, b_ref, out_ref):
    out_ref[...] = (a_ref[...].astype(f32) + b_ref[...].astype(f32)).astype(out_ref.dtype)


def added(a, b, waits=()):
    return call(add_kernel, [(a.shape, a.dtype)], (a, b), waits=waits, name="added")[0]


def blocks_of(refs):
    return [ref.at[i] for ref in refs for i in range(ref.shape[0])]


def halve_kernel(*refs):
    *in_refs, first_stays, first_goes, second_stays, second_goes = refs
    n = len(in_refs) // 4
    parts = [blocks_of(in_refs[n * i : n * (i + 1)]) for i in range(4)]
    outs = (blocks_of((first_stays, first_goes)), blocks_of((second_stays, second_goes)))
    for kept, got, out in zip(parts[:2], parts[2:], outs):
        for kept_ref, got_ref, out_ref in zip(kept, got, out):
            out_ref[...] = (kept_ref[...].astype(f32) + got_ref[...].astype(f32)).astype(bf16)


def halve(kept, got, waits=()):
    n = sum(value.shape[0] for value in kept) // 4
    out = call(halve_kernel, [((n, *kept[0].shape[1:]), bf16)] * 4, (*kept, *got), waits=waits, name="halve")
    return out[0::2], out[1::2]


def merge_kernel(own_ref, got_ref, away_ref, out_ref):
    value = own_ref[...].astype(f32) + got_ref[...].astype(f32) + away_ref[...].astype(f32)
    out_ref[...] = value.astype(bf16)


def merge(own, got, away, waits=()):
    return call(merge_kernel, [(own.shape, bf16)], (own, got, away), waits=waits, name="merge")[0]


def finish_kernel(where_ref, *refs):
    *in_refs, out_ref = refs
    width = in_refs[0].shape[-1]
    for part in range(2):
        kept_ref, got_ref = in_refs[part], in_refs[2 + part]
        lane = pl.ds(pl.multiple_of((where_ref[0] ^ part) * width, LANES), width)
        out_ref[:, :, lane] = (kept_ref[0].astype(f32) + got_ref[0].astype(f32)).astype(bf16)


def finish(where, kept, got, waits=()):
    _, rows, block, width = kept[0].shape
    return call(finish_kernel, [((rows, block, 2 * width), bf16)], (*kept, *got), (where,), waits, name="finish")[0]


def stats_kernel(x_ref, keep_ref, out_ref):
    total, block, features = x_ref.shape

    def row(column):
        return jnp.transpose(jnp.broadcast_to(column, (block, LANES)))[0:1, :]

    for r in range(total):
        out_ref[r, :block, :] = x_ref[r]
        x = x_ref[r].astype(f32)
        mean = jnp.sum(x, axis=-1, keepdims=True) * (1.0 / features)
        centred = x - mean
        inv = lax.rsqrt(jnp.sum(centred * centred, axis=-1, keepdims=True) * (1.0 / features) + EPSILON)
        rows = [keep_ref[r]]
        for value in (row(mean), row(inv)):
            for _ in range(3):
                upper = value.astype(bf16).astype(f32)
                rows.append(upper)
                value = value - upper
        rows = jnp.concatenate(rows + [jnp.zeros_like(rows[0])] * (STATS - len(rows)), axis=0)
        if block < LANES:
            rows = jnp.concatenate([rows, jnp.zeros((STATS, LANES - block), f32)], axis=1)
        out_ref[r, block:, :LANES] = rows.astype(bf16)
        out_ref[r, block:, LANES:] = jnp.zeros((STATS, features - LANES), bf16)


def stats(inputs, keep, waits):
    rows, block, features = inputs.shape
    return call(stats_kernel, [((rows, block + STATS, features), bf16)], (inputs, keep), waits=waits, name="stats")[0]


def norm_kernel(where_ref, gain_ref, shift_ref, *refs, count):
    block_refs, (normed_ref, stats_ref, keep_ref, *own_refs) = refs[:count], refs[count:]
    total, block, features = block_refs[0].shape
    block -= STATS
    half_width = features // 2
    per_block = BLOCK // block

    def device(r, x_ref, q):
        at = pl.ds(pl.multiple_of(q * block, block), block)
        spaced_at = pl.ds(pl.multiple_of(q // per_block * SPACED + q % per_block * block, 8), block)
        rows = x_ref[r, block:, :block].astype(f32)

        def column(*of):
            row = functools.reduce(jnp.add, [rows[k : k + 1, :] for k in of])
            return jnp.transpose(jnp.broadcast_to(row, (LANES, block)))

        keep_ref[r, spaced_at, :] = column(0)
        mean, inv = column(1, 2, 3), column(4, 5, 6)
        stats_ref[r, 0, at, :] = mean
        stats_ref[r, 1, at, :] = inv
        for part in range(2):
            lane = pl.multiple_of((where_ref[0] ^ part) * half_width, LANES)
            for j in range(half_width // LANES):
                x = x_ref[r, :block, pl.ds(lane + j * LANES, LANES)].astype(f32)
                out = slice(part * half_width + j * LANES, part * half_width + (j + 1) * LANES)
                normed_ref[r, at, out] = ((x - mean) * inv * gain_ref[:, out] + shift_ref[:, out]).astype(bf16)
        for ref in own_refs:
            for i in range(2):
                lane = pl.ds(pl.multiple_of(i * half_width + where_ref[3] * LANES, LANES), LANES)
                ref[r, i, at, :] = x_ref[r, :block, lane]

    for r in range(total):
        for d, ref in enumerate(block_refs):
            device(r, ref, where_ref[3] ^ d)


def norm(where, blocks, gain, shift, aligned, waits):
    rows, block, features = blocks[0].shape
    tokens = len(blocks) * (block - STATS)
    out_shape = [
        ((rows, tokens, features), bf16),
        ((rows, 2, tokens, LANES), f32),
        ((rows, tokens // BLOCK * SPACED, LANES), f32),
    ]
    if aligned:
        out_shape.append(((rows, 2, tokens, LANES), bf16))
    kernel = functools.partial(norm_kernel, count=len(blocks))
    return call(kernel, out_shape, (gain, shift, *blocks), (where,), waits, name="norm")


def weight_into(w_ref, parts):
    if len(parts) == 1:
        w_ref[...] = parts[0][...]
        return
    pieces = len(parts) // 2
    group, _, columns = parts[0].shape
    block = sum(part.shape[1] for part in parts[:pieces])
    for rank in range(2):
        start = 0
        for part in parts[rank * pieces : (rank + 1) * pieces]:
            rows = part.shape[1]
            for q in range(group):
                row = q * block + start
                w_ref[row : row + rows, rank * columns : (rank + 1) * columns] = part[q]
            start += rows


def slot_of(where_ref, s, slots):
    return lax.rem(where_ref[4] + s, slots)


def project_kernel(where_ref, normed_ref, rows_ref, *refs):
    *parts, sum_ref, vectors_ref, w_ref = refs
    weight_into(w_ref, parts)
    depth = w_ref.shape[0]
    total, slots = sum_ref.shape[:2]
    step = 2 * BLOCK
    vectors_ref[...] = jnp.dot(rows_ref[:, :depth], w_ref[...], preferred_element_type=f32)
    for r in range(total):

        @pl.loop(0, normed_ref.shape[1] // step)
        def _(j):
            at = pl.ds(pl.multiple_of(j * step, step), step)
            p = jnp.dot(normed_ref[r, at, :depth], w_ref[...], preferred_element_type=f32)
            for s in range(slots):
                sum_ref[r, s, at, :] = p[:, LANES * s : LANES * (s + 1)]


def project(where, normed, vector_rows, parts, depth, slots):
    rows, tokens, _ = normed.shape
    out_shape = [
        ((rows, slots, tokens, LANES), f32), ((vector_rows.shape[0], slots * LANES), f32), ((depth, slots * LANES), bf16),
    ]
    return call(project_kernel, out_shape, (normed, vector_rows, *parts), (where,), name="project")


def blocks_kernel(where_ref, normed_ref, rows_ref, sum_ref, some_ref, bias_ref, keep_ref, hfv_ref, init_ref, *refs):
    *parts, p_ref, seg_ref, lead_ref, end_ref, lead_end_ref, vectors_ref, w_ref = refs
    weight_into(w_ref, parts)
    depth = w_ref.shape[0]
    total, slots = p_ref.shape[:2]
    tiles = slots // 3
    step = 2 * BLOCK
    features = normed_ref.shape[2]
    by_column = some_ref[...] + jnp.dot(rows_ref[:, features - depth :], w_ref[...], preferred_element_type=f32)
    for s in range(slots):
        slot = slot_of(where_ref, s, slots)
        lanes = slice(LANES * s, LANES * (s + 1))
        vectors_ref[slot, 0:1, :] = jnp.sum(by_column[0:3, lanes], axis=0, keepdims=True)
        vectors_ref[slot, 1:2, :] = jnp.sum(by_column[3:6, lanes], axis=0, keepdims=True) + bias_ref[slot]
    for r in range(total):

        @pl.loop(0, normed_ref.shape[1] // step)
        def _(j):
            at = pl.ds(pl.multiple_of(j * step, step), step)
            p = jnp.dot(normed_ref[r, at, features - depth :], w_ref[...], preferred_element_type=f32)
            for s in range(slots):
                slot = slot_of(where_ref, s, slots)
                scale = jnp.where(slot < tiles, 1.0, 0.5)
                value = scale * (p[:, LANES * s : LANES * (s + 1)] + sum_ref[r, s, at, :] + bias_ref[slot])
                for k in range(2):
                    to = pl.ds(pl.multiple_of((2 * j + k) * SPACED, 8), BLOCK)
                    p_ref[r, slot, to, :] = value[BLOCK * k : BLOCK * (k + 1)]

        row_blocks(
            p_ref.at[r], keep_ref.at[r], hfv_ref, init_ref.at[r], seg_ref.at[r], lead_ref.at[r], end_ref.at[r],
            lead_end_ref.at[r],
        )


def blocks_forward(where, normed, vector_rows, some, some_vectors, bias, keep, hfv, init, parts, depth):
    rows, tokens, _ = normed.shape
    slots = bias.shape[0]
    tiles = slots // 3
    state = ((rows, 1, tiles * LANES), f32)
    length = tokens // BLOCK * SPACED
    out_shape = [
        ((rows, slots, length, LANES), f32), ((rows, tiles, length, LANES), f32),
        ((rows, tiles, spaced(COVERED), LANES), f32), state, state, ((slots, 2, LANES), f32), ((depth, slots * LANES), bf16),
    ]
    return call(
        blocks_kernel, out_shape, (normed, vector_rows, some, some_vectors, bias, keep, hfv, init, *parts), (where,),
        name="blocks_forward",
    )


def chain_step(p_ref, kb_ref, prev_ref, hfv, carried, row, next_row):
    tiles = len(hfv)
    keep = kb_ref[next_row, :]
    out = []
    for i, (y, prev) in enumerate(carried):
        tau = jnp.tanh(y)
        half = 0.5 * p_ref[i, row, :]
        mid, gap = 0.5 * prev + half, 0.5 * prev - half
        prev_ref[i, row, :] = prev
        reach = hfv[i] * keep
        out.append(
            ((p_ref[tiles + i, next_row, :] + reach * mid) + (reach * gap) * tau, (keep * mid) + (keep * gap) * tau)
        )
    return out


def begin(p_ref, hfv, previous, row):
    return [(p_ref[len(hfv) + i, row, :] + hfv[i] * prev, prev) for i, prev in enumerate(previous)]


def rows_of(token):
    return pl.ds(spaced(token), 1)


def run_chain(p_ref, kb_ref, prev_ref, hfv, carried, first, count):
    def body(j, now):
        for u in range(UNROLL):
            token = first + j * UNROLL + u
            now = chain_step(p_ref, kb_ref, prev_ref, hfv, now, rows_of(token), rows_of(token + 1))
        return now

    return lax.fori_loop(0, count // UNROLL, body, carried)


def row_blocks(p_ref, kb_ref, hfv_ref, init_ref, seg_ref, lead_ref, end_ref, lead_end_ref):
    tiles = seg_ref.shape[0]
    blocks = p_ref.shape[1] // SPACED
    hfv = tiles_of(hfv_ref, tiles)

    def seg_step(cells, step, store):
        row = pl.ds(step, blocks, stride=SPACED)
        keep = kb_ref[row, :]
        out = []
        for i, cell in enumerate(cells):
            prev = keep * cell
            tau = jnp.tanh(p_ref[tiles + i, row, :] + (hfv[i] * keep) * cell)
            half = 0.5 * p_ref[i, row, :]
            if store:
                seg_ref[i, row, :] = prev
            out.append((0.5 * prev + half) + (0.5 * prev - half) * tau)
        return out

    def run(cells, lead, first, token, count, store):
        def body(j, carried):
            cells, lead = carried
            for u in range(UNROLL):
                at = j * UNROLL + u
                cells = seg_step(cells, first + at, store)
                lead = chain_step(p_ref, kb_ref, lead_ref, hfv, lead, rows_of(token + at), rows_of(token + at + 1))
            return cells, lead

        return lax.fori_loop(0, count // UNROLL, body, (cells, lead))

    def moved(cells):
        return [jnp.concatenate([jnp.zeros((1, LANES), f32), cell[:-1]], axis=0) for cell in cells]

    cells = [jnp.zeros((blocks, LANES), f32) for _ in range(tiles)]
    lead = begin(p_ref, hfv, [kb_ref[0:1, :] * v for v in tiles_of(init_ref, tiles)], pl.ds(0, 1))
    cells, lead = run(cells, lead, BLOCK - EARLY, 0, EARLY, False)
    cells, lead = run(moved(cells), lead, 0, EARLY, BLOCK, False)
    cells, lead = run(moved(cells), lead, 0, EARLY + BLOCK, BLOCK, True)
    for i in range(tiles):
        end_ref[:, LANES * i : LANES * (i + 1)] = cells[i][-1:]
        lead_end_ref[:, LANES * i : LANES * (i + 1)] = lead[i][1]


def lead_kernel(p_ref, keep_ref, hfv_ref, start_ref, early_ref, lead_ref):
    rows, tiles = lead_ref.shape[:2]
    hfv = tiles_of(hfv_ref, tiles)
    lead_ref[:, :, : spaced(COVERED), :] = early_ref[...]
    for r in range(rows):
        carried = begin(p_ref.at[r], hfv, tiles_of(start_ref.at[r], tiles), rows_of(COVERED))
        run_chain(p_ref.at[r], keep_ref.at[r], lead_ref.at[r], hfv, carried, COVERED, LEAD - COVERED)


def lead_forward(p, keep, hfv, start, early):
    rows, tiles = early.shape[:2]
    out_shape = [((rows, tiles, spaced(LEAD), LANES), f32)]
    return call(lead_kernel, out_shape, (p, keep, hfv, start, early), name="lead_forward")[0]


def token_terms(prev, c, yf, yr, x, g, keep, hfv, hrv):
    tau_f = jnp.tanh(yf + hfv * prev)
    tau_r = jnp.tanh(yr + hrv * prev)
    f, omf, gate, omg = 0.5 + 0.5 * tau_f, 0.5 - 0.5 * tau_f, 0.5 + 0.5 * tau_r, 0.5 - 0.5 * tau_r
    cell = f * prev + omf * c
    gg = g * gate
    dr = gg * omg * (cell - x)
    e = (prev - c) * f * omf
    slope = f + e * (2.0 * hfv)
    return dict(
        cell=cell, hidden=gate * cell + omg * x, high=g * omg, gg=gg, dr=dr, e=e, omf=omf,
        a=keep * slope, b=keep * (slope * gg + dr * (2.0 * hrv)),
    )


def block_terms(p_ref, keep_ref, prev_ref, x_ref, g_ref, hfv, hrv, r, k, i):
    tiles = len(hfv)
    at = pl.ds(pl.multiple_of(k * SPACED, 8), BLOCK)
    devices = BLOCK // g_ref.shape[2]
    lanes = slice(LANES * i, LANES * (i + 1))
    g = jnp.concatenate([g_ref[k * devices + n, r, :, lanes].astype(f32) for n in range(devices)], axis=0)
    x = x_ref[r, i, pl.ds(pl.multiple_of(k * BLOCK, BLOCK), BLOCK), :].astype(f32)
    c, yf, yr = (p_ref[r, m * tiles + i, at, :] for m in range(3))
    return token_terms(prev_ref[i, at, :], c, yf, yr, x, g, keep_ref[r, at, :], hfv[i], hrv[i])


def run_back(a_ref, b_ref, d_ref, carried, count):
    def body(j, carried):
        base = pl.multiple_of(count - UNROLL * (j + 1), UNROLL)
        for u in reversed(range(UNROLL)):
            row = pl.ds(base + u, 1)
            now = []
            for i, d in enumerate(carried):
                if d_ref is not None:
                    d_ref[i, row, :] = d
                now.append(a_ref[i, row, :] * d + b_ref[i, row, :])
            carried = now
        return carried

    return lax.fori_loop(0, count // UNROLL, body, carried)


def entry_kernel(
    p_ref, keep_ref, seg_ref, x_ref, g_ref, hfv_ref, hrv_ref, start_ref, first_ref, back_ref, prev_ref, a_ref, b_ref
):
    rows, slots = p_ref.shape[:2]
    tiles = slots // 3
    hfv, hrv = tiles_of(hfv_ref, tiles), tiles_of(hrv_ref, tiles)
    blocks = -(-REACH // BLOCK)
    for r in range(rows):
        prev_ref[...] = seg_ref[r, :, : blocks * SPACED, :]
        start = [keep_ref[r, 0:1, :] * v for v in tiles_of(start_ref.at[r], tiles)]
        run_chain(p_ref.at[r], keep_ref.at[r], prev_ref, hfv, begin(p_ref.at[r], hfv, start, pl.ds(0, 1)), 0, REACH)
        first_ref[r] = prev_ref[:, : spaced(REACH), :]
        for k in range(blocks):
            for i in range(tiles):
                t = block_terms(p_ref, keep_ref, prev_ref, x_ref, g_ref, hfv, hrv, r, k, i)
                a_ref[i, BLOCK * k : BLOCK * (k + 1), :] = t["a"]
                b_ref[i, BLOCK * k : BLOCK * (k + 1), :] = t["b"]
        carried = run_back(a_ref, b_ref, None, [jnp.zeros((1, LANES), f32)] * tiles, blocks * BLOCK)
        for i in range(tiles):
            back_ref[r, :, LANES * i : LANES * (i + 1)] = carried[i]


def entry(p, keep, seg, x_own, g_own, hfv, hrv, start, waits):
    rows, slots, _, _ = p.shape
    tiles = slots // 3
    blocks = -(-REACH // BLOCK)
    length, count = blocks * SPACED, blocks * BLOCK
    return call(
        entry_kernel,
        [((rows, tiles, spaced(REACH), LANES), f32), ((rows, 1, tiles * LANES), f32)],
        (p, keep, seg, x_own, g_own, hfv, hrv, start),
        waits=waits,
        scratch=[((tiles, length, LANES), f32)] + [((tiles, count, LANES), f32)] * 2,
        name="entry",
    )


def backward_kernel(
    where_ref, p_ref, keep_ref, seg_ref, lead_ref, first_ref, x_ref, g_ref, hfv_ref, hrv_ref, carry_ref, vectors_ref,
    gp_ref, hidden_ref, high_ref, sums_ref, final_ref, means_ref,
    prev_ref, a_ref, b_ref, gg_ref, e_ref, omf_ref, dr_ref, d_ref,
):
    rows, slots = p_ref.shape[:2]
    tiles = slots // 3
    blocks = p_ref.shape[2] // SPACED
    hfv, hrv = tiles_of(hfv_ref, tiles), tiles_of(hrv_ref, tiles)
    devices, block = BLOCK // g_ref.shape[2], g_ref.shape[2]
    sums_ref[...] = jnp.zeros_like(sums_ref)
    for r in range(rows):
        prev_ref[...] = seg_ref[r]

        @pl.when(where_ref[0] == 0)
        def _():
            prev_ref[:, : spaced(LEAD), :] = lead_ref[r]

        @pl.when(where_ref[0] != 0)
        def _():
            prev_ref[:, : spaced(REACH), :] = first_ref[r]

        @pl.loop(0, blocks)
        def _(k):
            out = pl.ds(pl.multiple_of(k * BLOCK, BLOCK), BLOCK)
            for i in range(tiles):
                t = block_terms(p_ref, keep_ref, prev_ref, x_ref, g_ref, hfv, hrv, r, k, i)
                lanes = slice(LANES * i, LANES * (i + 1))
                for n in range(devices):
                    hidden_ref[k * devices + n, r, :, lanes] = t["hidden"][n * block : (n + 1) * block].astype(bf16)
                high_ref[r, i, out, :] = t["high"].astype(bf16)
                for ref, name in zip((a_ref, b_ref, gg_ref, e_ref, omf_ref, dr_ref), ("a", "b", "gg", "e", "omf", "dr")):
                    ref[i, out, :] = t[name]
                final_ref[r, :, lanes] = t["cell"][-1:]

        run_back(a_ref, b_ref, d_ref, tiles_of(carry_ref.at[r], tiles), blocks * BLOCK)

        @pl.loop(0, blocks)
        def _(k):
            at = pl.ds(pl.multiple_of(k * SPACED, 8), BLOCK)
            out = pl.ds(pl.multiple_of(k * BLOCK, BLOCK), BLOCK)
            first, second = jnp.zeros((BLOCK, LANES), f32), jnp.zeros((BLOCK, LANES), f32)
            for i in range(tiles):
                prev = prev_ref[i, at, :]
                u = d_ref[i, out, :] + gg_ref[i, out, :]
                df, dr = u * e_ref[i, out, :], dr_ref[i, out, :]
                dc = u * omf_ref[i, out, :]
                for m, value in enumerate((dc, df, dr)):
                    slot = m * tiles + i
                    lane = lax.rem(slot + slots - where_ref[4], slots) * LANES
                    gp_ref[r, out, pl.ds(pl.multiple_of(lane, LANES), LANES)] = value.astype(bf16)
                    first += value * vectors_ref[slot, 0:1, :]
                    second += value * ((1.0 if m == 0 else 2.0) * p_ref[r, slot, at, :] - vectors_ref[slot, 1:2, :])
                lanes = slice(LANES * i, LANES * (i + 1))
                for m, value in enumerate((df * prev, dr * prev, df, dr)):
                    sums_ref[m : m + 1, lanes] += jnp.sum(value, axis=0, keepdims=True)
                for m, value in enumerate((dc, df, dr)):
                    lane = lax.rem(m * tiles + i + slots - where_ref[4], slots) * LANES
                    at_lane = pl.ds(pl.multiple_of(lane, LANES), LANES)
                    sums_ref[7:8, at_lane] += jnp.sum(value, axis=0, keepdims=True)
            means_ref[r, 0, out, :] = first
            means_ref[r, 1, out, :] = second


def backward(where, p, keep, seg, lead, first, x_own, g_own, hfv, hrv, carry, vectors):
    rows, slots, length, _ = p.shape
    tiles = slots // 3
    tokens = length // SPACED * BLOCK
    width = tiles * LANES
    return call(
        backward_kernel,
        [
            ((rows, tokens, 3 * width), bf16),
            (g_own.shape, bf16),
            ((rows, tiles, tokens, LANES), bf16),
            ((8, 3 * width), f32),
            ((rows, 1, width), f32),
            ((rows, 2, tokens, LANES), f32),
        ],
        (p, keep, seg, lead, first, x_own, g_own, hfv, hrv, carry, vectors),
        (where,),
        scratch=[((tiles, length, LANES), f32)] + [((tiles, tokens, LANES), f32)] * 7,
        name="backward",
    )


def weight_back_kernel(normed_ref, gp_ref, sums_ref, *refs, part, group, cuts):
    count = sum(len(rows) for rows in cuts)
    w_refs, (by_feature_ref, *out_refs) = refs[: len(refs) - count - 1], refs[len(refs) - count - 1 :]
    total, _, features = normed_ref.shape
    row_block = features // 2 // group
    columns = out_refs[0].shape[2]
    span = 2 * LANES
    devices = span // row_block
    lane_tiles = gp_ref.shape[2] // LANES
    for k in range(group // devices):
        lane = slice(part * (features // 2) + k * span, part * (features // 2) + (k + 1) * span)
        p = sum(
            lax.dot_general(normed_ref[r, :, lane], gp_ref[r], (((0,), (0,)), ((), ())), preferred_element_type=f32)
            for r in range(total)
        )
        first = w_refs[0].shape[0]
        w = [w_refs[0][lane.start : min(lane.stop, first), :]] if lane.start < first else []
        if lane.stop > first:
            w.append(w_refs[1][max(lane.start - first, 0) : lane.stop - first, :])
        w = jnp.concatenate(w).astype(f32)
        for m, value in enumerate((p * w, w * sums_ref[7:8, :])):
            value = functools.reduce(jnp.add, [value[:, LANES * j : LANES * (j + 1)] for j in range(lane_tiles)])
            by_feature_ref[m : m + 1, k * span : (k + 1) * span] = jnp.sum(jnp.transpose(value), axis=0, keepdims=True)
        p = p.astype(bf16)
        outs = iter(out_refs)
        for split, rows in enumerate(cuts):
            start = 0
            for step in rows:
                out_ref = next(outs)
                for n in range(devices):
                    row = n * row_block + start
                    out_ref[k * devices + n] = p[row : row + step, split * columns : (split + 1) * columns]
                start += step


def weight_back(normed, gp, sums, weights, part, group, cuts, waits):
    features = normed.shape[2]
    columns = gp.shape[2] // len(cuts)
    kernel = functools.partial(weight_back_kernel, part=part, group=group, cuts=cuts)
    out_shape = [((2, features // 2), f32)] + [((group, step, columns), bf16) for rows in cuts for step in rows]
    return call(kernel, out_shape, (normed, gp, sums, *weights), waits=waits, name="weight_back")


def norm_back_kernel(where_ref, stats_ref, means_ref, gp_ref, gain_ref, *refs, orders, odd, with_high):
    count = len(orders[0])
    x_refs, refs = refs[:count], refs[count:]
    *w_refs, high_ref, a_low, a_high, b_low, b_high, some_ref, gn_ref = refs
    half_count, total, block, half_width = a_low.shape
    out_refs = ((a_low, a_high), (b_low, b_high))
    features = 2 * half_width
    together = gn_ref.shape[0] // block
    for r in range(total):
        for d in range(0, count, together):
            tokens = []
            for n in range(together):
                place = where_ref[3] ^ (orders[0][d + n] | odd)
                tokens.append(pl.ds(pl.multiple_of(place * block, 16), block))
                some_ref[n * block : (n + 1) * block, :] = gp_ref[r, tokens[n], :]
            lane = 0
            for w_ref in w_refs:
                rows = w_ref.shape[0]
                gn_ref[:, lane : lane + rows] = lax.dot_general(
                    some_ref[...], w_ref[...], (((1,), (1,)), ((), ())), preferred_element_type=f32
                )
                lane += rows
            for n in range(together):
                mean, inv = stats_ref[r, 0, tokens[n], :], stats_ref[r, 1, tokens[n], :]
                first, second = (
                    jnp.sum(means_ref[r, m, tokens[n], :], axis=-1, keepdims=True) * (1.0 / features) for m in range(2)
                )
                slope = inv * inv * second
                rest = inv * first - slope * mean
                for part in range(2):
                    at_d = orders[part].index(orders[0][d + n])
                    out_ref = out_refs[part][at_d // half_count]
                    start = pl.multiple_of((where_ref[0] ^ part) * half_width, LANES)
                    if with_high:
                        high = high_ref[r, where_ref[0] ^ part, tokens[n], :].astype(f32)
                    for j in range(half_width // LANES):
                        at = slice(part * half_width + LANES * j, part * half_width + LANES * (j + 1))
                        value = inv * (gn_ref[n * block : (n + 1) * block, at] * gain_ref[:, at])
                        x = x_refs[d + n][r, :block, pl.ds(start + LANES * j, LANES)].astype(f32)
                        value -= slope * x + rest
                        if with_high:
                            value += jnp.where(where_ref[3] == j, high, 0.0)
                        out_ref[at_d % half_count, r, :, LANES * j : LANES * (j + 1)] = value.astype(bf16)


def norm_back(where, blocks, orders, odd, stats, means, gp, weights, gain, high, with_high, waits):
    count = len(blocks)
    rows, block, features = blocks[0].shape
    block -= STATS
    together = 2 * LANES // block
    return call(
        functools.partial(norm_back_kernel, orders=orders, odd=odd, with_high=with_high),
        [((count // 2, rows, block, features // 2), bf16)] * 4,
        (stats, means, gp, gain, *blocks, *weights, high), (where,), waits,
        scratch=[((together * block, gp.shape[2]), bf16), ((together * block, features), f32)],
        name="norm_back",
    )


def totals_kernel(where_ref, sums_ref, own_ref, other_ref, gain_ref, shift_ref, out_ref, *, chunk):
    half_width = own_ref.shape[1]
    out_ref[...] = jnp.zeros_like(out_ref)
    for i in range(2):
        lane = pl.ds(pl.multiple_of(i * chunk + where_ref[3] * LANES, LANES), LANES)
        out_ref[0:4, lane] = sums_ref[0:4, LANES * i : LANES * (i + 1)]
    for part, ref in enumerate((own_ref, other_ref)):
        lane = pl.ds(pl.multiple_of((where_ref[0] ^ part) * half_width, LANES), half_width)
        at = slice(part * half_width, (part + 1) * half_width)
        out_ref[4:5, lane] = (ref[0:1, :] - shift_ref[:, at] * ref[1:2, :]) / gain_ref[:, at]
        out_ref[5:6, lane] = ref[1:2, :]


def bf16_parts(row):
    rows = []
    for _ in range(3):
        upper = lax.reduce_precision(row, 8, 7)
        rows.append(upper.astype(bf16))
        row = row - upper
    return rows


def local(inputs, weight, gain, shift, forget_vec, reset_vec, forget_bias, reset_bias, initial, resets, grad_out):
    rows, block_len, features = inputs.shape
    row_block, columns_here = weight.shape
    sections = lax.axis_size("fsdp")
    ranks = lax.axis_size("dp")
    group = sections // 2
    tokens = group * block_len
    index = lax.axis_index("fsdp")
    half, place = index // group, index % group
    rank = lax.axis_index("dp")
    first_half = half == 0
    groups = [list(range(group)), list(range(group, sections))]
    chunk = math.gcd(features, columns_here)
    chunks, piece = features // chunk, chunk // group
    width = chunks * piece
    tiles = width // LANES
    slots = 3 * tiles
    parts = columns_here // chunk
    columns = parts * piece
    aligned = piece == LANES and chunks == 2
    paired = ranks == 2 and aligned
    turn = rank * (columns // LANES) if paired else jnp.zeros_like(rank)
    where = jnp.stack([half, rank, index % 2, place, turn]).astype(jnp.int32)
    bits = [1 << b for b in range(1, group.bit_length() - 1)]
    ways = (bits[::-1], bits)
    orders = []
    for way in ways:
        order = [0]
        for bit in way:
            order += [d | bit for d in order]
        orders.append(order)

    def across(value):
        return lax.ppermute(value, "fsdp", [(j, (j + group) % sections) for j in range(sections)])

    def flipped(value, bit):
        return lax.ppermute(value, "fsdp", [(j, j ^ bit) for j in range(sections)])

    def swapped(value):
        return lax.ppermute(value, "dp", [(0, 1), (1, 0)])

    def shared(value):
        return lax.all_to_all(value, "fsdp", 0, 0, tiled=True, axis_index_groups=groups)

    def own(vector):
        return lax.dynamic_index_in_dim(vector.reshape(-1, chunks, group, piece), place, 2, False).reshape(-1, width)

    def halves_turned(vector):
        low, high = vector[..., : features // 2], vector[..., features // 2 :]
        return jnp.concatenate([jnp.where(first_half, low, high), jnp.where(first_half, high, low)], axis=-1)

    def dealt(value, waits=()):
        if aligned:
            return deal(value, group, waits)
        n, wide = value.shape
        return value.reshape(n, wide // chunk, group, piece).transpose(2, 0, 1, 3).reshape(group, n, wide // group)

    def collected(pieces, dtype, waits=()):
        if aligned:
            return collect(pieces, dtype, waits)
        wide = pieces[0].shape[2]
        back = lambda v: v.reshape(group, -1, wide // piece, piece).transpose(1, 2, 0, 3).reshape(-1, wide * group)
        return jnp.concatenate([back(v) for v in pieces]).astype(dtype)

    mine = shared(dealt(weight))
    theirs = across(mine)
    beside = swapped(mine) if paired else mine
    blocks = {0: stats(inputs, (1 - resets).astype(f32)[:, None, :], (mine,))}
    for bit in bits[::-1]:
        blocks |= {d | bit: flipped(value, bit) for d, value in blocks.items()}
    blocks = {d: fence(value, (theirs, beside)) for d, value in blocks.items()}
    blocks |= {d | 1: flipped(value, 1) for d, value in blocks.items()}
    blocks = [blocks[d] for d in range(group)]
    early_rows = features // 2
    if paired:
        early, late = [mine, beside], [theirs, swapped(theirs)]
    else:
        early, late = (
            [lax.all_gather(v.reshape(-1, columns), "dp", axis=1, tiled=True)] for v in (mine, theirs)
        )
    hfv, hrv = 0.5 * own(forget_vec), 0.5 * own(reset_vec)
    bias = jnp.concatenate([jnp.zeros((1, width), f32), own(forget_bias), own(reset_bias)]).reshape(-1, 1, LANES)
    gain_row, shift_row = halves_turned(gain)[None], halves_turned(shift)[None]
    vector_rows = [*bf16_parts(gain_row), *bf16_parts(shift_row)]
    vector_rows = jnp.pad(jnp.concatenate(vector_rows), ((0, 10), (0, 0)))
    g_own = shared(dealt(grad_out.reshape(-1, features)).reshape(group, rows, block_len, width))
    normed, token_stats, keep, *x_own = norm(where, blocks, gain_row, shift_row, aligned, (g_own,))
    if aligned:
        x_own = x_own[0]
    else:
        in_order = jnp.stack(blocks)[place ^ jnp.arange(group)][:, :, :block_len].swapaxes(0, 1)
        x_own = own(in_order.reshape(rows * tokens, features)).reshape(rows, tokens, tiles, LANES).swapaxes(1, 2)
    some, some_vectors, early_weight = project(where, normed, vector_rows, early, early_rows, slots)
    p, seg, lead, end, lead_end, vectors, late_weight = blocks_forward(
        where, normed, vector_rows, some, some_vectors, bias, keep, hfv, own(initial)[:, None, :], late,
        features - early_rows,
    )
    weights = (early_weight, late_weight)
    start = across(end)
    lead = lead_forward(p, keep, hfv, lead_end, lead)
    first, back = entry(p, keep, seg, x_own, g_own, hfv, hrv, start, ())
    carry = jnp.where(first_half, across(back), 0.0)
    gp, hidden_own, high_own, sums, final, means = backward(
        where, p, keep, seg, lead, first, x_own, g_own, hfv, hrv, carry, vectors
    )

    mask = (jnp.arange(group) == place)[:, None]

    def norm_part(odd, waits):
        out = norm_back(
            where, [blocks[d | odd] for d in orders[0]], orders, odd, token_stats, means, gp, weights, gain_row, high_own, aligned,
            waits,
        )
        if aligned:
            return out
        spread = high_own.swapaxes(1, 2).reshape(rows, group, block_len, chunks, 1, piece).swapaxes(0, 1)
        spread = jnp.where(mask, spread.astype(f32), 0.0).reshape(group, rows, block_len, features)
        spread = halves_turned(spread)[place ^ jnp.arange(group)]
        halves = (spread[..., : features // 2], spread[..., features // 2 :])
        add = [add[d | odd] for add, order in zip(halves, orders) for d in order]
        n = group // 4
        return [(v.astype(f32) + jnp.stack(add[i * n : (i + 1) * n])).astype(bf16) for i, v in enumerate(out)]

    pieces = 1
    cuts = [(row_block // pieces,) * pieces] * (2 if paired else 1)
    by_feature_other, *away = weight_back(normed, gp, sums, weights, 1, group, cuts, ())
    away_got = [swapped(value) for value in away[pieces:]]
    sent = norm_part(1, (by_feature_other,))
    got = [flipped(value, 1) for value in sent]
    by_feature_own, *here = weight_back(normed, gp, sums, weights, 0, group, cuts, sent[:1])
    kept = norm_part(0, (by_feature_own,))
    kept, sent = halve(kept, got, kept[:1])
    bit_pairs = list(zip(*(w[::-1] for w in ways)))
    got = [flipped(value, bit) for value, bit in zip(sent, bit_pairs.pop(0))]
    hidden_got = shared(hidden_own)
    if paired:
        away = [added(a, b, kept[:1]) for a, b in zip(away, away_got)]
        here_got = [swapped(fence(value, away)) for value in here[pieces:]]
    else:
        away, here = ([lax.psum_scatter(x, "dp", scatter_dimension=2, tiled=True) for x in v] for v in (away, here))
    z_got = [across(value) for value in away]

    hidden = collected([hidden_got.reshape(group, -1, width)], bf16).reshape(rows, block_len, features)
    for way in bit_pairs:
        kept, sent = halve(kept, got, (hidden,))
        got = [flipped(value, bit) for value, bit in zip(sent, way)]
    grad_inputs = finish(where, kept, got)

    if aligned:
        totals = call(
            functools.partial(totals_kernel, chunk=chunk), [((8, features), f32)],
            (sums, by_feature_own, by_feature_other, gain_row, shift_row), (where,), kept[:1], name="totals",
        )[0]
    else:
        spread = jnp.where(mask, sums[:4, :width].reshape(4, chunks, 1, piece), 0.0).reshape(4, features)
        product, shift_sum = jnp.concatenate([by_feature_own, by_feature_other], axis=1)
        gain_sum = (product - shift_row[0] * shift_sum) / gain_row[0]
        totals = jnp.concatenate([spread, halves_turned(jnp.stack([gain_sum, shift_sum]))], axis=0)
    for bit in [1 << b for b in range(group.bit_length() - 1)]:
        totals = added(totals, flipped(totals, bit))
    waits = (grad_inputs, totals)
    grad_weight = []
    for i in range(pieces):
        value = merge(here[i], here_got[i], z_got[i], waits) if paired else added(here[i], z_got[i], waits)
        grad_weight.append(shared(value))
    grad_weight = collected(grad_weight, f32)
    totals = added(totals, swapped(totals)) if ranks == 2 else lax.psum(totals, "dp")
    totals = added(totals, across(totals))

    own_width = features // sections
    if piece == own_width and chunks == 2:
        final = final[:, 0]
        low_part = lax.ppermute(final[:, :piece], "fsdp", [(j + group, j) for j in range(group)])
        final_state = jnp.where(first_half, low_part, final[:, piece:])
    else:
        spread = jnp.where(mask, final.reshape(rows, chunks, 1, piece), 0.0).reshape(rows, features)
        spread = lax.psum(jnp.where(first_half, 0.0, spread), "fsdp")
        final_state = lax.dynamic_slice_in_dim(spread, index * own_width, own_width, 1)

    return (hidden, grad_inputs, final_state, grad_weight, *[totals[i] for i in range(6)])


def solution(mesh):
    in_specs = (
        P("dp", "fsdp", None), P("fsdp", "dp"), P(), P(), P(), P(), P(), P(),
        P("dp", None), P("dp", "fsdp"), P("dp", "fsdp", None),
    )
    out_specs = (
        P("dp", "fsdp", None), P("dp", "fsdp", None), P("dp", "fsdp"), P("fsdp", "dp"), P(), P(), P(), P(), P(), P(),
    )
    return jax.shard_map(local, mesh=mesh, in_specs=in_specs, out_specs=out_specs, check_vma=False)
```

```python
import functools
import math

import jax
import jax.numpy as jnp
from jax import lax
from jax.experimental import pallas as pl
from jax.experimental.pallas import tpu as pltpu
from jax.sharding import PartitionSpec as P

SENT = 128
LEAD = 768
REACH = 192
EPSILON = 1e-05
LANES = 128
BLOCK = 128
SPACED = 136
EARLY = REACH - BLOCK
COVERED = EARLY + 2 * BLOCK
STATS = 16
UNROLL = 8
f32 = jnp.float32
bf16 = jnp.bfloat16


def spaced(token):
    return token + (SPACED - BLOCK) * (token // BLOCK)


def tiles_of(ref, count):
    return [ref[:, LANES * i : LANES * (i + 1)] for i in range(count)]


def call(kernel, out_shape, operands, scalars=(), waits=(), scratch=(), mebibytes=14, name=None):
    in_vmem, in_smem = pl.BlockSpec(memory_space=pltpu.VMEM), pl.BlockSpec(memory_space=pltpu.SMEM)
    before = len(scalars) + len(operands)

    def body(*refs):
        kernel(*refs[:before], *refs[before + len(waits) :])

    return pl.pallas_call(
        body,
        in_specs=[in_smem] * len(scalars) + [in_vmem] * len(operands) + [pl.BlockSpec(memory_space=pl.ANY)] * len(waits),
        out_specs=[in_vmem] * len(out_shape),
        out_shape=[jax.ShapeDtypeStruct(*shape) for shape in out_shape],
        scratch_shapes=[pltpu.VMEM(*shape) for shape in scratch],
        compiler_params=pltpu.CompilerParams(vmem_limit_bytes=mebibytes << 20),
        name=name,
    )(*scalars, *operands, *waits)


def fence(value, waits):
    return pl.pallas_call(
        lambda *refs: None,
        in_specs=[pl.BlockSpec(memory_space=pl.ANY)] * (1 + len(waits)),
        out_specs=pl.BlockSpec(memory_space=pl.ANY),
        out_shape=jax.ShapeDtypeStruct(value.shape, value.dtype),
        input_output_aliases={0: 0},
        name="fence",
    )(value, *waits)


def deal_kernel(in_ref, out_ref, *, chunks):
    group = out_ref.shape[0]
    for q in range(group):
        for c in range(chunks):
            lane = (c * group + q) * LANES
            out_ref[q, :, LANES * c : LANES * (c + 1)] = in_ref[:, lane : lane + LANES]


def deal(value, group, waits=()):
    n, features = value.shape
    kernel = functools.partial(deal_kernel, chunks=features // group // LANES)
    return call(kernel, [((group, n, features // group), value.dtype)], (value,), waits=waits, name="deal")[0]


def collect_kernel(*refs):
    *in_refs, out_ref = refs
    row = 0
    for ref in in_refs:
        group, n, width = ref.shape
        for q in range(group):
            for c in range(width // LANES):
                lane = (c * group + q) * LANES
                value = ref[q, :, LANES * c : LANES * (c + 1)]
                out_ref[row : row + n, lane : lane + LANES] = value.astype(out_ref.dtype)
        row += n


def collect(pieces, dtype, waits=()):
    group, _, width = pieces[0].shape
    shape = (sum(value.shape[1] for value in pieces), group * width)
    return call(collect_kernel, [(shape, dtype)], pieces, waits=waits, name="collect")[0]


def add_kernel(a_ref, b_ref, out_ref):
    out_ref[...] = (a_ref[...].astype(f32) + b_ref[...].astype(f32)).astype(out_ref.dtype)


def added(a, b, waits=()):
    return call(add_kernel, [(a.shape, a.dtype)], (a, b), waits=waits, name="added")[0]


def blocks_of(refs):
    return [ref.at[i] for ref in refs for i in range(ref.shape[0])]


def halve_kernel(*refs):
    *in_refs, first_stays, first_goes, second_stays, second_goes = refs
    n = len(in_refs) // 4
    parts = [blocks_of(in_refs[n * i : n * (i + 1)]) for i in range(4)]
    outs = (blocks_of((first_stays, first_goes)), blocks_of((second_stays, second_goes)))
    for kept, got, out in zip(parts[:2], parts[2:], outs):
        for kept_ref, got_ref, out_ref in zip(kept, got, out):
            out_ref[...] = (kept_ref[...].astype(f32) + got_ref[...].astype(f32)).astype(bf16)


def halve(kept, got, waits=()):
    n = sum(value.shape[0] for value in kept) // 4
    out = call(halve_kernel, [((n, *kept[0].shape[1:]), bf16)] * 4, (*kept, *got), waits=waits, name="halve")
    return out[0::2], out[1::2]


def merge_kernel(own_ref, away_ref, *refs):
    *got_refs, out_ref = refs
    start = 0
    for ref in got_refs:
        rows = slice(start, start + ref.shape[1])
        value = own_ref[:, rows, :].astype(f32) + ref[...].astype(f32) + away_ref[:, rows, :].astype(f32)
        out_ref[:, rows, :] = value.astype(bf16)
        start = rows.stop


def merge(own, got, away, waits=()):
    return call(merge_kernel, [(own.shape, bf16)], (own, away, *got), waits=waits, name="merge")[0]


def finish_kernel(where_ref, *refs):
    *in_refs, out_ref = refs
    width = in_refs[0].shape[-1]
    for part in range(2):
        kept_ref, got_ref = in_refs[part], in_refs[2 + part]
        lane = pl.ds(pl.multiple_of((where_ref[0] ^ part) * width, LANES), width)
        out_ref[:, :, lane] = (kept_ref[0].astype(f32) + got_ref[0].astype(f32)).astype(bf16)


def finish(where, kept, got, waits=()):
    _, rows, block, width = kept[0].shape
    return call(finish_kernel, [((rows, block, 2 * width), bf16)], (*kept, *got), (where,), waits, name="finish")[0]


def stats_kernel(x_ref, keep_ref, out_ref):
    total, block, features = x_ref.shape

    def row(column):
        return jnp.transpose(jnp.broadcast_to(column, (block, LANES)))[0:1, :]

    for r in range(total):
        out_ref[r, :block, :] = x_ref[r]
        x = x_ref[r].astype(f32)
        mean = jnp.sum(x, axis=-1, keepdims=True) * (1.0 / features)
        centred = x - mean
        inv = lax.rsqrt(jnp.sum(centred * centred, axis=-1, keepdims=True) * (1.0 / features) + EPSILON)
        rows = [keep_ref[r]]
        for value in (row(mean), row(inv)):
            for _ in range(3):
                upper = value.astype(bf16).astype(f32)
                rows.append(upper)
                value = value - upper
        rows = jnp.concatenate(rows + [jnp.zeros_like(rows[0])] * (STATS - len(rows)), axis=0)
        if block < LANES:
            rows = jnp.concatenate([rows, jnp.zeros((STATS, LANES - block), f32)], axis=1)
        out_ref[r, block:, :LANES] = rows.astype(bf16)
        out_ref[r, block:, LANES:] = jnp.zeros((STATS, features - LANES), bf16)


def stats(inputs, keep, waits):
    rows, block, features = inputs.shape
    return call(stats_kernel, [((rows, block + STATS, features), bf16)], (inputs, keep), waits=waits, name="stats")[0]


def norm_kernel(where_ref, gain_ref, shift_ref, *refs, count):
    block_refs, (normed_ref, stats_ref, keep_ref, *own_refs) = refs[:count], refs[count:]
    total, block, features = block_refs[0].shape
    block -= STATS
    half_width = features // 2
    per_block = BLOCK // block

    def device(r, x_ref, q):
        at = pl.ds(pl.multiple_of(q * block, block), block)
        spaced_at = pl.ds(pl.multiple_of(q // per_block * SPACED + q % per_block * block, 8), block)
        rows = x_ref[r, block:, :block].astype(f32)

        def column(*of):
            row = functools.reduce(jnp.add, [rows[k : k + 1, :] for k in of])
            return jnp.transpose(jnp.broadcast_to(row, (LANES, block)))

        keep_ref[r, spaced_at, :] = column(0)
        mean, inv = column(1, 2, 3), column(4, 5, 6)
        stats_ref[r, 0, at, :] = mean
        stats_ref[r, 1, at, :] = inv
        for part in range(2):
            lane = pl.multiple_of((where_ref[0] ^ part) * half_width, LANES)
            for j in range(half_width // LANES):
                x = x_ref[r, :block, pl.ds(lane + j * LANES, LANES)].astype(f32)
                out = slice(part * half_width + j * LANES, part * half_width + (j + 1) * LANES)
                normed_ref[r, at, out] = ((x - mean) * inv * gain_ref[:, out] + shift_ref[:, out]).astype(bf16)
        for ref in own_refs:
            for i in range(2):
                lane = pl.ds(pl.multiple_of(i * half_width + where_ref[3] * LANES, LANES), LANES)
                ref[r, i, at, :] = x_ref[r, :block, lane]

    for r in range(total):
        for d, ref in enumerate(block_refs):
            device(r, ref, where_ref[3] ^ d)


def norm(where, blocks, gain, shift, aligned, waits):
    rows, block, features = blocks[0].shape
    tokens = len(blocks) * (block - STATS)
    out_shape = [
        ((rows, tokens, features), bf16),
        ((rows, 2, tokens, LANES), f32),
        ((rows, tokens // BLOCK * SPACED, LANES), f32),
    ]
    if aligned:
        out_shape.append(((rows, 2, tokens, LANES), bf16))
    kernel = functools.partial(norm_kernel, count=len(blocks))
    return call(kernel, out_shape, (gain, shift, *blocks), (where,), waits, name="norm")


def weight_into(w_ref, parts):
    if len(parts) == 1:
        w_ref[...] = parts[0][...]
        return
    pieces = len(parts) // 2
    group, _, columns = parts[0].shape
    block = sum(part.shape[1] for part in parts[:pieces])
    for rank in range(2):
        start = 0
        for part in parts[rank * pieces : (rank + 1) * pieces]:
            rows = part.shape[1]
            for q in range(group):
                row = q * block + start
                w_ref[row : row + rows, rank * columns : (rank + 1) * columns] = part[q]
            start += rows


def slot_of(where_ref, s, slots):
    return lax.rem(where_ref[4] + s, slots)


def project_kernel(where_ref, normed_ref, rows_ref, *refs):
    *parts, sum_ref, vectors_ref, w_ref = refs
    weight_into(w_ref, parts)
    depth = w_ref.shape[0]
    total, slots = sum_ref.shape[:2]
    step = 2 * BLOCK
    vectors_ref[...] = jnp.dot(rows_ref[:, :depth], w_ref[...], preferred_element_type=f32)
    for r in range(total):

        @pl.loop(0, normed_ref.shape[1] // step)
        def _(j):
            at = pl.ds(pl.multiple_of(j * step, step), step)
            p = jnp.dot(normed_ref[r, at, :depth], w_ref[...], preferred_element_type=f32)
            for s in range(slots):
                sum_ref[r, s, at, :] = p[:, LANES * s : LANES * (s + 1)]


def project(where, normed, vector_rows, parts, depth, slots):
    rows, tokens, _ = normed.shape
    out_shape = [
        ((rows, slots, tokens, LANES), f32), ((vector_rows.shape[0], slots * LANES), f32), ((depth, slots * LANES), bf16),
    ]
    return call(project_kernel, out_shape, (normed, vector_rows, *parts), (where,), name="project")


def blocks_kernel(where_ref, normed_ref, rows_ref, sum_ref, some_ref, bias_ref, keep_ref, hfv_ref, init_ref, *refs):
    *parts, p_ref, seg_ref, lead_ref, end_ref, lead_end_ref, vectors_ref, w_ref = refs
    weight_into(w_ref, parts)
    depth = w_ref.shape[0]
    total, slots = p_ref.shape[:2]
    tiles = slots // 3
    step = 2 * BLOCK
    features = normed_ref.shape[2]
    by_column = some_ref[...] + jnp.dot(rows_ref[:, features - depth :], w_ref[...], preferred_element_type=f32)
    for s in range(slots):
        slot = slot_of(where_ref, s, slots)
        lanes = slice(LANES * s, LANES * (s + 1))
        vectors_ref[slot, 0:1, :] = jnp.sum(by_column[0:3, lanes], axis=0, keepdims=True)
        vectors_ref[slot, 1:2, :] = jnp.sum(by_column[3:6, lanes], axis=0, keepdims=True) + bias_ref[slot]
    for r in range(total):

        @pl.loop(0, normed_ref.shape[1] // step)
        def _(j):
            at = pl.ds(pl.multiple_of(j * step, step), step)
            p = jnp.dot(normed_ref[r, at, features - depth :], w_ref[...], preferred_element_type=f32)
            for s in range(slots):
                slot = slot_of(where_ref, s, slots)
                scale = jnp.where(slot < tiles, 1.0, 0.5)
                value = scale * (p[:, LANES * s : LANES * (s + 1)] + sum_ref[r, s, at, :] + bias_ref[slot])
                for k in range(2):
                    to = pl.ds(pl.multiple_of((2 * j + k) * SPACED, 8), BLOCK)
                    p_ref[r, slot, to, :] = value[BLOCK * k : BLOCK * (k + 1)]

        row_blocks(
            p_ref.at[r], keep_ref.at[r], hfv_ref, init_ref.at[r], seg_ref.at[r], lead_ref.at[r], end_ref.at[r],
            lead_end_ref.at[r],
        )


def blocks_forward(where, normed, vector_rows, some, some_vectors, bias, keep, hfv, init, parts, depth):
    rows, tokens, _ = normed.shape
    slots = bias.shape[0]
    tiles = slots // 3
    state = ((rows, 1, tiles * LANES), f32)
    length = tokens // BLOCK * SPACED
    out_shape = [
        ((rows, slots, length, LANES), f32), ((rows, tiles, length, LANES), f32),
        ((rows, tiles, spaced(COVERED), LANES), f32), state, state, ((slots, 2, LANES), f32), ((depth, slots * LANES), bf16),
    ]
    return call(
        blocks_kernel, out_shape, (normed, vector_rows, some, some_vectors, bias, keep, hfv, init, *parts), (where,),
        name="blocks_forward",
    )


def chain_step(p_ref, kb_ref, prev_ref, hfv, carried, row, next_row):
    tiles = len(hfv)
    keep = kb_ref[next_row, :]
    out = []
    for i, (y, prev) in enumerate(carried):
        tau = jnp.tanh(y)
        half = 0.5 * p_ref[i, row, :]
        mid, gap = 0.5 * prev + half, 0.5 * prev - half
        prev_ref[i, row, :] = prev
        reach = hfv[i] * keep
        out.append(
            ((p_ref[tiles + i, next_row, :] + reach * mid) + (reach * gap) * tau, (keep * mid) + (keep * gap) * tau)
        )
    return out


def begin(p_ref, hfv, previous, row):
    return [(p_ref[len(hfv) + i, row, :] + hfv[i] * prev, prev) for i, prev in enumerate(previous)]


def rows_of(token):
    return pl.ds(spaced(token), 1)


def run_chain(p_ref, kb_ref, prev_ref, hfv, carried, first, count):
    def body(j, now):
        for u in range(UNROLL):
            token = first + j * UNROLL + u
            now = chain_step(p_ref, kb_ref, prev_ref, hfv, now, rows_of(token), rows_of(token + 1))
        return now

    return lax.fori_loop(0, count // UNROLL, body, carried)


def row_blocks(p_ref, kb_ref, hfv_ref, init_ref, seg_ref, lead_ref, end_ref, lead_end_ref):
    tiles = seg_ref.shape[0]
    blocks = p_ref.shape[1] // SPACED
    hfv = tiles_of(hfv_ref, tiles)

    def seg_step(cells, step, store):
        row = pl.ds(step, blocks, stride=SPACED)
        keep = kb_ref[row, :]
        out = []
        for i, cell in enumerate(cells):
            prev = keep * cell
            tau = jnp.tanh(p_ref[tiles + i, row, :] + (hfv[i] * keep) * cell)
            half = 0.5 * p_ref[i, row, :]
            if store:
                seg_ref[i, row, :] = prev
            out.append((0.5 * prev + half) + (0.5 * prev - half) * tau)
        return out

    def run(cells, lead, first, token, count, store):
        def body(j, carried):
            cells, lead = carried
            for u in range(UNROLL):
                at = j * UNROLL + u
                cells = seg_step(cells, first + at, store)
                lead = chain_step(p_ref, kb_ref, lead_ref, hfv, lead, rows_of(token + at), rows_of(token + at + 1))
            return cells, lead

        return lax.fori_loop(0, count // UNROLL, body, (cells, lead))

    def moved(cells):
        return [jnp.concatenate([jnp.zeros((1, LANES), f32), cell[:-1]], axis=0) for cell in cells]

    cells = [jnp.zeros((blocks, LANES), f32) for _ in range(tiles)]
    lead = begin(p_ref, hfv, [kb_ref[0:1, :] * v for v in tiles_of(init_ref, tiles)], pl.ds(0, 1))
    cells, lead = run(cells, lead, BLOCK - EARLY, 0, EARLY, False)
    cells, lead = run(moved(cells), lead, 0, EARLY, BLOCK, False)
    cells, lead = run(moved(cells), lead, 0, EARLY + BLOCK, BLOCK, True)
    for i in range(tiles):
        end_ref[:, LANES * i : LANES * (i + 1)] = cells[i][-1:]
        lead_end_ref[:, LANES * i : LANES * (i + 1)] = lead[i][1]


def lead_kernel(p_ref, keep_ref, hfv_ref, start_ref, early_ref, lead_ref):
    rows, tiles = lead_ref.shape[:2]
    hfv = tiles_of(hfv_ref, tiles)
    lead_ref[:, :, : spaced(COVERED), :] = early_ref[...]
    for r in range(rows):
        carried = begin(p_ref.at[r], hfv, tiles_of(start_ref.at[r], tiles), rows_of(COVERED))
        run_chain(p_ref.at[r], keep_ref.at[r], lead_ref.at[r], hfv, carried, COVERED, LEAD - COVERED)


def lead_forward(p, keep, hfv, start, early):
    rows, tiles = early.shape[:2]
    out_shape = [((rows, tiles, spaced(LEAD), LANES), f32)]
    return call(lead_kernel, out_shape, (p, keep, hfv, start, early), name="lead_forward")[0]


def token_terms(prev, c, yf, yr, x, g, keep, hfv, hrv):
    tau_f = jnp.tanh(yf + hfv * prev)
    tau_r = jnp.tanh(yr + hrv * prev)
    f, omf, gate, omg = 0.5 + 0.5 * tau_f, 0.5 - 0.5 * tau_f, 0.5 + 0.5 * tau_r, 0.5 - 0.5 * tau_r
    cell = f * prev + omf * c
    gg = g * gate
    dr = gg * omg * (cell - x)
    e = (prev - c) * f * omf
    slope = f + e * (2.0 * hfv)
    return dict(
        cell=cell, hidden=gate * cell + omg * x, high=g * omg, gg=gg, dr=dr, e=e, omf=omf,
        a=keep * slope, b=keep * (slope * gg + dr * (2.0 * hrv)),
    )


def block_terms(p_ref, keep_ref, prev_ref, x_ref, g_ref, hfv, hrv, r, k, i):
    tiles = len(hfv)
    at = pl.ds(pl.multiple_of(k * SPACED, 8), BLOCK)
    devices = BLOCK // g_ref.shape[2]
    lanes = slice(LANES * i, LANES * (i + 1))
    g = jnp.concatenate([g_ref[k * devices + n, r, :, lanes].astype(f32) for n in range(devices)], axis=0)
    x = x_ref[r, i, pl.ds(pl.multiple_of(k * BLOCK, BLOCK), BLOCK), :].astype(f32)
    c, yf, yr = (p_ref[r, m * tiles + i, at, :] for m in range(3))
    return token_terms(prev_ref[i, at, :], c, yf, yr, x, g, keep_ref[r, at, :], hfv[i], hrv[i])


def run_back(a_ref, b_ref, d_ref, carried, count):
    def body(j, carried):
        base = pl.multiple_of(count - UNROLL * (j + 1), UNROLL)
        for u in reversed(range(UNROLL)):
            row = pl.ds(base + u, 1)
            now = []
            for i, d in enumerate(carried):
                if d_ref is not None:
                    d_ref[i, row, :] = d
                now.append(a_ref[i, row, :] * d + b_ref[i, row, :])
            carried = now
        return carried

    return lax.fori_loop(0, count // UNROLL, body, carried)


def entry_kernel(
    p_ref, keep_ref, seg_ref, x_ref, g_ref, hfv_ref, hrv_ref, start_ref, first_ref, back_ref, prev_ref, a_ref, b_ref
):
    rows, slots = p_ref.shape[:2]
    tiles = slots // 3
    hfv, hrv = tiles_of(hfv_ref, tiles), tiles_of(hrv_ref, tiles)
    blocks = -(-REACH // BLOCK)
    for r in range(rows):
        prev_ref[...] = seg_ref[r, :, : blocks * SPACED, :]
        start = [keep_ref[r, 0:1, :] * v for v in tiles_of(start_ref.at[r], tiles)]
        run_chain(p_ref.at[r], keep_ref.at[r], prev_ref, hfv, begin(p_ref.at[r], hfv, start, pl.ds(0, 1)), 0, REACH)
        first_ref[r] = prev_ref[:, : spaced(REACH), :]
        for k in range(blocks):
            for i in range(tiles):
                t = block_terms(p_ref, keep_ref, prev_ref, x_ref, g_ref, hfv, hrv, r, k, i)
                a_ref[i, BLOCK * k : BLOCK * (k + 1), :] = t["a"]
                b_ref[i, BLOCK * k : BLOCK * (k + 1), :] = t["b"]
        carried = run_back(a_ref, b_ref, None, [jnp.zeros((1, LANES), f32)] * tiles, blocks * BLOCK)
        for i in range(tiles):
            back_ref[r, :, LANES * i : LANES * (i + 1)] = carried[i]


def entry(p, keep, seg, x_own, g_own, hfv, hrv, start, waits):
    rows, slots, _, _ = p.shape
    tiles = slots // 3
    blocks = -(-REACH // BLOCK)
    length, count = blocks * SPACED, blocks * BLOCK
    return call(
        entry_kernel,
        [((rows, tiles, spaced(REACH), LANES), f32), ((rows, 1, tiles * LANES), f32)],
        (p, keep, seg, x_own, g_own, hfv, hrv, start),
        waits=waits,
        scratch=[((tiles, length, LANES), f32)] + [((tiles, count, LANES), f32)] * 2,
        name="entry",
    )


def backward_kernel(
    where_ref, p_ref, keep_ref, seg_ref, lead_ref, first_ref, x_ref, g_ref, hfv_ref, hrv_ref, carry_ref, vectors_ref,
    gp_ref, hidden_ref, high_ref, sums_ref, final_ref, means_ref,
    prev_ref, a_ref, b_ref, gg_ref, e_ref, omf_ref, dr_ref, d_ref,
):
    rows, slots = p_ref.shape[:2]
    tiles = slots // 3
    blocks = p_ref.shape[2] // SPACED
    hfv, hrv = tiles_of(hfv_ref, tiles), tiles_of(hrv_ref, tiles)
    devices, block = BLOCK // g_ref.shape[2], g_ref.shape[2]
    sums_ref[...] = jnp.zeros_like(sums_ref)
    for r in range(rows):
        prev_ref[...] = seg_ref[r]

        @pl.when(where_ref[0] == 0)
        def _():
            prev_ref[:, : spaced(LEAD), :] = lead_ref[r]

        @pl.when(where_ref[0] != 0)
        def _():
            prev_ref[:, : spaced(REACH), :] = first_ref[r]

        @pl.loop(0, blocks)
        def _(k):
            out = pl.ds(pl.multiple_of(k * BLOCK, BLOCK), BLOCK)
            for i in range(tiles):
                t = block_terms(p_ref, keep_ref, prev_ref, x_ref, g_ref, hfv, hrv, r, k, i)
                lanes = slice(LANES * i, LANES * (i + 1))
                for n in range(devices):
                    hidden_ref[k * devices + n, r, :, lanes] = t["hidden"][n * block : (n + 1) * block].astype(bf16)
                high_ref[r, i, out, :] = t["high"].astype(bf16)
                for ref, name in zip((a_ref, b_ref, gg_ref, e_ref, omf_ref, dr_ref), ("a", "b", "gg", "e", "omf", "dr")):
                    ref[i, out, :] = t[name]
                final_ref[r, :, lanes] = t["cell"][-1:]

        run_back(a_ref, b_ref, d_ref, tiles_of(carry_ref.at[r], tiles), blocks * BLOCK)

        @pl.loop(0, blocks)
        def _(k):
            at = pl.ds(pl.multiple_of(k * SPACED, 8), BLOCK)
            out = pl.ds(pl.multiple_of(k * BLOCK, BLOCK), BLOCK)
            first, second = jnp.zeros((BLOCK, LANES), f32), jnp.zeros((BLOCK, LANES), f32)
            for i in range(tiles):
                prev = prev_ref[i, at, :]
                u = d_ref[i, out, :] + gg_ref[i, out, :]
                df, dr = u * e_ref[i, out, :], dr_ref[i, out, :]
                dc = u * omf_ref[i, out, :]
                for m, value in enumerate((dc, df, dr)):
                    slot = m * tiles + i
                    lane = lax.rem(slot + slots - where_ref[4], slots) * LANES
                    gp_ref[r, out, pl.ds(pl.multiple_of(lane, LANES), LANES)] = value.astype(bf16)
                    first += value * vectors_ref[slot, 0:1, :]
                    second += value * ((1.0 if m == 0 else 2.0) * p_ref[r, slot, at, :] - vectors_ref[slot, 1:2, :])
                lanes = slice(LANES * i, LANES * (i + 1))
                for m, value in enumerate((df * prev, dr * prev, df, dr)):
                    sums_ref[m : m + 1, lanes] += jnp.sum(value, axis=0, keepdims=True)
                for m, value in enumerate((dc, df, dr)):
                    lane = lax.rem(m * tiles + i + slots - where_ref[4], slots) * LANES
                    at_lane = pl.ds(pl.multiple_of(lane, LANES), LANES)
                    sums_ref[7:8, at_lane] += jnp.sum(value, axis=0, keepdims=True)
            means_ref[r, 0, out, :] = first
            means_ref[r, 1, out, :] = second


def backward(where, p, keep, seg, lead, first, x_own, g_own, hfv, hrv, carry, vectors):
    rows, slots, length, _ = p.shape
    tiles = slots // 3
    tokens = length // SPACED * BLOCK
    width = tiles * LANES
    return call(
        backward_kernel,
        [
            ((rows, tokens, 3 * width), bf16),
            (g_own.shape, bf16),
            ((rows, tiles, tokens, LANES), bf16),
            ((8, 3 * width), f32),
            ((rows, 1, width), f32),
            ((rows, 2, tokens, LANES), f32),
        ],
        (p, keep, seg, lead, first, x_own, g_own, hfv, hrv, carry, vectors),
        (where,),
        scratch=[((tiles, length, LANES), f32)] + [((tiles, tokens, LANES), f32)] * 7,
        name="backward",
    )


def weight_back_kernel(normed_ref, gp_ref, sums_ref, *refs, part, group, cuts):
    count = sum(len(rows) for rows in cuts)
    w_refs, (by_feature_ref, *out_refs) = refs[: len(refs) - count - 1], refs[len(refs) - count - 1 :]
    total, _, features = normed_ref.shape
    row_block = features // 2 // group
    columns = out_refs[0].shape[2]
    span = 2 * LANES
    devices = span // row_block
    lane_tiles = gp_ref.shape[2] // LANES
    for k in range(group // devices):
        lane = slice(part * (features // 2) + k * span, part * (features // 2) + (k + 1) * span)
        p = sum(
            lax.dot_general(normed_ref[r, :, lane], gp_ref[r], (((0,), (0,)), ((), ())), preferred_element_type=f32)
            for r in range(total)
        )
        first = w_refs[0].shape[0]
        w = [w_refs[0][lane.start : min(lane.stop, first), :]] if lane.start < first else []
        if lane.stop > first:
            w.append(w_refs[1][max(lane.start - first, 0) : lane.stop - first, :])
        w = jnp.concatenate(w).astype(f32)
        for m, value in enumerate((p * w, w * sums_ref[7:8, :])):
            value = functools.reduce(jnp.add, [value[:, LANES * j : LANES * (j + 1)] for j in range(lane_tiles)])
            by_feature_ref[m : m + 1, k * span : (k + 1) * span] = jnp.sum(jnp.transpose(value), axis=0, keepdims=True)
        p = p.astype(bf16)
        outs = iter(out_refs)
        for split, rows in enumerate(cuts):
            start = 0
            for step in rows:
                out_ref = next(outs)
                for n in range(devices):
                    row = n * row_block + start
                    out_ref[k * devices + n] = p[row : row + step, split * columns : (split + 1) * columns]
                start += step


def weight_back(normed, gp, sums, weights, part, group, cuts, waits):
    features = normed.shape[2]
    columns = gp.shape[2] // len(cuts)
    kernel = functools.partial(weight_back_kernel, part=part, group=group, cuts=cuts)
    out_shape = [((2, features // 2), f32)] + [((group, step, columns), bf16) for rows in cuts for step in rows]
    return call(kernel, out_shape, (normed, gp, sums, *weights), waits=waits, name="weight_back")


def norm_back_kernel(where_ref, stats_ref, means_ref, gp_ref, gain_ref, *refs, orders, with_high):
    count = len(orders[0])
    x_refs, refs = refs[: 2 * count], refs[2 * count :]
    *w_refs, high_ref = refs[:-10]
    all_out_refs, (some_ref, gn_ref) = refs[-10:-2], refs[-2:]
    half_count, total, block, half_width = all_out_refs[0].shape
    features = 2 * half_width
    together = gn_ref.shape[0] // block
    for odd in (1, 0):
        out_refs = all_out_refs[4 * (1 - odd) : 4 * (2 - odd)]
        for r in range(total):
            for d in range(0, count, together):
                tokens = []
                for n in range(together):
                    place = where_ref[3] ^ (orders[0][d + n] | odd)
                    tokens.append(pl.ds(pl.multiple_of(place * block, 16), block))
                    some_ref[n * block : (n + 1) * block, :] = gp_ref[r, tokens[n], :]
                lane = 0
                for w_ref in w_refs:
                    rows = w_ref.shape[0]
                    gn_ref[:, lane : lane + rows] = lax.dot_general(
                        some_ref[...], w_ref[...], (((1,), (1,)), ((), ())), preferred_element_type=f32
                    )
                    lane += rows
                for n in range(together):
                    x_ref = x_refs[orders[0][d + n] | odd]
                    mean, inv = stats_ref[r, 0, tokens[n], :], stats_ref[r, 1, tokens[n], :]
                    first, second = (
                        jnp.sum(means_ref[r, m, tokens[n], :], axis=-1, keepdims=True) * (1.0 / features)
                        for m in range(2)
                    )
                    slope = inv * inv * second
                    rest = inv * first - slope * mean
                    for part in range(2):
                        at_d = orders[part].index(orders[0][d + n])
                        out_ref = out_refs[2 * part + at_d // half_count]
                        start = pl.multiple_of((where_ref[0] ^ part) * half_width, LANES)
                        if with_high:
                            high = high_ref[r, where_ref[0] ^ part, tokens[n], :].astype(f32)
                        for j in range(half_width // LANES):
                            at = slice(part * half_width + LANES * j, part * half_width + LANES * (j + 1))
                            value = inv * (gn_ref[n * block : (n + 1) * block, at] * gain_ref[:, at])
                            x = x_ref[r, :block, pl.ds(start + LANES * j, LANES)].astype(f32)
                            value -= slope * x + rest
                            if with_high:
                                value += jnp.where(where_ref[3] == j, high, 0.0)
                            out_ref[at_d % half_count, r, :, LANES * j : LANES * (j + 1)] = value.astype(bf16)


def norm_back(where, blocks, orders, stats, means, gp, weights, gain, high, with_high, waits):
    rows, block, features = blocks[0].shape
    block -= STATS
    together = 2 * LANES // block
    out = call(
        functools.partial(norm_back_kernel, orders=orders, with_high=with_high),
        [((len(blocks) // 4, rows, block, features // 2), bf16)] * 8,
        (stats, means, gp, gain, *blocks, *weights, high), (where,), waits,
        scratch=[((together * block, gp.shape[2]), bf16), ((together * block, features), f32)],
        name="norm_back",
    )
    return out[:4], out[4:]


def totals_kernel(where_ref, sums_ref, own_ref, other_ref, gain_ref, shift_ref, out_ref, *, chunk):
    half_width = own_ref.shape[1]
    out_ref[...] = jnp.zeros_like(out_ref)
    for i in range(2):
        lane = pl.ds(pl.multiple_of(i * chunk + where_ref[3] * LANES, LANES), LANES)
        out_ref[0:4, lane] = sums_ref[0:4, LANES * i : LANES * (i + 1)]
    for part, ref in enumerate((own_ref, other_ref)):
        lane = pl.ds(pl.multiple_of((where_ref[0] ^ part) * half_width, LANES), half_width)
        at = slice(part * half_width, (part + 1) * half_width)
        out_ref[4:5, lane] = (ref[0:1, :] - shift_ref[:, at] * ref[1:2, :]) / gain_ref[:, at]
        out_ref[5:6, lane] = ref[1:2, :]


def bf16_parts(row):
    rows = []
    for _ in range(3):
        upper = lax.reduce_precision(row, 8, 7)
        rows.append(upper.astype(bf16))
        row = row - upper
    return rows


def local(inputs, weight, gain, shift, forget_vec, reset_vec, forget_bias, reset_bias, initial, resets, grad_out):
    rows, block_len, features = inputs.shape
    row_block, columns_here = weight.shape
    sections = lax.axis_size("fsdp")
    ranks = lax.axis_size("dp")
    group = sections // 2
    tokens = group * block_len
    index = lax.axis_index("fsdp")
    half, place = index // group, index % group
    rank = lax.axis_index("dp")
    first_half = half == 0
    groups = [list(range(group)), list(range(group, sections))]
    chunk = math.gcd(features, columns_here)
    chunks, piece = features // chunk, chunk // group
    width = chunks * piece
    tiles = width // LANES
    slots = 3 * tiles
    parts = columns_here // chunk
    columns = parts * piece
    aligned = piece == LANES and chunks == 2
    paired = ranks == 2 and aligned
    turn = rank * (columns // LANES) if paired else jnp.zeros_like(rank)
    where = jnp.stack([half, rank, index % 2, place, turn]).astype(jnp.int32)
    bits = [1 << b for b in range(1, group.bit_length() - 1)]
    ways = (bits[::-1], bits)
    orders = []
    for way in ways:
        order = [0]
        for bit in way:
            order += [d | bit for d in order]
        orders.append(order)

    def across(value):
        return lax.ppermute(value, "fsdp", [(j, (j + group) % sections) for j in range(sections)])

    def flipped(value, bit):
        return lax.ppermute(value, "fsdp", [(j, j ^ bit) for j in range(sections)])

    def swapped(value):
        return lax.ppermute(value, "dp", [(0, 1), (1, 0)])

    def shared(value):
        return lax.all_to_all(value, "fsdp", 0, 0, tiled=True, axis_index_groups=groups)

    def own(vector):
        return lax.dynamic_index_in_dim(vector.reshape(-1, chunks, group, piece), place, 2, False).reshape(-1, width)

    def halves_turned(vector):
        low, high = vector[..., : features // 2], vector[..., features // 2 :]
        return jnp.concatenate([jnp.where(first_half, low, high), jnp.where(first_half, high, low)], axis=-1)

    def dealt(value, waits=()):
        if aligned:
            return deal(value, group, waits)
        n, wide = value.shape
        return value.reshape(n, wide // chunk, group, piece).transpose(2, 0, 1, 3).reshape(group, n, wide // group)

    def collected(pieces, dtype, waits=()):
        if aligned:
            return collect(pieces, dtype, waits)
        wide = pieces[0].shape[2]
        back = lambda v: v.reshape(group, -1, wide // piece, piece).transpose(1, 2, 0, 3).reshape(-1, wide * group)
        return jnp.concatenate([back(v) for v in pieces]).astype(dtype)

    mine = shared(dealt(weight))
    theirs = across(mine)
    beside = swapped(mine) if paired else mine
    blocks = {0: stats(inputs, (1 - resets).astype(f32)[:, None, :], (mine,))}
    for bit in bits[::-1]:
        blocks |= {d | bit: flipped(value, bit) for d, value in blocks.items()}
    blocks = {d: fence(value, (theirs, beside)) for d, value in blocks.items()}
    blocks |= {d | 1: flipped(value, 1) for d, value in blocks.items()}
    blocks = [blocks[d] for d in range(group)]
    early_rows = features // 2
    if paired:
        early, late = [mine, beside], [theirs, swapped(theirs)]
    else:
        early, late = (
            [lax.all_gather(v.reshape(-1, columns), "dp", axis=1, tiled=True)] for v in (mine, theirs)
        )
    hfv, hrv = 0.5 * own(forget_vec), 0.5 * own(reset_vec)
    bias = jnp.concatenate([jnp.zeros((1, width), f32), own(forget_bias), own(reset_bias)]).reshape(-1, 1, LANES)
    gain_row, shift_row = halves_turned(gain)[None], halves_turned(shift)[None]
    vector_rows = [*bf16_parts(gain_row), *bf16_parts(shift_row)]
    vector_rows = jnp.pad(jnp.concatenate(vector_rows), ((0, 10), (0, 0)))
    g_own = shared(dealt(grad_out.reshape(-1, features)).reshape(group, rows, block_len, width))
    normed, token_stats, keep, *x_own = norm(where, blocks, gain_row, shift_row, aligned, (g_own,))
    if aligned:
        x_own = x_own[0]
    else:
        in_order = jnp.stack(blocks)[place ^ jnp.arange(group)][:, :, :block_len].swapaxes(0, 1)
        x_own = own(in_order.reshape(rows * tokens, features)).reshape(rows, tokens, tiles, LANES).swapaxes(1, 2)
    some, some_vectors, early_weight = project(where, normed, vector_rows, early, early_rows, slots)
    p, seg, lead, end, lead_end, vectors, late_weight = blocks_forward(
        where, normed, vector_rows, some, some_vectors, bias, keep, hfv, own(initial)[:, None, :], late,
        features - early_rows,
    )
    weights = (early_weight, late_weight)
    start = across(end)
    lead = lead_forward(p, keep, hfv, lead_end, lead)
    first, back = entry(p, keep, seg, x_own, g_own, hfv, hrv, start, ())
    carry = jnp.where(first_half, across(back), 0.0)
    gp, hidden_own, high_own, sums, final, means = backward(
        where, p, keep, seg, lead, first, x_own, g_own, hfv, hrv, carry, vectors
    )

    mask = (jnp.arange(group) == place)[:, None]

    splits = 2 if paired else 1
    by_feature_other, *away = weight_back(normed, gp, sums, weights, 1, group, [(row_block,)] * splits, ())
    away_got = swapped(away[1]) if paired else None

    sent, kept = norm_back(
        where, blocks, orders, token_stats, means, gp, weights, gain_row, high_own, aligned, (by_feature_other,)
    )
    if not aligned:
        spread = high_own.swapaxes(1, 2).reshape(rows, group, block_len, chunks, 1, piece).swapaxes(0, 1)
        spread = jnp.where(mask, spread.astype(f32), 0.0).reshape(group, rows, block_len, features)
        spread = halves_turned(spread)[place ^ jnp.arange(group)]
        halves = (spread[..., : features // 2], spread[..., features // 2 :])
        n = group // 4

        def with_high(arrays, odd):
            add = [half[d | odd] for half, order in zip(halves, orders) for d in order]
            return [(v.astype(f32) + jnp.stack(add[i * n : (i + 1) * n])).astype(bf16) for i, v in enumerate(arrays)]

        sent, kept = with_high(sent, 1), with_high(kept, 0)
    got = [flipped(value, 1) for value in sent]
    if paired:
        away = added(away[0], away_got, kept[:1])
    else:
        away = lax.psum_scatter(away[0], "dp", scatter_dimension=2, tiled=True)
    z_got = across(away)
    kept, sent = halve(kept, got)
    bit_pairs = list(zip(*(w[::-1] for w in ways)))
    got = [flipped(value, bit) for value, bit in zip(sent, bit_pairs.pop(0))]
    cuts = [(row_block,), (row_block // 2,) * 2][:splits]
    by_feature_own, *here = weight_back(normed, gp, sums, weights, 0, group, cuts, (away,))
    if paired:
        here_got = [swapped(value) for value in here[1:]]
    else:
        here = lax.psum_scatter(here[0], "dp", scatter_dimension=2, tiled=True)
    hidden = collected([shared(hidden_own).reshape(group, -1, width)], bf16).reshape(rows, block_len, features)

    if aligned:
        totals = call(
            functools.partial(totals_kernel, chunk=chunk), [((8, features), f32)],
            (sums, by_feature_own, by_feature_other, gain_row, shift_row), (where,), name="totals",
        )[0]
    else:
        spread = jnp.where(mask, sums[:4, :width].reshape(4, chunks, 1, piece), 0.0).reshape(4, features)
        product, shift_sum = jnp.concatenate([by_feature_own, by_feature_other], axis=1)
        gain_sum = (product - shift_row[0] * shift_sum) / gain_row[0]
        totals = jnp.concatenate([spread, halves_turned(jnp.stack([gain_sum, shift_sum]))], axis=0)
    for way in bit_pairs:
        kept, sent = halve(kept, got, (hidden,))
        got = [flipped(value, bit) for value, bit in zip(sent, way)]
    grad_inputs = finish(where, kept, got)
    for bit in [1 << b for b in range(group.bit_length() - 1)]:
        totals = added(totals, flipped(totals, bit))
    waits = (grad_inputs, totals)
    value = merge(here[0], here_got, z_got, waits) if paired else added(here, z_got, waits)
    grad_weight = collected([shared(value)], f32)
    totals = added(totals, swapped(totals)) if ranks == 2 else lax.psum(totals, "dp")
    totals = added(totals, across(totals))

    own_width = features // sections
    if piece == own_width and chunks == 2:
        final = final[:, 0]
        low_part = lax.ppermute(final[:, :piece], "fsdp", [(j + group, j) for j in range(group)])
        final_state = jnp.where(first_half, low_part, final[:, piece:])
    else:
        spread = jnp.where(mask, final.reshape(rows, chunks, 1, piece), 0.0).reshape(rows, features)
        spread = lax.psum(jnp.where(first_half, 0.0, spread), "fsdp")
        final_state = lax.dynamic_slice_in_dim(spread, index * own_width, own_width, 1)

    return (hidden, grad_inputs, final_state, grad_weight, *[totals[i] for i in range(6)])


def solution(mesh):
    in_specs = (
        P("dp", "fsdp", None), P("fsdp", "dp"), P(), P(), P(), P(), P(), P(),
        P("dp", None), P("dp", "fsdp"), P("dp", "fsdp", None),
    )
    out_specs = (
        P("dp", "fsdp", None), P("dp", "fsdp", None), P("dp", "fsdp"), P("fsdp", "dp"), P(), P(), P(), P(), P(), P(),
    )
    return jax.shard_map(local, mesh=mesh, in_specs=in_specs, out_specs=out_specs, check_vma=False)
```

```python
import functools
import math

import jax
import jax.numpy as jnp
from jax import lax
from jax.experimental import pallas as pl
from jax.experimental.pallas import tpu as pltpu
from jax.sharding import PartitionSpec as P

SENT = 128
LEAD = 768
REACH = 192
EPSILON = 1e-05
LANES = 128
BLOCK = 128
SPACED = 136
EARLY = REACH - BLOCK
COVERED = EARLY + 2 * BLOCK
STATS = 16
SPARE = 16
UNROLL = 8
f32 = jnp.float32
bf16 = jnp.bfloat16


def spaced(token):
    return token + (SPACED - BLOCK) * (token // BLOCK)


def tiles_of(ref, count):
    return [ref[:, LANES * i : LANES * (i + 1)] for i in range(count)]


def call(kernel, out_shape, operands, scalars=(), waits=(), scratch=(), mebibytes=14, name=None):
    in_vmem, in_smem = pl.BlockSpec(memory_space=pltpu.VMEM), pl.BlockSpec(memory_space=pltpu.SMEM)
    before = len(scalars) + len(operands)

    def body(*refs):
        kernel(*refs[:before], *refs[before + len(waits) :])

    return pl.pallas_call(
        body,
        in_specs=[in_smem] * len(scalars) + [in_vmem] * len(operands) + [pl.BlockSpec(memory_space=pl.ANY)] * len(waits),
        out_specs=[in_vmem] * len(out_shape),
        out_shape=[jax.ShapeDtypeStruct(*shape) for shape in out_shape],
        scratch_shapes=[pltpu.VMEM(*shape) for shape in scratch],
        compiler_params=pltpu.CompilerParams(vmem_limit_bytes=mebibytes << 20),
        name=name,
    )(*scalars, *operands, *waits)


def fence(value, waits):
    return pl.pallas_call(
        lambda *refs: None,
        in_specs=[pl.BlockSpec(memory_space=pl.ANY)] * (1 + len(waits)),
        out_specs=pl.BlockSpec(memory_space=pl.ANY),
        out_shape=jax.ShapeDtypeStruct(value.shape, value.dtype),
        input_output_aliases={0: 0},
        name="fence",
    )(value, *waits)


def deal_kernel(in_ref, out_ref, *, chunks):
    group = out_ref.shape[0]
    for q in range(group):
        for c in range(chunks):
            lane = (c * group + q) * LANES
            out_ref[q, :, LANES * c : LANES * (c + 1)] = in_ref[:, lane : lane + LANES]


def deal(value, group, waits=()):
    n, features = value.shape
    kernel = functools.partial(deal_kernel, chunks=features // group // LANES)
    return call(kernel, [((group, n, features // group), value.dtype)], (value,), waits=waits, name="deal")[0]


def collect_kernel(*refs):
    *in_refs, out_ref = refs
    row = 0
    for ref in in_refs:
        group, n, width = ref.shape
        for q in range(group):
            for c in range(width // LANES):
                lane = (c * group + q) * LANES
                value = ref[q, :, LANES * c : LANES * (c + 1)]
                out_ref[row : row + n, lane : lane + LANES] = value.astype(out_ref.dtype)
        row += n


def collect(pieces, dtype, waits=()):
    group, _, width = pieces[0].shape
    shape = (sum(value.shape[1] for value in pieces), group * width)
    return call(collect_kernel, [(shape, dtype)], pieces, waits=waits, name="collect")[0]


def add_kernel(a_ref, b_ref, out_ref):
    b = b_ref[...] if b_ref.shape == a_ref.shape else b_ref[:, : a_ref.shape[1]]
    out_ref[...] = (a_ref[...].astype(f32) + b.astype(f32)).astype(out_ref.dtype)


def added(a, b, waits=()):
    return call(add_kernel, [(a.shape, a.dtype)], (a, b), waits=waits, name="added")[0]


def blocks_of(refs):
    return [ref.at[i] for ref in refs for i in range(ref.shape[0])]


def halve_kernel(*refs, width):
    *in_refs, first_stays, first_goes, second_stays, second_goes = refs
    n = len(in_refs) // 4
    parts = [blocks_of(in_refs[n * i : n * (i + 1)]) for i in range(4)]
    for part, (stays, goes) in enumerate(((first_stays, first_goes), (second_stays, second_goes))):
        out = blocks_of([stays, goes])
        for out_ref, a_ref, b_ref in zip(out, parts[part], parts[2 + part]):
            out_ref[:, :, :width] = (a_ref[:, :, :width].astype(f32) + b_ref[:, :, :width].astype(f32)).astype(bf16)
            there = a_ref.shape[2]
            if there > width:
                out_ref[:, :, width:there] = a_ref[:, :, width:]
                out_ref[:, :, there:] = b_ref[:, :, width:]


def halve(kept, got, width, waits=()):
    n = sum(value.shape[0] for value in kept) // 4
    *shape, there = kept[0].shape[1:]
    out = call(
        functools.partial(halve_kernel, width=width), [((n, *shape, 2 * there - width), bf16)] * 4, (*kept, *got),
        waits=waits, name="halve",
    )
    return out[0::2], out[1::2]


def merge_kernel(own_ref, away_ref, *refs):
    *got_refs, out_ref = refs
    start = 0
    for ref in got_refs:
        rows = slice(start, start + ref.shape[1])
        value = own_ref[:, rows, :].astype(f32) + ref[...].astype(f32) + away_ref[:, rows, :].astype(f32)
        out_ref[:, rows, :] = value.astype(bf16)
        start = rows.stop


def merge(own, got, away, waits=()):
    return call(merge_kernel, [(own.shape, bf16)], (own, away, *got), waits=waits, name="merge")[0]


def finish_kernel(where_ref, *refs, sources):
    in_refs, (out_ref, *hidden_ref) = refs[:4], refs[4:]
    half_width = out_ref.shape[2] // 2
    for part in range(2):
        kept_ref, got_ref = in_refs[part], in_refs[2 + part]
        value = kept_ref[0, :, :, :half_width].astype(f32) + got_ref[0, :, :, :half_width].astype(f32)
        lane = pl.multiple_of((where_ref[0] ^ part) * half_width, LANES)
        out_ref[:, :, pl.ds(lane, half_width)] = value.astype(bf16)
        if hidden_ref:
            tiles = [ref[0, :, :, at : at + LANES] for ref in (kept_ref, got_ref) for at in range(half_width, ref.shape[3], LANES)]
            for value, source in zip(tiles, sources[part]):
                lane = pl.multiple_of(part * half_width + (where_ref[3] ^ source) * LANES, LANES)
                hidden_ref[0][:, :, pl.ds(lane, LANES)] = value


def finish(where, kept, got, features, sources, waits=()):
    _, rows, block, there = kept[0].shape
    out_shape = [((rows, block, features), bf16)] * (1 + (there > features // 2))
    kernel = functools.partial(finish_kernel, sources=sources)
    return call(kernel, out_shape, (*kept, *got), (where,), waits, name="finish")


def stats_kernel(x_ref, keep_ref, out_ref):
    total, block, features = x_ref.shape

    def row(column):
        return jnp.transpose(jnp.broadcast_to(column, (block, LANES)))[0:1, :]

    for r in range(total):
        out_ref[r, :block, :] = x_ref[r]
        x = x_ref[r].astype(f32)
        mean = jnp.sum(x, axis=-1, keepdims=True) * (1.0 / features)
        centred = x - mean
        inv = lax.rsqrt(jnp.sum(centred * centred, axis=-1, keepdims=True) * (1.0 / features) + EPSILON)
        rows = [keep_ref[r]]
        for value in (row(mean), row(inv)):
            for _ in range(3):
                upper = value.astype(bf16).astype(f32)
                rows.append(upper)
                value = value - upper
        rows = jnp.concatenate(rows + [jnp.zeros_like(rows[0])] * (STATS - len(rows)), axis=0)
        if block < LANES:
            rows = jnp.concatenate([rows, jnp.zeros((STATS, LANES - block), f32)], axis=1)
        out_ref[r, block:, :LANES] = rows.astype(bf16)
        out_ref[r, block:, LANES:] = jnp.zeros((STATS, features - LANES), bf16)


def stats(inputs, keep, waits):
    rows, block, features = inputs.shape
    return call(stats_kernel, [((rows, block + STATS, features), bf16)], (inputs, keep), waits=waits, name="stats")[0]


def norm_kernel(where_ref, gain_ref, shift_ref, *refs, count):
    block_refs, (normed_ref, stats_ref, keep_ref, *own_refs) = refs[:count], refs[count:]
    total, block, features = block_refs[0].shape
    block -= STATS
    half_width = features // 2
    per_block = BLOCK // block

    def device(r, x_ref, q):
        at = pl.ds(pl.multiple_of(q * block, block), block)
        spaced_at = pl.ds(pl.multiple_of(q // per_block * SPACED + q % per_block * block, 8), block)
        rows = x_ref[r, block:, :block].astype(f32)

        def column(*of):
            row = functools.reduce(jnp.add, [rows[k : k + 1, :] for k in of])
            return jnp.transpose(jnp.broadcast_to(row, (LANES, block)))

        keep_ref[r, spaced_at, :] = column(0)
        mean, inv = column(1, 2, 3), column(4, 5, 6)
        stats_ref[r, 0, at, :] = mean
        stats_ref[r, 1, at, :] = inv
        for part in range(2):
            lane = pl.multiple_of((where_ref[0] ^ part) * half_width, LANES)
            for j in range(half_width // LANES):
                x = x_ref[r, :block, pl.ds(lane + j * LANES, LANES)].astype(f32)
                out = slice(part * half_width + j * LANES, part * half_width + (j + 1) * LANES)
                normed_ref[r, at, out] = ((x - mean) * inv * gain_ref[:, out] + shift_ref[:, out]).astype(bf16)
        for ref in own_refs:
            for i in range(2):
                lane = pl.ds(pl.multiple_of(i * half_width + where_ref[3] * LANES, LANES), LANES)
                ref[r, i, at, :] = x_ref[r, :block, lane]

    for r in range(total):
        for d, ref in enumerate(block_refs):
            device(r, ref, where_ref[3] ^ d)


def norm(where, blocks, gain, shift, aligned, waits):
    rows, block, features = blocks[0].shape
    tokens = len(blocks) * (block - STATS)
    out_shape = [
        ((rows, tokens, features), bf16),
        ((rows, 2, tokens, LANES), f32),
        ((rows, tokens // BLOCK * SPACED, LANES), f32),
    ]
    if aligned:
        out_shape.append(((rows, 2, tokens, LANES), bf16))
    kernel = functools.partial(norm_kernel, count=len(blocks))
    return call(kernel, out_shape, (gain, shift, *blocks), (where,), waits, name="norm")


def weight_into(w_ref, parts):
    if len(parts) == 1:
        w_ref[...] = parts[0][...]
        return
    pieces = len(parts) // 2
    group, _, columns = parts[0].shape
    block = sum(part.shape[1] for part in parts[:pieces])
    for rank in range(2):
        start = 0
        for part in parts[rank * pieces : (rank + 1) * pieces]:
            rows = part.shape[1]
            for q in range(group):
                row = q * block + start
                w_ref[row : row + rows, rank * columns : (rank + 1) * columns] = part[q]
            start += rows


def slot_of(where_ref, s, slots):
    return lax.rem(where_ref[4] + s, slots)


def project_kernel(where_ref, normed_ref, rows_ref, *refs):
    *parts, sum_ref, vectors_ref, w_ref = refs
    weight_into(w_ref, parts)
    depth = w_ref.shape[0]
    total, slots = sum_ref.shape[:2]
    step = 2 * BLOCK
    vectors_ref[...] = jnp.dot(rows_ref[:, :depth], w_ref[...], preferred_element_type=f32)
    for r in range(total):

        @pl.loop(0, normed_ref.shape[1] // step)
        def _(j):
            at = pl.ds(pl.multiple_of(j * step, step), step)
            p = jnp.dot(normed_ref[r, at, :depth], w_ref[...], preferred_element_type=f32)
            for s in range(slots):
                sum_ref[r, s, at, :] = p[:, LANES * s : LANES * (s + 1)]


def project(where, normed, vector_rows, parts, depth, slots):
    rows, tokens, _ = normed.shape
    out_shape = [
        ((rows, slots, tokens, LANES), f32), ((vector_rows.shape[0], slots * LANES), f32), ((depth, slots * LANES), bf16),
    ]
    return call(project_kernel, out_shape, (normed, vector_rows, *parts), (where,), name="project")


def blocks_kernel(where_ref, normed_ref, rows_ref, sum_ref, some_ref, bias_ref, keep_ref, hfv_ref, init_ref, *refs):
    *parts, p_ref, seg_ref, lead_ref, end_ref, lead_end_ref, vectors_ref, w_ref = refs
    weight_into(w_ref, parts)
    depth = w_ref.shape[0]
    total, slots = p_ref.shape[:2]
    tiles = slots // 3
    step = 2 * BLOCK
    features = normed_ref.shape[2]
    by_column = some_ref[...] + jnp.dot(rows_ref[:, features - depth :], w_ref[...], preferred_element_type=f32)
    for s in range(slots):
        slot = slot_of(where_ref, s, slots)
        lanes = slice(LANES * s, LANES * (s + 1))
        vectors_ref[slot, 0:1, :] = jnp.sum(by_column[0:3, lanes], axis=0, keepdims=True)
        vectors_ref[slot, 1:2, :] = jnp.sum(by_column[3:6, lanes], axis=0, keepdims=True) + bias_ref[slot]
    for r in range(total):

        @pl.loop(0, normed_ref.shape[1] // step)
        def _(j):
            at = pl.ds(pl.multiple_of(j * step, step), step)
            p = jnp.dot(normed_ref[r, at, features - depth :], w_ref[...], preferred_element_type=f32)
            for s in range(slots):
                slot = slot_of(where_ref, s, slots)
                scale = jnp.where(slot < tiles, 1.0, 0.5)
                value = scale * (p[:, LANES * s : LANES * (s + 1)] + sum_ref[r, s, at, :] + bias_ref[slot])
                for k in range(2):
                    to = pl.ds(pl.multiple_of((2 * j + k) * SPACED, 8), BLOCK)
                    p_ref[r, slot, to, :] = value[BLOCK * k : BLOCK * (k + 1)]

        row_blocks(
            p_ref.at[r], keep_ref.at[r], hfv_ref, init_ref.at[r], seg_ref.at[r], lead_ref.at[r], end_ref.at[r],
            lead_end_ref.at[r],
        )


def blocks_forward(where, normed, vector_rows, some, some_vectors, bias, keep, hfv, init, parts, depth):
    rows, tokens, _ = normed.shape
    slots = bias.shape[0]
    tiles = slots // 3
    state = ((rows, 1, tiles * LANES), f32)
    length = tokens // BLOCK * SPACED
    out_shape = [
        ((rows, slots, length, LANES), f32), ((rows, tiles, length, LANES), f32),
        ((rows, tiles, spaced(COVERED), LANES), f32), state, state, ((slots, 2, LANES), f32), ((depth, slots * LANES), bf16),
    ]
    return call(
        blocks_kernel, out_shape, (normed, vector_rows, some, some_vectors, bias, keep, hfv, init, *parts), (where,),
        name="blocks_forward",
    )


def chain_step(p_ref, kb_ref, prev_ref, hfv, carried, row, next_row):
    tiles = len(hfv)
    keep = kb_ref[next_row, :]
    out = []
    for i, (y, prev) in enumerate(carried):
        tau = jnp.tanh(y)
        half = 0.5 * p_ref[i, row, :]
        mid, gap = 0.5 * prev + half, 0.5 * prev - half
        prev_ref[i, row, :] = prev
        reach = hfv[i] * keep
        out.append(
            ((p_ref[tiles + i, next_row, :] + reach * mid) + (reach * gap) * tau, (keep * mid) + (keep * gap) * tau)
        )
    return out


def begin(p_ref, hfv, previous, row):
    return [(p_ref[len(hfv) + i, row, :] + hfv[i] * prev, prev) for i, prev in enumerate(previous)]


def rows_of(token):
    return pl.ds(spaced(token), 1)


def run_chain(p_ref, kb_ref, prev_ref, hfv, carried, first, count):
    def body(j, now):
        for u in range(UNROLL):
            token = first + j * UNROLL + u
            now = chain_step(p_ref, kb_ref, prev_ref, hfv, now, rows_of(token), rows_of(token + 1))
        return now

    return lax.fori_loop(0, count // UNROLL, body, carried)


def row_blocks(p_ref, kb_ref, hfv_ref, init_ref, seg_ref, lead_ref, end_ref, lead_end_ref):
    tiles = seg_ref.shape[0]
    blocks = p_ref.shape[1] // SPACED
    hfv = tiles_of(hfv_ref, tiles)

    def seg_step(cells, step, store):
        row = pl.ds(step, blocks, stride=SPACED)
        keep = kb_ref[row, :]
        out = []
        for i, cell in enumerate(cells):
            prev = keep * cell
            tau = jnp.tanh(p_ref[tiles + i, row, :] + (hfv[i] * keep) * cell)
            half = 0.5 * p_ref[i, row, :]
            if store:
                seg_ref[i, row, :] = prev
            out.append((0.5 * prev + half) + (0.5 * prev - half) * tau)
        return out

    def run(cells, lead, first, token, count, store):
        def body(j, carried):
            cells, lead = carried
            for u in range(UNROLL):
                at = j * UNROLL + u
                cells = seg_step(cells, first + at, store)
                lead = chain_step(p_ref, kb_ref, lead_ref, hfv, lead, rows_of(token + at), rows_of(token + at + 1))
            return cells, lead

        return lax.fori_loop(0, count // UNROLL, body, (cells, lead))

    def moved(cells):
        return [jnp.concatenate([jnp.zeros((1, LANES), f32), cell[:-1]], axis=0) for cell in cells]

    cells = [jnp.zeros((blocks, LANES), f32) for _ in range(tiles)]
    lead = begin(p_ref, hfv, [kb_ref[0:1, :] * v for v in tiles_of(init_ref, tiles)], pl.ds(0, 1))
    cells, lead = run(cells, lead, BLOCK - EARLY, 0, EARLY, False)
    cells, lead = run(moved(cells), lead, 0, EARLY, BLOCK, False)
    cells, lead = run(moved(cells), lead, 0, EARLY + BLOCK, BLOCK, True)
    for i in range(tiles):
        end_ref[:, LANES * i : LANES * (i + 1)] = cells[i][-1:]
        lead_end_ref[:, LANES * i : LANES * (i + 1)] = lead[i][1]


def lead_kernel(p_ref, keep_ref, hfv_ref, start_ref, early_ref, lead_ref):
    rows, tiles = lead_ref.shape[:2]
    hfv = tiles_of(hfv_ref, tiles)
    lead_ref[:, :, : spaced(COVERED), :] = early_ref[...]
    for r in range(rows):
        carried = begin(p_ref.at[r], hfv, tiles_of(start_ref.at[r], tiles), rows_of(COVERED))
        run_chain(p_ref.at[r], keep_ref.at[r], lead_ref.at[r], hfv, carried, COVERED, LEAD - COVERED)


def lead_forward(p, keep, hfv, start, early):
    rows, tiles = early.shape[:2]
    out_shape = [((rows, tiles, spaced(LEAD), LANES), f32)]
    return call(lead_kernel, out_shape, (p, keep, hfv, start, early), name="lead_forward")[0]


def token_terms(prev, c, yf, yr, x, g, keep, hfv, hrv):
    tau_f = jnp.tanh(yf + hfv * prev)
    tau_r = jnp.tanh(yr + hrv * prev)
    f, omf, gate, omg = 0.5 + 0.5 * tau_f, 0.5 - 0.5 * tau_f, 0.5 + 0.5 * tau_r, 0.5 - 0.5 * tau_r
    cell = f * prev + omf * c
    gg = g * gate
    dr = gg * omg * (cell - x)
    e = (prev - c) * f * omf
    slope = f + e * (2.0 * hfv)
    return dict(
        cell=cell, hidden=gate * cell + omg * x, high=g * omg, gg=gg, dr=dr, e=e, omf=omf,
        a=keep * slope, b=keep * (slope * gg + dr * (2.0 * hrv)),
    )


def block_terms(p_ref, keep_ref, prev_ref, x_ref, g_ref, hfv, hrv, r, k, i):
    tiles = len(hfv)
    at = pl.ds(pl.multiple_of(k * SPACED, 8), BLOCK)
    devices = BLOCK // g_ref.shape[2]
    lanes = slice(LANES * i, LANES * (i + 1))
    g = jnp.concatenate([g_ref[k * devices + n, r, :, lanes].astype(f32) for n in range(devices)], axis=0)
    x = x_ref[r, i, pl.ds(pl.multiple_of(k * BLOCK, BLOCK), BLOCK), :].astype(f32)
    c, yf, yr = (p_ref[r, m * tiles + i, at, :] for m in range(3))
    return token_terms(prev_ref[i, at, :], c, yf, yr, x, g, keep_ref[r, at, :], hfv[i], hrv[i])


def run_back(a_ref, b_ref, d_ref, carried, count):
    def body(j, carried):
        base = pl.multiple_of(count - UNROLL * (j + 1), UNROLL)
        for u in reversed(range(UNROLL)):
            row = pl.ds(base + u, 1)
            now = []
            for i, d in enumerate(carried):
                if d_ref is not None:
                    d_ref[i, row, :] = d
                now.append(a_ref[i, row, :] * d + b_ref[i, row, :])
            carried = now
        return carried

    return lax.fori_loop(0, count // UNROLL, body, carried)


def entry_kernel(
    p_ref, keep_ref, seg_ref, x_ref, g_ref, hfv_ref, hrv_ref, start_ref, first_ref, back_ref, prev_ref, a_ref, b_ref
):
    rows, slots = p_ref.shape[:2]
    tiles = slots // 3
    hfv, hrv = tiles_of(hfv_ref, tiles), tiles_of(hrv_ref, tiles)
    blocks = -(-REACH // BLOCK)
    for r in range(rows):
        prev_ref[...] = seg_ref[r, :, : blocks * SPACED, :]
        start = [keep_ref[r, 0:1, :] * v for v in tiles_of(start_ref.at[r], tiles)]
        run_chain(p_ref.at[r], keep_ref.at[r], prev_ref, hfv, begin(p_ref.at[r], hfv, start, pl.ds(0, 1)), 0, REACH)
        first_ref[r] = prev_ref[:, : spaced(REACH), :]
        for k in range(blocks):
            for i in range(tiles):
                t = block_terms(p_ref, keep_ref, prev_ref, x_ref, g_ref, hfv, hrv, r, k, i)
                a_ref[i, BLOCK * k : BLOCK * (k + 1), :] = t["a"]
                b_ref[i, BLOCK * k : BLOCK * (k + 1), :] = t["b"]
        carried = run_back(a_ref, b_ref, None, [jnp.zeros((1, LANES), f32)] * tiles, blocks * BLOCK)
        for i in range(tiles):
            back_ref[r, :, LANES * i : LANES * (i + 1)] = carried[i]


def entry(p, keep, seg, x_own, g_own, hfv, hrv, start, waits):
    rows, slots, _, _ = p.shape
    tiles = slots // 3
    blocks = -(-REACH // BLOCK)
    length, count = blocks * SPACED, blocks * BLOCK
    return call(
        entry_kernel,
        [((rows, tiles, spaced(REACH), LANES), f32), ((rows, 1, tiles * LANES), f32)],
        (p, keep, seg, x_own, g_own, hfv, hrv, start),
        waits=waits,
        scratch=[((tiles, length, LANES), f32)] + [((tiles, count, LANES), f32)] * 2,
        name="entry",
    )


def backward_kernel(
    where_ref, p_ref, keep_ref, seg_ref, lead_ref, first_ref, x_ref, g_ref, hfv_ref, hrv_ref, carry_ref, vectors_ref,
    gp_ref, hidden_ref, high_ref, sums_ref, final_ref, means_ref,
    prev_ref, a_ref, b_ref, gg_ref, e_ref, omf_ref, dr_ref, d_ref,
):
    rows, slots = p_ref.shape[:2]
    tiles = slots // 3
    blocks = p_ref.shape[2] // SPACED
    hfv, hrv = tiles_of(hfv_ref, tiles), tiles_of(hrv_ref, tiles)
    devices, block = BLOCK // g_ref.shape[2], g_ref.shape[2]
    sums_ref[...] = jnp.zeros_like(sums_ref)
    for r in range(rows):
        prev_ref[...] = seg_ref[r]

        @pl.when(where_ref[0] == 0)
        def _():
            prev_ref[:, : spaced(LEAD), :] = lead_ref[r]

        @pl.when(where_ref[0] != 0)
        def _():
            prev_ref[:, : spaced(REACH), :] = first_ref[r]

        @pl.loop(0, blocks)
        def _(k):
            out = pl.ds(pl.multiple_of(k * BLOCK, BLOCK), BLOCK)
            for i in range(tiles):
                t = block_terms(p_ref, keep_ref, prev_ref, x_ref, g_ref, hfv, hrv, r, k, i)
                lanes = slice(LANES * i, LANES * (i + 1))
                for n in range(devices):
                    hidden_ref[k * devices + n, r, :, lanes] = t["hidden"][n * block : (n + 1) * block].astype(bf16)
                high_ref[r, i, out, :] = t["high"].astype(bf16)
                for ref, name in zip((a_ref, b_ref, gg_ref, e_ref, omf_ref, dr_ref), ("a", "b", "gg", "e", "omf", "dr")):
                    ref[i, out, :] = t[name]
                final_ref[r, :, lanes] = t["cell"][-1:]

        run_back(a_ref, b_ref, d_ref, tiles_of(carry_ref.at[r], tiles), blocks * BLOCK)

        @pl.loop(0, blocks)
        def _(k):
            at = pl.ds(pl.multiple_of(k * SPACED, 8), BLOCK)
            out = pl.ds(pl.multiple_of(k * BLOCK, BLOCK), BLOCK)
            first, second = jnp.zeros((BLOCK, LANES), f32), jnp.zeros((BLOCK, LANES), f32)
            for i in range(tiles):
                prev = prev_ref[i, at, :]
                u = d_ref[i, out, :] + gg_ref[i, out, :]
                df, dr = u * e_ref[i, out, :], dr_ref[i, out, :]
                dc = u * omf_ref[i, out, :]
                for m, value in enumerate((dc, df, dr)):
                    slot = m * tiles + i
                    lane = lax.rem(slot + slots - where_ref[4], slots) * LANES
                    gp_ref[r, out, pl.ds(pl.multiple_of(lane, LANES), LANES)] = value.astype(bf16)
                    first += value * vectors_ref[slot, 0:1, :]
                    second += value * ((1.0 if m == 0 else 2.0) * p_ref[r, slot, at, :] - vectors_ref[slot, 1:2, :])
                lanes = slice(LANES * i, LANES * (i + 1))
                for m, value in enumerate((df * prev, dr * prev, df, dr)):
                    sums_ref[m : m + 1, lanes] += jnp.sum(value, axis=0, keepdims=True)
                for m, value in enumerate((dc, df, dr)):
                    lane = lax.rem(m * tiles + i + slots - where_ref[4], slots) * LANES
                    at_lane = pl.ds(pl.multiple_of(lane, LANES), LANES)
                    sums_ref[7:8, at_lane] += jnp.sum(value, axis=0, keepdims=True)
            means_ref[r, 0, out, :] = first
            means_ref[r, 1, out, :] = second


def backward(where, p, keep, seg, lead, first, x_own, g_own, hfv, hrv, carry, vectors):
    rows, slots, length, _ = p.shape
    tiles = slots // 3
    tokens = length // SPACED * BLOCK
    width = tiles * LANES
    return call(
        backward_kernel,
        [
            ((rows, tokens, 3 * width), bf16),
            (g_own.shape, bf16),
            ((rows, tiles, tokens, LANES), bf16),
            ((8, 3 * width), f32),
            ((rows, 1, width), f32),
            ((rows, 2, tokens, LANES), f32),
        ],
        (p, keep, seg, lead, first, x_own, g_own, hfv, hrv, carry, vectors),
        (where,),
        scratch=[((tiles, length, LANES), f32)] + [((tiles, tokens, LANES), f32)] * 7,
        name="backward",
    )


def weight_back_kernel(normed_ref, gp_ref, sums_ref, *refs, part, group, cuts):
    count = sum(len(rows) for rows in cuts)
    w_refs, (by_feature_ref, *out_refs) = refs[: len(refs) - count - 1], refs[len(refs) - count - 1 :]
    total, _, features = normed_ref.shape
    row_block = features // 2 // group
    columns = out_refs[0].shape[2]
    span = 2 * LANES
    devices = span // row_block
    lane_tiles = gp_ref.shape[2] // LANES
    for k in range(group // devices):
        lane = slice(part * (features // 2) + k * span, part * (features // 2) + (k + 1) * span)
        p = sum(
            lax.dot_general(normed_ref[r, :, lane], gp_ref[r], (((0,), (0,)), ((), ())), preferred_element_type=f32)
            for r in range(total)
        )
        first = w_refs[0].shape[0]
        w = [w_refs[0][lane.start : min(lane.stop, first), :]] if lane.start < first else []
        if lane.stop > first:
            w.append(w_refs[1][max(lane.start - first, 0) : lane.stop - first, :])
        w = jnp.concatenate(w).astype(f32)
        for m, value in enumerate((p * w, w * sums_ref[7:8, :])):
            value = functools.reduce(jnp.add, [value[:, LANES * j : LANES * (j + 1)] for j in range(lane_tiles)])
            by_feature_ref[m : m + 1, k * span : (k + 1) * span] = jnp.sum(jnp.transpose(value), axis=0, keepdims=True)
        p = p.astype(bf16)
        outs = iter(out_refs)
        for split, rows in enumerate(cuts):
            start = 0
            for step in rows:
                out_ref = next(outs)
                for n in range(devices):
                    row = n * row_block + start
                    out_ref[k * devices + n, :step] = p[row : row + step, split * columns : (split + 1) * columns]
                    if out_ref.shape[1] > step:
                        out_ref[k * devices + n, step:] = jnp.zeros((out_ref.shape[1] - step, columns), bf16)
                start += step


def weight_back(normed, gp, sums, weights, part, group, cuts, waits, spare=0):
    features = normed.shape[2]
    columns = gp.shape[2] // len(cuts)
    kernel = functools.partial(weight_back_kernel, part=part, group=group, cuts=cuts)
    out_shape = [((2, features // 2), f32)] + [((group, step, columns), bf16) for rows in cuts for step in rows]
    (count, step, width), dtype = out_shape[-1]
    out_shape[-1] = ((count, step + spare, width), dtype)
    return call(kernel, out_shape, (normed, gp, sums, *weights), waits=waits, name="weight_back")


def norm_back_kernel(where_ref, stats_ref, means_ref, gp_ref, gain_ref, *refs, orders, with_hidden):
    count = len(orders[0])
    x_refs, refs = refs[: 2 * count], refs[2 * count :]
    *w_refs, high_ref, hidden_ref = refs[:-10]
    all_out_refs, (some_ref, gn_ref) = refs[-10:-2], refs[-2:]
    half_count, total, block, _ = all_out_refs[0].shape
    features = gain_ref.shape[1]
    half_width = features // 2
    together = gn_ref.shape[0] // block
    for odd in (1, 0):
        out_refs = all_out_refs[4 * (1 - odd) : 4 * (2 - odd)]
        for r in range(total):
            for d in range(0, count, together):
                tokens = []
                for n in range(together):
                    place = where_ref[3] ^ (orders[0][d + n] | odd)
                    tokens.append(pl.ds(pl.multiple_of(place * block, 16), block))
                    some_ref[n * block : (n + 1) * block, :] = gp_ref[r, tokens[n], :]
                lane = 0
                for w_ref in w_refs:
                    rows = w_ref.shape[0]
                    gn_ref[:, lane : lane + rows] = lax.dot_general(
                        some_ref[...], w_ref[...], (((1,), (1,)), ((), ())), preferred_element_type=f32
                    )
                    lane += rows
                for n in range(together):
                    x_ref = x_refs[orders[0][d + n] | odd]
                    mean, inv = stats_ref[r, 0, tokens[n], :], stats_ref[r, 1, tokens[n], :]
                    first, second = (
                        jnp.sum(means_ref[r, m, tokens[n], :], axis=-1, keepdims=True) * (1.0 / features)
                        for m in range(2)
                    )
                    slope = inv * inv * second
                    rest = inv * first - slope * mean
                    for part in range(2):
                        at_d = orders[part].index(orders[0][d + n])
                        out_ref = out_refs[2 * part + at_d // half_count]
                        start = pl.multiple_of((where_ref[0] ^ part) * half_width, LANES)
                        if with_hidden:
                            high = high_ref[r, where_ref[0] ^ part, tokens[n], :].astype(f32)
                        for j in range(half_width // LANES):
                            at = slice(part * half_width + LANES * j, part * half_width + LANES * (j + 1))
                            value = inv * (gn_ref[n * block : (n + 1) * block, at] * gain_ref[:, at])
                            x = x_ref[r, :block, pl.ds(start + LANES * j, LANES)].astype(f32)
                            value -= slope * x + rest
                            if with_hidden:
                                value += jnp.where(where_ref[3] == j, high, 0.0)
                            out_ref[at_d % half_count, r, :, LANES * j : LANES * (j + 1)] = value.astype(bf16)
                        if with_hidden:
                            hidden = hidden_ref[where_ref[3] ^ (orders[0][d + n] | odd), r]
                            out_ref[at_d % half_count, r, :, half_width:] = hidden[:, LANES * part : LANES * (part + 1)]


def norm_back(where, blocks, orders, stats, means, gp, weights, gain, high, hidden, with_hidden, waits):
    rows, block, features = blocks[0].shape
    block -= STATS
    together = 2 * LANES // block
    out = call(
        functools.partial(norm_back_kernel, orders=orders, with_hidden=with_hidden),
        [((len(blocks) // 4, rows, block, features // 2 + with_hidden * LANES), bf16)] * 8,
        (stats, means, gp, gain, *blocks, *weights, high, hidden), (where,), waits,
        scratch=[((together * block, gp.shape[2]), bf16), ((together * block, features), f32)],
        name="norm_back",
    )
    return out[:4], out[4:]


def totals_kernel(where_ref, sums_ref, own_ref, other_ref, gain_ref, shift_ref, out_ref, *, chunk):
    half_width = own_ref.shape[1]
    out_ref[...] = jnp.zeros_like(out_ref)
    for i in range(2):
        lane = pl.ds(pl.multiple_of(i * chunk + where_ref[3] * LANES, LANES), LANES)
        out_ref[0:4, lane] = sums_ref[0:4, LANES * i : LANES * (i + 1)]
    for part, ref in enumerate((own_ref, other_ref)):
        lane = pl.ds(pl.multiple_of((where_ref[0] ^ part) * half_width, LANES), half_width)
        at = slice(part * half_width, (part + 1) * half_width)
        out_ref[4:5, lane] = (ref[0:1, :] - shift_ref[:, at] * ref[1:2, :]) / gain_ref[:, at]
        out_ref[5:6, lane] = ref[1:2, :]


def bf16_parts(row):
    rows = []
    for _ in range(3):
        upper = lax.reduce_precision(row, 8, 7)
        rows.append(upper.astype(bf16))
        row = row - upper
    return rows


def local(inputs, weight, gain, shift, forget_vec, reset_vec, forget_bias, reset_bias, initial, resets, grad_out):
    rows, block_len, features = inputs.shape
    row_block, columns_here = weight.shape
    sections = lax.axis_size("fsdp")
    ranks = lax.axis_size("dp")
    group = sections // 2
    tokens = group * block_len
    index = lax.axis_index("fsdp")
    half, place = index // group, index % group
    rank = lax.axis_index("dp")
    first_half = half == 0
    groups = [list(range(group)), list(range(group, sections))]
    chunk = math.gcd(features, columns_here)
    chunks, piece = features // chunk, chunk // group
    width = chunks * piece
    tiles = width // LANES
    slots = 3 * tiles
    parts = columns_here // chunk
    columns = parts * piece
    aligned = piece == LANES and chunks == 2
    paired = ranks == 2 and aligned
    turn = rank * (columns // LANES) if paired else jnp.zeros_like(rank)
    where = jnp.stack([half, rank, index % 2, place, turn]).astype(jnp.int32)
    bits = [1 << b for b in range(1, group.bit_length() - 1)]
    ways = (bits[::-1], bits)
    orders = []
    for way in ways:
        order = [0]
        for bit in way:
            order += [d | bit for d in order]
        orders.append(order)

    def across(value):
        return lax.ppermute(value, "fsdp", [(j, (j + group) % sections) for j in range(sections)])

    def flipped(value, bit):
        return lax.ppermute(value, "fsdp", [(j, j ^ bit) for j in range(sections)])

    def swapped(value):
        return lax.ppermute(value, "dp", [(0, 1), (1, 0)])

    def shared(value):
        return lax.all_to_all(value, "fsdp", 0, 0, tiled=True, axis_index_groups=groups)

    def own(vector):
        return lax.dynamic_index_in_dim(vector.reshape(-1, chunks, group, piece), place, 2, False).reshape(-1, width)

    def halves_turned(vector):
        low, high = vector[..., : features // 2], vector[..., features // 2 :]
        return jnp.concatenate([jnp.where(first_half, low, high), jnp.where(first_half, high, low)], axis=-1)

    def dealt(value, waits=()):
        if aligned:
            return deal(value, group, waits)
        n, wide = value.shape
        return value.reshape(n, wide // chunk, group, piece).transpose(2, 0, 1, 3).reshape(group, n, wide // group)

    def collected(pieces, dtype, waits=()):
        if aligned:
            return collect(pieces, dtype, waits)
        wide = pieces[0].shape[2]
        back = lambda v: v.reshape(group, -1, wide // piece, piece).transpose(1, 2, 0, 3).reshape(-1, wide * group)
        return jnp.concatenate([back(v) for v in pieces]).astype(dtype)

    mine = shared(dealt(weight))
    theirs = across(mine)
    beside = swapped(mine) if paired else mine
    blocks = {0: stats(inputs, (1 - resets).astype(f32)[:, None, :], (mine,))}
    for bit in bits[::-1]:
        blocks |= {d | bit: flipped(value, bit) for d, value in blocks.items()}
    blocks = {d: fence(value, (theirs, beside)) for d, value in blocks.items()}
    blocks |= {d | 1: flipped(value, 1) for d, value in blocks.items()}
    blocks = [blocks[d] for d in range(group)]
    early_rows = features // 2
    if paired:
        early, late = [mine, beside], [theirs, swapped(theirs)]
    else:
        early, late = (
            [lax.all_gather(v.reshape(-1, columns), "dp", axis=1, tiled=True)] for v in (mine, theirs)
        )
    hfv, hrv = 0.5 * own(forget_vec), 0.5 * own(reset_vec)
    bias = jnp.concatenate([jnp.zeros((1, width), f32), own(forget_bias), own(reset_bias)]).reshape(-1, 1, LANES)
    gain_row, shift_row = halves_turned(gain)[None], halves_turned(shift)[None]
    vector_rows = [*bf16_parts(gain_row), *bf16_parts(shift_row)]
    vector_rows = jnp.pad(jnp.concatenate(vector_rows), ((0, 10), (0, 0)))
    g_own = shared(dealt(grad_out.reshape(-1, features)).reshape(group, rows, block_len, width))
    normed, token_stats, keep, *x_own = norm(where, blocks, gain_row, shift_row, aligned, (g_own,))
    if aligned:
        x_own = x_own[0]
    else:
        in_order = jnp.stack(blocks)[place ^ jnp.arange(group)][:, :, :block_len].swapaxes(0, 1)
        x_own = own(in_order.reshape(rows * tokens, features)).reshape(rows, tokens, tiles, LANES).swapaxes(1, 2)
    some, some_vectors, early_weight = project(where, normed, vector_rows, early, early_rows, slots)
    p, seg, lead, end, lead_end, vectors, late_weight = blocks_forward(
        where, normed, vector_rows, some, some_vectors, bias, keep, hfv, own(initial)[:, None, :], late,
        features - early_rows,
    )
    weights = (early_weight, late_weight)
    start = across(end)
    lead = lead_forward(p, keep, hfv, lead_end, lead)
    first, back = entry(p, keep, seg, x_own, g_own, hfv, hrv, start, ())
    carry = jnp.where(first_half, across(back), 0.0)
    gp, hidden_own, high_own, sums, final, means = backward(
        where, p, keep, seg, lead, first, x_own, g_own, hfv, hrv, carry, vectors
    )

    mask = (jnp.arange(group) == place)[:, None]

    splits = 2 if paired else 1
    by_feature_other, *away = weight_back(normed, gp, sums, weights, 1, group, [(row_block,)] * splits, (), SPARE * paired)
    away_got = swapped(away[1]) if paired else None

    sent, kept = norm_back(
        where, blocks, orders, token_stats, means, gp, weights, gain_row, high_own, hidden_own, aligned,
        (by_feature_other,),
    )
    if not aligned:
        spread = high_own.swapaxes(1, 2).reshape(rows, group, block_len, chunks, 1, piece).swapaxes(0, 1)
        spread = jnp.where(mask, spread.astype(f32), 0.0).reshape(group, rows, block_len, features)
        spread = halves_turned(spread)[place ^ jnp.arange(group)]
        halves = (spread[..., : features // 2], spread[..., features // 2 :])
        n = group // 4

        def with_high(arrays, odd):
            add = [half[d | odd] for half, order in zip(halves, orders) for d in order]
            return [(v.astype(f32) + jnp.stack(add[i * n : (i + 1) * n])).astype(bf16) for i, v in enumerate(arrays)]

        sent, kept = with_high(sent, 1), with_high(kept, 0)
    got = [flipped(value, 1) for value in sent]
    if paired:
        away = added(away[0], away_got, kept[:1])
    else:
        away = lax.psum_scatter(away[0], "dp", scatter_dimension=2, tiled=True)
    z_got = across(away)
    kept, sent = halve(kept, got, features // 2)
    bit_pairs = list(zip(*(w[::-1] for w in ways)))
    got = [flipped(value, bit) for value, bit in zip(sent, bit_pairs.pop(0))]
    cuts = [(row_block,), (row_block // 2,) * 2][:splits]
    by_feature_own, *here = weight_back(normed, gp, sums, weights, 0, group, cuts, (away,))
    if paired:
        here_got = [swapped(value) for value in here[1:]]
    else:
        here = lax.psum_scatter(here[0], "dp", scatter_dimension=2, tiled=True)
    if aligned:
        totals = call(
            functools.partial(totals_kernel, chunk=chunk), [((8, features), f32)],
            (sums, by_feature_own, by_feature_other, gain_row, shift_row), (where,), name="totals",
        )[0]
    else:
        spread = jnp.where(mask, sums[:4, :width].reshape(4, chunks, 1, piece), 0.0).reshape(4, features)
        product, shift_sum = jnp.concatenate([by_feature_own, by_feature_other], axis=1)
        gain_sum = (product - shift_row[0] * shift_sum) / gain_row[0]
        totals = jnp.concatenate([spread, halves_turned(jnp.stack([gain_sum, shift_sum]))], axis=0)
    for way in bit_pairs:
        kept, sent = halve(kept, got, features // 2)
        got = [flipped(value, bit) for value, bit in zip(sent, way)]
    sources = []
    for way in ways:
        sources.append([0])
        for bit in (1, *way[::-1]):
            sources[-1] += [d | bit for d in sources[-1]]
    grad_inputs, *hidden = finish(where, kept, got, features, sources)
    if aligned:
        hidden = hidden[0]
    else:
        hidden = collected([shared(hidden_own).reshape(group, -1, width)], bf16).reshape(rows, block_len, features)
    for bit in [1 << b for b in range(group.bit_length() - 1)]:
        totals = added(totals, flipped(totals, bit))
    waits = (*got, totals)
    value = merge(here[0], here_got, z_got, waits) if paired else added(here, z_got, waits)
    grad_weight = collected([shared(value)], f32)
    totals = added(totals, swapped(totals)) if ranks == 2 else lax.psum(totals, "dp")
    totals = added(totals, across(totals))

    own_width = features // sections
    if piece == own_width and chunks == 2:
        final = final[:, 0]
        low_part = lax.ppermute(final[:, :piece], "fsdp", [(j + group, j) for j in range(group)])
        final_state = jnp.where(first_half, low_part, final[:, piece:])
    else:
        spread = jnp.where(mask, final.reshape(rows, chunks, 1, piece), 0.0).reshape(rows, features)
        spread = lax.psum(jnp.where(first_half, 0.0, spread), "fsdp")
        final_state = lax.dynamic_slice_in_dim(spread, index * own_width, own_width, 1)

    return (hidden, grad_inputs, final_state, grad_weight, *[totals[i] for i in range(6)])


def solution(mesh):
    in_specs = (
        P("dp", "fsdp", None), P("fsdp", "dp"), P(), P(), P(), P(), P(), P(),
        P("dp", None), P("dp", "fsdp"), P("dp", "fsdp", None),
    )
    out_specs = (
        P("dp", "fsdp", None), P("dp", "fsdp", None), P("dp", "fsdp"), P("fsdp", "dp"), P(), P(), P(), P(), P(), P(),
    )
    return jax.shard_map(local, mesh=mesh, in_specs=in_specs, out_specs=out_specs, check_vma=False)
```

```python
import functools
import math

import jax
import jax.numpy as jnp
from jax import lax
from jax.experimental import pallas as pl
from jax.experimental.pallas import tpu as pltpu
from jax.sharding import PartitionSpec as P

SENT = 128
LEAD = 768
REACH = 192
EPSILON = 1e-05
LANES = 128
BLOCK = 128
SPACED = 136
EARLY = REACH - BLOCK
COVERED = EARLY + 2 * BLOCK
STATS = 16
SPARE = 16
UNROLL = 8
TOGETHER = 8
f32 = jnp.float32
bf16 = jnp.bfloat16


def spaced(token):
    return token + (SPACED - BLOCK) * (token // BLOCK)


def tiles_of(ref, count):
    return [ref[:, LANES * i : LANES * (i + 1)] for i in range(count)]


def call(kernel, out_shape, operands, scalars=(), waits=(), scratch=(), mebibytes=14, name=None):
    in_vmem, in_smem = pl.BlockSpec(memory_space=pltpu.VMEM), pl.BlockSpec(memory_space=pltpu.SMEM)
    before = len(scalars) + len(operands)

    def body(*refs):
        kernel(*refs[:before], *refs[before + len(waits) :])

    return pl.pallas_call(
        body,
        in_specs=[in_smem] * len(scalars) + [in_vmem] * len(operands) + [pl.BlockSpec(memory_space=pl.ANY)] * len(waits),
        out_specs=[in_vmem] * len(out_shape),
        out_shape=[jax.ShapeDtypeStruct(*shape) for shape in out_shape],
        scratch_shapes=[pltpu.VMEM(*shape) for shape in scratch],
        compiler_params=pltpu.CompilerParams(vmem_limit_bytes=mebibytes << 20),
        name=name,
    )(*scalars, *operands, *waits)


def fence(value, waits):
    return pl.pallas_call(
        lambda *refs: None,
        in_specs=[pl.BlockSpec(memory_space=pl.ANY)] * (1 + len(waits)),
        out_specs=pl.BlockSpec(memory_space=pl.ANY),
        out_shape=jax.ShapeDtypeStruct(value.shape, value.dtype),
        input_output_aliases={0: 0},
        name="fence",
    )(value, *waits)


def deal_kernel(in_ref, out_ref, *, chunks):
    group = out_ref.shape[0]
    for q in range(group):
        for c in range(chunks):
            lane = (c * group + q) * LANES
            out_ref[q, :, LANES * c : LANES * (c + 1)] = in_ref[:, lane : lane + LANES]


def deal(value, group, waits=()):
    n, features = value.shape
    kernel = functools.partial(deal_kernel, chunks=features // group // LANES)
    return call(kernel, [((group, n, features // group), value.dtype)], (value,), waits=waits, name="deal")[0]


def collect_kernel(*refs):
    *in_refs, out_ref = refs
    row = 0
    for ref in in_refs:
        group, n, width = ref.shape
        for q in range(group):
            for c in range(width // LANES):
                lane = (c * group + q) * LANES
                value = ref[q, :, LANES * c : LANES * (c + 1)]
                out_ref[row : row + n, lane : lane + LANES] = value.astype(out_ref.dtype)
        row += n


def collect(pieces, dtype, waits=()):
    group, _, width = pieces[0].shape
    shape = (sum(value.shape[1] for value in pieces), group * width)
    return call(collect_kernel, [(shape, dtype)], pieces, waits=waits, name="collect")[0]


def add_kernel(a_ref, b_ref, out_ref):
    b = b_ref[...] if b_ref.shape == a_ref.shape else b_ref[:, : a_ref.shape[1]]
    out_ref[...] = (a_ref[...].astype(f32) + b.astype(f32)).astype(out_ref.dtype)


def added(a, b, waits=()):
    return call(add_kernel, [(a.shape, a.dtype)], (a, b), waits=waits, name="added")[0]


def blocks_of(refs):
    return [ref.at[i] for ref in refs for i in range(ref.shape[0])]


def halve_kernel(*refs, width):
    *in_refs, first_stays, first_goes, second_stays, second_goes = refs
    n = len(in_refs) // 4
    parts = [blocks_of(in_refs[n * i : n * (i + 1)]) for i in range(4)]
    for part, (stays, goes) in enumerate(((first_stays, first_goes), (second_stays, second_goes))):
        out = blocks_of([stays, goes])
        for out_ref, a_ref, b_ref in zip(out, parts[part], parts[2 + part]):
            out_ref[:, :, :width] = (a_ref[:, :, :width].astype(f32) + b_ref[:, :, :width].astype(f32)).astype(bf16)
            there = a_ref.shape[2]
            if there > width:
                out_ref[:, :, width:there] = a_ref[:, :, width:]
                out_ref[:, :, there:] = b_ref[:, :, width:]


def halve(kept, got, width, waits=()):
    n = sum(value.shape[0] for value in kept) // 4
    *shape, there = kept[0].shape[1:]
    out = call(
        functools.partial(halve_kernel, width=width), [((n, *shape, 2 * there - width), bf16)] * 4, (*kept, *got),
        waits=waits, name="halve",
    )
    return out[0::2], out[1::2]


def merge_kernel(own_ref, away_ref, *refs):
    *got_refs, out_ref = refs
    start = 0
    for ref in got_refs:
        rows = slice(start, start + ref.shape[1])
        value = own_ref[:, rows, :].astype(f32) + ref[...].astype(f32) + away_ref[:, rows, :].astype(f32)
        out_ref[:, rows, :] = value.astype(bf16)
        start = rows.stop


def merge(own, got, away, waits=()):
    return call(merge_kernel, [(own.shape, bf16)], (own, away, *got), waits=waits, name="merge")[0]


def finish_kernel(where_ref, *refs, sources):
    in_refs, (out_ref, *hidden_ref) = refs[:4], refs[4:]
    half_width = out_ref.shape[2] // 2
    for part in range(2):
        kept_ref, got_ref = in_refs[part], in_refs[2 + part]
        value = kept_ref[0, :, :, :half_width].astype(f32) + got_ref[0, :, :, :half_width].astype(f32)
        lane = pl.multiple_of((where_ref[0] ^ part) * half_width, LANES)
        out_ref[:, :, pl.ds(lane, half_width)] = value.astype(bf16)
        if hidden_ref:
            tiles = [ref[0, :, :, at : at + LANES] for ref in (kept_ref, got_ref) for at in range(half_width, ref.shape[3], LANES)]
            for value, source in zip(tiles, sources[part]):
                lane = pl.multiple_of(part * half_width + (where_ref[3] ^ source) * LANES, LANES)
                hidden_ref[0][:, :, pl.ds(lane, LANES)] = value


def finish(where, kept, got, features, sources, waits=()):
    _, rows, block, there = kept[0].shape
    out_shape = [((rows, block, features), bf16)] * (1 + (there > features // 2))
    kernel = functools.partial(finish_kernel, sources=sources)
    return call(kernel, out_shape, (*kept, *got), (where,), waits, name="finish")


def stats_kernel(x_ref, keep_ref, out_ref):
    total, block, features = x_ref.shape

    def row(column):
        return jnp.transpose(jnp.broadcast_to(column, (block, LANES)))[0:1, :]

    for r in range(total):
        out_ref[r, :block, :] = x_ref[r]
        x = x_ref[r].astype(f32)
        mean = jnp.sum(x, axis=-1, keepdims=True) * (1.0 / features)
        centred = x - mean
        inv = lax.rsqrt(jnp.sum(centred * centred, axis=-1, keepdims=True) * (1.0 / features) + EPSILON)
        rows = [keep_ref[r]]
        for value in (row(mean), row(inv)):
            for _ in range(3):
                upper = value.astype(bf16).astype(f32)
                rows.append(upper)
                value = value - upper
        rows = jnp.concatenate(rows + [jnp.zeros_like(rows[0])] * (STATS - len(rows)), axis=0)
        if block < LANES:
            rows = jnp.concatenate([rows, jnp.zeros((STATS, LANES - block), f32)], axis=1)
        out_ref[r, block:, :LANES] = rows.astype(bf16)
        out_ref[r, block:, LANES:] = jnp.zeros((STATS, features - LANES), bf16)


def stats(inputs, keep, waits):
    rows, block, features = inputs.shape
    return call(stats_kernel, [((rows, block + STATS, features), bf16)], (inputs, keep), waits=waits, name="stats")[0]


def norm_kernel(where_ref, gain_ref, shift_ref, *refs, count):
    block_refs, (normed_ref, stats_ref, keep_ref, *own_refs) = refs[:count], refs[count:]
    total, block, features = block_refs[0].shape
    block -= STATS
    half_width = features // 2
    per_block = BLOCK // block

    def device(r, x_ref, q):
        at = pl.ds(pl.multiple_of(q * block, block), block)
        spaced_at = pl.ds(pl.multiple_of(q // per_block * SPACED + q % per_block * block, 8), block)
        rows = x_ref[r, block:, :block].astype(f32)

        def column(*of):
            row = functools.reduce(jnp.add, [rows[k : k + 1, :] for k in of])
            return jnp.transpose(jnp.broadcast_to(row, (LANES, block)))

        keep_ref[r, spaced_at, :] = column(0)
        mean, inv = column(1, 2, 3), column(4, 5, 6)
        stats_ref[r, 0, at, :] = mean
        stats_ref[r, 1, at, :] = inv
        for part in range(2):
            lane = pl.multiple_of((where_ref[0] ^ part) * half_width, LANES)
            for j in range(half_width // LANES):
                x = x_ref[r, :block, pl.ds(lane + j * LANES, LANES)].astype(f32)
                out = slice(part * half_width + j * LANES, part * half_width + (j + 1) * LANES)
                normed_ref[r, at, out] = ((x - mean) * inv * gain_ref[:, out] + shift_ref[:, out]).astype(bf16)
        for ref in own_refs:
            for i in range(2):
                lane = pl.ds(pl.multiple_of(i * half_width + where_ref[3] * LANES, LANES), LANES)
                ref[r, i, at, :] = x_ref[r, :block, lane]

    for r in range(total):
        for d, ref in enumerate(block_refs):
            device(r, ref, where_ref[3] ^ d)


def norm(where, blocks, gain, shift, aligned, waits):
    rows, block, features = blocks[0].shape
    tokens = len(blocks) * (block - STATS)
    out_shape = [
        ((rows, tokens, features), bf16),
        ((rows, 2, tokens, LANES), f32),
        ((rows, tokens // BLOCK * SPACED, LANES), f32),
    ]
    if aligned:
        out_shape.append(((rows, 2, tokens, LANES), bf16))
    kernel = functools.partial(norm_kernel, count=len(blocks))
    return call(kernel, out_shape, (gain, shift, *blocks), (where,), waits, name="norm")


def weight_into(w_ref, parts):
    if len(parts) == 1:
        w_ref[...] = parts[0][...]
        return
    pieces = len(parts) // 2
    group, _, columns = parts[0].shape
    block = sum(part.shape[1] for part in parts[:pieces])
    for rank in range(2):
        start = 0
        for part in parts[rank * pieces : (rank + 1) * pieces]:
            rows = part.shape[1]
            for q in range(group):
                row = q * block + start
                w_ref[row : row + rows, rank * columns : (rank + 1) * columns] = part[q]
            start += rows


def slot_of(where_ref, s, slots):
    return lax.rem(where_ref[4] + s, slots)


def project_kernel(where_ref, normed_ref, rows_ref, *refs):
    *parts, sum_ref, vectors_ref, w_ref = refs
    weight_into(w_ref, parts)
    depth = w_ref.shape[0]
    total, slots = sum_ref.shape[:2]
    step = 2 * BLOCK
    vectors_ref[...] = jnp.dot(rows_ref[:, :depth], w_ref[...], preferred_element_type=f32)
    for r in range(total):

        @pl.loop(0, normed_ref.shape[1] // step)
        def _(j):
            at = pl.ds(pl.multiple_of(j * step, step), step)
            p = jnp.dot(normed_ref[r, at, :depth], w_ref[...], preferred_element_type=f32)
            for s in range(slots):
                sum_ref[r, s, at, :] = p[:, LANES * s : LANES * (s + 1)]


def project(where, normed, vector_rows, parts, depth, slots):
    rows, tokens, _ = normed.shape
    out_shape = [
        ((rows, slots, tokens, LANES), f32), ((vector_rows.shape[0], slots * LANES), f32), ((depth, slots * LANES), bf16),
    ]
    return call(project_kernel, out_shape, (normed, vector_rows, *parts), (where,), name="project")


def blocks_kernel(where_ref, normed_ref, rows_ref, sum_ref, some_ref, bias_ref, keep_ref, hfv_ref, init_ref, *refs):
    *parts, p_ref, seg_ref, lead_ref, end_ref, lead_end_ref, vectors_ref, w_ref = refs
    weight_into(w_ref, parts)
    depth = w_ref.shape[0]
    total, slots = p_ref.shape[:2]
    tiles = slots // 3
    step = 2 * BLOCK
    features = normed_ref.shape[2]
    by_column = some_ref[...] + jnp.dot(rows_ref[:, features - depth :], w_ref[...], preferred_element_type=f32)
    for s in range(slots):
        slot = slot_of(where_ref, s, slots)
        lanes = slice(LANES * s, LANES * (s + 1))
        vectors_ref[slot, 0:1, :] = jnp.sum(by_column[0:3, lanes], axis=0, keepdims=True)
        vectors_ref[slot, 1:2, :] = jnp.sum(by_column[3:6, lanes], axis=0, keepdims=True) + bias_ref[slot]
    for r in range(total):

        @pl.loop(0, normed_ref.shape[1] // step)
        def _(j):
            at = pl.ds(pl.multiple_of(j * step, step), step)
            p = jnp.dot(normed_ref[r, at, features - depth :], w_ref[...], preferred_element_type=f32)
            for s in range(slots):
                slot = slot_of(where_ref, s, slots)
                scale = jnp.where(slot < tiles, 1.0, 0.5)
                value = scale * (p[:, LANES * s : LANES * (s + 1)] + sum_ref[r, s, at, :] + bias_ref[slot])
                for k in range(2):
                    to = pl.ds(pl.multiple_of((2 * j + k) * SPACED, 8), BLOCK)
                    p_ref[r, slot, to, :] = value[BLOCK * k : BLOCK * (k + 1)]

        row_blocks(
            p_ref.at[r], keep_ref.at[r], hfv_ref, init_ref.at[r], seg_ref.at[r], lead_ref.at[r], end_ref.at[r],
            lead_end_ref.at[r],
        )


def blocks_forward(where, normed, vector_rows, some, some_vectors, bias, keep, hfv, init, parts, depth):
    rows, tokens, _ = normed.shape
    slots = bias.shape[0]
    tiles = slots // 3
    state = ((rows, 1, tiles * LANES), f32)
    length = tokens // BLOCK * SPACED
    out_shape = [
        ((rows, slots, length, LANES), f32), ((rows, tiles, length, LANES), f32),
        ((rows, tiles, spaced(COVERED), LANES), f32), state, state, ((slots, 2, LANES), f32), ((depth, slots * LANES), bf16),
    ]
    return call(
        blocks_kernel, out_shape, (normed, vector_rows, some, some_vectors, bias, keep, hfv, init, *parts), (where,),
        name="blocks_forward",
    )


def chain_step(p_ref, kb_ref, prev_ref, hfv, carried, row, next_row):
    tiles = len(hfv)
    keep = kb_ref[next_row, :]
    out = []
    for i, (y, prev) in enumerate(carried):
        tau = jnp.tanh(y)
        half = 0.5 * p_ref[i, row, :]
        mid, gap = 0.5 * prev + half, 0.5 * prev - half
        prev_ref[i, row, :] = prev
        reach = hfv[i] * keep
        out.append(
            ((p_ref[tiles + i, next_row, :] + reach * mid) + (reach * gap) * tau, (keep * mid) + (keep * gap) * tau)
        )
    return out


def begin(p_ref, hfv, previous, row):
    return [(p_ref[len(hfv) + i, row, :] + hfv[i] * prev, prev) for i, prev in enumerate(previous)]


def rows_of(token):
    return pl.ds(spaced(token), 1)


def run_chain(p_ref, kb_ref, prev_ref, hfv, carried, first, count):
    def body(j, now):
        for u in range(UNROLL):
            token = first + j * UNROLL + u
            now = chain_step(p_ref, kb_ref, prev_ref, hfv, now, rows_of(token), rows_of(token + 1))
        return now

    return lax.fori_loop(0, count // UNROLL, body, carried)


def row_blocks(p_ref, kb_ref, hfv_ref, init_ref, seg_ref, lead_ref, end_ref, lead_end_ref):
    tiles = seg_ref.shape[0]
    blocks = p_ref.shape[1] // SPACED
    hfv = tiles_of(hfv_ref, tiles)

    def seg_step(cells, step, store):
        row = pl.ds(step, blocks, stride=SPACED)
        keep = kb_ref[row, :]
        out = []
        for i, cell in enumerate(cells):
            prev = keep * cell
            tau = jnp.tanh(p_ref[tiles + i, row, :] + (hfv[i] * keep) * cell)
            half = 0.5 * p_ref[i, row, :]
            if store:
                seg_ref[i, row, :] = prev
            out.append((0.5 * prev + half) + (0.5 * prev - half) * tau)
        return out

    def run(cells, lead, first, token, count, store):
        def body(j, carried):
            cells, lead = carried
            for u in range(UNROLL):
                at = j * UNROLL + u
                cells = seg_step(cells, first + at, store)
                lead = chain_step(p_ref, kb_ref, lead_ref, hfv, lead, rows_of(token + at), rows_of(token + at + 1))
            return cells, lead

        return lax.fori_loop(0, count // UNROLL, body, (cells, lead))

    def moved(cells):
        return [jnp.concatenate([jnp.zeros((1, LANES), f32), cell[:-1]], axis=0) for cell in cells]

    cells = [jnp.zeros((blocks, LANES), f32) for _ in range(tiles)]
    lead = begin(p_ref, hfv, [kb_ref[0:1, :] * v for v in tiles_of(init_ref, tiles)], pl.ds(0, 1))
    cells, lead = run(cells, lead, BLOCK - EARLY, 0, EARLY, False)
    cells, lead = run(moved(cells), lead, 0, EARLY, BLOCK, False)
    cells, lead = run(moved(cells), lead, 0, EARLY + BLOCK, BLOCK, True)
    for i in range(tiles):
        end_ref[:, LANES * i : LANES * (i + 1)] = cells[i][-1:]
        lead_end_ref[:, LANES * i : LANES * (i + 1)] = lead[i][1]


def lead_kernel(p_ref, keep_ref, hfv_ref, start_ref, early_ref, lead_ref):
    rows, tiles = lead_ref.shape[:2]
    hfv = tiles_of(hfv_ref, tiles)
    lead_ref[:, :, : spaced(COVERED), :] = early_ref[...]
    for r in range(rows):
        carried = begin(p_ref.at[r], hfv, tiles_of(start_ref.at[r], tiles), rows_of(COVERED))
        run_chain(p_ref.at[r], keep_ref.at[r], lead_ref.at[r], hfv, carried, COVERED, LEAD - COVERED)


def lead_forward(p, keep, hfv, start, early):
    rows, tiles = early.shape[:2]
    out_shape = [((rows, tiles, spaced(LEAD), LANES), f32)]
    return call(lead_kernel, out_shape, (p, keep, hfv, start, early), name="lead_forward")[0]


def token_terms(prev, c, yf, yr, x, g, keep, hfv, hrv):
    tau_f = jnp.tanh(yf + hfv * prev)
    tau_r = jnp.tanh(yr + hrv * prev)
    f, omf, gate, omg = 0.5 + 0.5 * tau_f, 0.5 - 0.5 * tau_f, 0.5 + 0.5 * tau_r, 0.5 - 0.5 * tau_r
    cell = f * prev + omf * c
    gg = g * gate
    dr = gg * omg * (cell - x)
    e = (prev - c) * f * omf
    slope = f + e * (2.0 * hfv)
    return dict(
        cell=cell, hidden=gate * cell + omg * x, high=g * omg, gg=gg, dr=dr, e=e, omf=omf,
        a=keep * slope, b=keep * (slope * gg + dr * (2.0 * hrv)),
    )


def block_terms(p_ref, keep_ref, prev_ref, x_ref, g_ref, hfv, hrv, r, k, i):
    tiles = len(hfv)
    at = pl.ds(pl.multiple_of(k * SPACED, 8), BLOCK)
    devices = BLOCK // g_ref.shape[2]
    lanes = slice(LANES * i, LANES * (i + 1))
    g = jnp.concatenate([g_ref[k * devices + n, r, :, lanes].astype(f32) for n in range(devices)], axis=0)
    x = x_ref[r, i, pl.ds(pl.multiple_of(k * BLOCK, BLOCK), BLOCK), :].astype(f32)
    c, yf, yr = (p_ref[r, m * tiles + i, at, :] for m in range(3))
    return token_terms(prev_ref[i, at, :], c, yf, yr, x, g, keep_ref[r, at, :], hfv[i], hrv[i])


def composed(a, b):
    p, q = (value.reshape(-1, TOGETHER, LANES) for value in (a, b))
    row = lax.broadcasted_iota(jnp.int32, p.shape, 1)
    step = 1
    while step < TOGETHER:
        there = row < TOGETHER - step
        q += jnp.where(there, p * pltpu.roll(q, TOGETHER - step, 1), 0.0)
        p *= jnp.where(there, pltpu.roll(p, TOGETHER - step, 1), 1.0)
        step *= 2
    return p.reshape(a.shape), q.reshape(a.shape)


def entering(p, q, d):
    left = pltpu.roll((p * d + q).reshape(-1, TOGETHER, LANES), TOGETHER - 1, 1)
    row = lax.broadcasted_iota(jnp.int32, left.shape, 1)
    return jnp.where(row < TOGETHER - 1, left, d.reshape(left.shape)).reshape(d.shape)


def run_back(p_ref, q_ref, d_ref, carried, count):
    carried = [jnp.broadcast_to(d, (TOGETHER, LANES)) for d in carried]

    def body(j, carried):
        base = pl.multiple_of(count - UNROLL * TOGETHER * (j + 1), UNROLL * TOGETHER)
        for u in reversed(range(UNROLL)):
            at = base + u * TOGETHER
            now = []
            for i, d in enumerate(carried):
                if d_ref is not None:
                    d_ref[i, pl.ds(at, TOGETHER), :] = d
                now.append(p_ref[i, pl.ds(at, 1), :] * d + q_ref[i, pl.ds(at, 1), :])
            carried = now
        return carried

    carried = lax.fori_loop(0, count // (UNROLL * TOGETHER), body, carried)
    return [d[0:1] for d in carried]


def entry_kernel(
    p_ref, keep_ref, seg_ref, x_ref, g_ref, hfv_ref, hrv_ref, start_ref, first_ref, back_ref, prev_ref, a_ref, b_ref
):
    rows, slots = p_ref.shape[:2]
    tiles = slots // 3
    hfv, hrv = tiles_of(hfv_ref, tiles), tiles_of(hrv_ref, tiles)
    blocks = -(-REACH // BLOCK)
    for r in range(rows):
        prev_ref[...] = seg_ref[r, :, : blocks * SPACED, :]
        start = [keep_ref[r, 0:1, :] * v for v in tiles_of(start_ref.at[r], tiles)]
        run_chain(p_ref.at[r], keep_ref.at[r], prev_ref, hfv, begin(p_ref.at[r], hfv, start, pl.ds(0, 1)), 0, REACH)
        first_ref[r] = prev_ref[:, : spaced(REACH), :]
        for k in range(blocks):
            for i in range(tiles):
                t = block_terms(p_ref, keep_ref, prev_ref, x_ref, g_ref, hfv, hrv, r, k, i)
                rows_here = slice(BLOCK * k, BLOCK * (k + 1))
                a_ref[i, rows_here, :], b_ref[i, rows_here, :] = composed(t["a"], t["b"])
        carried = run_back(a_ref, b_ref, None, [jnp.zeros((1, LANES), f32)] * tiles, blocks * BLOCK)
        for i in range(tiles):
            back_ref[r, :, LANES * i : LANES * (i + 1)] = carried[i]


def entry(p, keep, seg, x_own, g_own, hfv, hrv, start, waits):
    rows, slots, _, _ = p.shape
    tiles = slots // 3
    blocks = -(-REACH // BLOCK)
    length, count = blocks * SPACED, blocks * BLOCK
    return call(
        entry_kernel,
        [((rows, tiles, spaced(REACH), LANES), f32), ((rows, 1, tiles * LANES), f32)],
        (p, keep, seg, x_own, g_own, hfv, hrv, start),
        waits=waits,
        scratch=[((tiles, length, LANES), f32)] + [((tiles, count, LANES), f32)] * 2,
        name="entry",
    )


def backward_kernel(
    where_ref, p_ref, keep_ref, seg_ref, lead_ref, first_ref, x_ref, g_ref, hfv_ref, hrv_ref, carry_ref, vectors_ref,
    gp_ref, hidden_ref, high_ref, sums_ref, final_ref, means_ref,
    prev_ref, a_ref, b_ref, gg_ref, e_ref, omf_ref, dr_ref, d_ref,
):
    rows, slots = p_ref.shape[:2]
    tiles = slots // 3
    blocks = p_ref.shape[2] // SPACED
    hfv, hrv = tiles_of(hfv_ref, tiles), tiles_of(hrv_ref, tiles)
    devices, block = BLOCK // g_ref.shape[2], g_ref.shape[2]
    sums_ref[...] = jnp.zeros_like(sums_ref)
    for r in range(rows):
        prev_ref[...] = seg_ref[r]

        @pl.when(where_ref[0] == 0)
        def _():
            prev_ref[:, : spaced(LEAD), :] = lead_ref[r]

        @pl.when(where_ref[0] != 0)
        def _():
            prev_ref[:, : spaced(REACH), :] = first_ref[r]

        @pl.loop(0, blocks)
        def _(k):
            out = pl.ds(pl.multiple_of(k * BLOCK, BLOCK), BLOCK)
            for i in range(tiles):
                t = block_terms(p_ref, keep_ref, prev_ref, x_ref, g_ref, hfv, hrv, r, k, i)
                lanes = slice(LANES * i, LANES * (i + 1))
                for n in range(devices):
                    hidden_ref[k * devices + n, r, :, lanes] = t["hidden"][n * block : (n + 1) * block].astype(bf16)
                high_ref[r, i, out, :] = t["high"].astype(bf16)
                a_ref[i, out, :], b_ref[i, out, :] = composed(t["a"], t["b"])
                for ref, name in zip((gg_ref, e_ref, omf_ref, dr_ref), ("gg", "e", "omf", "dr")):
                    ref[i, out, :] = t[name]
                final_ref[r, :, lanes] = t["cell"][-1:]

        run_back(a_ref, b_ref, d_ref, tiles_of(carry_ref.at[r], tiles), blocks * BLOCK)

        @pl.loop(0, blocks)
        def _(k):
            at = pl.ds(pl.multiple_of(k * SPACED, 8), BLOCK)
            out = pl.ds(pl.multiple_of(k * BLOCK, BLOCK), BLOCK)
            first, second = jnp.zeros((BLOCK, LANES), f32), jnp.zeros((BLOCK, LANES), f32)
            for i in range(tiles):
                prev = prev_ref[i, at, :]
                u = entering(a_ref[i, out, :], b_ref[i, out, :], d_ref[i, out, :]) + gg_ref[i, out, :]
                df, dr = u * e_ref[i, out, :], dr_ref[i, out, :]
                dc = u * omf_ref[i, out, :]
                for m, value in enumerate((dc, df, dr)):
                    slot = m * tiles + i
                    lane = lax.rem(slot + slots - where_ref[4], slots) * LANES
                    gp_ref[r, out, pl.ds(pl.multiple_of(lane, LANES), LANES)] = value.astype(bf16)
                    first += value * vectors_ref[slot, 0:1, :]
                    second += value * ((1.0 if m == 0 else 2.0) * p_ref[r, slot, at, :] - vectors_ref[slot, 1:2, :])
                lanes = slice(LANES * i, LANES * (i + 1))
                for m, value in enumerate((df * prev, dr * prev, df, dr)):
                    sums_ref[m : m + 1, lanes] += jnp.sum(value, axis=0, keepdims=True)
                for m, value in enumerate((dc, df, dr)):
                    lane = lax.rem(m * tiles + i + slots - where_ref[4], slots) * LANES
                    at_lane = pl.ds(pl.multiple_of(lane, LANES), LANES)
                    sums_ref[7:8, at_lane] += jnp.sum(value, axis=0, keepdims=True)
            means_ref[r, 0, out, :] = first
            means_ref[r, 1, out, :] = second


def backward(where, p, keep, seg, lead, first, x_own, g_own, hfv, hrv, carry, vectors):
    rows, slots, length, _ = p.shape
    tiles = slots // 3
    tokens = length // SPACED * BLOCK
    width = tiles * LANES
    return call(
        backward_kernel,
        [
            ((rows, tokens, 3 * width), bf16),
            (g_own.shape, bf16),
            ((rows, tiles, tokens, LANES), bf16),
            ((8, 3 * width), f32),
            ((rows, 1, width), f32),
            ((rows, 2, tokens, LANES), f32),
        ],
        (p, keep, seg, lead, first, x_own, g_own, hfv, hrv, carry, vectors),
        (where,),
        scratch=[((tiles, length, LANES), f32)] + [((tiles, tokens, LANES), f32)] * 7,
        name="backward",
    )


def weight_back_kernel(normed_ref, gp_ref, sums_ref, *refs, part, group, cuts):
    count = sum(len(rows) for rows in cuts)
    w_refs, (by_feature_ref, *out_refs) = refs[: len(refs) - count - 1], refs[len(refs) - count - 1 :]
    total, _, features = normed_ref.shape
    row_block = features // 2 // group
    columns = out_refs[0].shape[2]
    span = 2 * LANES
    devices = span // row_block
    lane_tiles = gp_ref.shape[2] // LANES
    for k in range(group // devices):
        lane = slice(part * (features // 2) + k * span, part * (features // 2) + (k + 1) * span)
        p = sum(
            lax.dot_general(normed_ref[r, :, lane], gp_ref[r], (((0,), (0,)), ((), ())), preferred_element_type=f32)
            for r in range(total)
        )
        first = w_refs[0].shape[0]
        w = [w_refs[0][lane.start : min(lane.stop, first), :]] if lane.start < first else []
        if lane.stop > first:
            w.append(w_refs[1][max(lane.start - first, 0) : lane.stop - first, :])
        w = jnp.concatenate(w).astype(f32)
        for m, value in enumerate((p * w, w * sums_ref[7:8, :])):
            value = functools.reduce(jnp.add, [value[:, LANES * j : LANES * (j + 1)] for j in range(lane_tiles)])
            by_feature_ref[m : m + 1, k * span : (k + 1) * span] = jnp.sum(jnp.transpose(value), axis=0, keepdims=True)
        p = p.astype(bf16)
        outs = iter(out_refs)
        for split, rows in enumerate(cuts):
            start = 0
            for step in rows:
                out_ref = next(outs)
                for n in range(devices):
                    row = n * row_block + start
                    out_ref[k * devices + n, :step] = p[row : row + step, split * columns : (split + 1) * columns]
                    if out_ref.shape[1] > step:
                        out_ref[k * devices + n, step:] = jnp.zeros((out_ref.shape[1] - step, columns), bf16)
                start += step


def weight_back(normed, gp, sums, weights, part, group, cuts, waits, spare=0):
    features = normed.shape[2]
    columns = gp.shape[2] // len(cuts)
    kernel = functools.partial(weight_back_kernel, part=part, group=group, cuts=cuts)
    out_shape = [((2, features // 2), f32)] + [((group, step, columns), bf16) for rows in cuts for step in rows]
    (count, step, width), dtype = out_shape[-1]
    out_shape[-1] = ((count, step + spare, width), dtype)
    return call(kernel, out_shape, (normed, gp, sums, *weights), waits=waits, name="weight_back")


def norm_back_kernel(where_ref, stats_ref, means_ref, gp_ref, gain_ref, *refs, orders, with_hidden):
    count = len(orders[0])
    x_refs, refs = refs[: 2 * count], refs[2 * count :]
    *w_refs, high_ref, hidden_ref = refs[:-10]
    all_out_refs, (some_ref, gn_ref) = refs[-10:-2], refs[-2:]
    half_count, total, block, _ = all_out_refs[0].shape
    features = gain_ref.shape[1]
    half_width = features // 2
    together = gn_ref.shape[0] // block
    for odd in (1, 0):
        out_refs = all_out_refs[4 * (1 - odd) : 4 * (2 - odd)]
        for r in range(total):
            for d in range(0, count, together):
                tokens = []
                for n in range(together):
                    place = where_ref[3] ^ (orders[0][d + n] | odd)
                    tokens.append(pl.ds(pl.multiple_of(place * block, 16), block))
                    some_ref[n * block : (n + 1) * block, :] = gp_ref[r, tokens[n], :]
                lane = 0
                for w_ref in w_refs:
                    rows = w_ref.shape[0]
                    gn_ref[:, lane : lane + rows] = lax.dot_general(
                        some_ref[...], w_ref[...], (((1,), (1,)), ((), ())), preferred_element_type=f32
                    )
                    lane += rows
                for n in range(together):
                    x_ref = x_refs[orders[0][d + n] | odd]
                    mean, inv = stats_ref[r, 0, tokens[n], :], stats_ref[r, 1, tokens[n], :]
                    first, second = (
                        jnp.sum(means_ref[r, m, tokens[n], :], axis=-1, keepdims=True) * (1.0 / features)
                        for m in range(2)
                    )
                    slope = inv * inv * second
                    rest = inv * first - slope * mean
                    for part in range(2):
                        at_d = orders[part].index(orders[0][d + n])
                        out_ref = out_refs[2 * part + at_d // half_count]
                        start = pl.multiple_of((where_ref[0] ^ part) * half_width, LANES)
                        if with_hidden:
                            high = high_ref[r, where_ref[0] ^ part, tokens[n], :].astype(f32)
                        for j in range(half_width // LANES):
                            at = slice(part * half_width + LANES * j, part * half_width + LANES * (j + 1))
                            value = inv * (gn_ref[n * block : (n + 1) * block, at] * gain_ref[:, at])
                            x = x_ref[r, :block, pl.ds(start + LANES * j, LANES)].astype(f32)
                            value -= slope * x + rest
                            if with_hidden:
                                value += jnp.where(where_ref[3] == j, high, 0.0)
                            out_ref[at_d % half_count, r, :, LANES * j : LANES * (j + 1)] = value.astype(bf16)
                        if with_hidden:
                            hidden = hidden_ref[where_ref[3] ^ (orders[0][d + n] | odd), r]
                            out_ref[at_d % half_count, r, :, half_width:] = hidden[:, LANES * part : LANES * (part + 1)]


def norm_back(where, blocks, orders, stats, means, gp, weights, gain, high, hidden, with_hidden, waits):
    rows, block, features = blocks[0].shape
    block -= STATS
    together = 2 * LANES // block
    out = call(
        functools.partial(norm_back_kernel, orders=orders, with_hidden=with_hidden),
        [((len(blocks) // 4, rows, block, features // 2 + with_hidden * LANES), bf16)] * 8,
        (stats, means, gp, gain, *blocks, *weights, high, hidden), (where,), waits,
        scratch=[((together * block, gp.shape[2]), bf16), ((together * block, features), f32)],
        name="norm_back",
    )
    return out[:4], out[4:]


def totals_kernel(where_ref, sums_ref, own_ref, other_ref, gain_ref, shift_ref, out_ref, *, chunk):
    half_width = own_ref.shape[1]
    out_ref[...] = jnp.zeros_like(out_ref)
    for i in range(2):
        lane = pl.ds(pl.multiple_of(i * chunk + where_ref[3] * LANES, LANES), LANES)
        out_ref[0:4, lane] = sums_ref[0:4, LANES * i : LANES * (i + 1)]
    for part, ref in enumerate((own_ref, other_ref)):
        lane = pl.ds(pl.multiple_of((where_ref[0] ^ part) * half_width, LANES), half_width)
        at = slice(part * half_width, (part + 1) * half_width)
        out_ref[4:5, lane] = (ref[0:1, :] - shift_ref[:, at] * ref[1:2, :]) / gain_ref[:, at]
        out_ref[5:6, lane] = ref[1:2, :]


def bf16_parts(row):
    rows = []
    for _ in range(3):
        upper = lax.reduce_precision(row, 8, 7)
        rows.append(upper.astype(bf16))
        row = row - upper
    return rows


def local(inputs, weight, gain, shift, forget_vec, reset_vec, forget_bias, reset_bias, initial, resets, grad_out):
    rows, block_len, features = inputs.shape
    row_block, columns_here = weight.shape
    sections = lax.axis_size("fsdp")
    ranks = lax.axis_size("dp")
    group = sections // 2
    tokens = group * block_len
    index = lax.axis_index("fsdp")
    half, place = index // group, index % group
    rank = lax.axis_index("dp")
    first_half = half == 0
    groups = [list(range(group)), list(range(group, sections))]
    chunk = math.gcd(features, columns_here)
    chunks, piece = features // chunk, chunk // group
    width = chunks * piece
    tiles = width // LANES
    slots = 3 * tiles
    parts = columns_here // chunk
    columns = parts * piece
    aligned = piece == LANES and chunks == 2
    paired = ranks == 2 and aligned
    turn = rank * (columns // LANES) if paired else jnp.zeros_like(rank)
    where = jnp.stack([half, rank, index % 2, place, turn]).astype(jnp.int32)
    bits = [1 << b for b in range(1, group.bit_length() - 1)]
    ways = (bits[::-1], bits)
    orders = []
    for way in ways:
        order = [0]
        for bit in way:
            order += [d | bit for d in order]
        orders.append(order)

    def across(value):
        return lax.ppermute(value, "fsdp", [(j, (j + group) % sections) for j in range(sections)])

    def flipped(value, bit):
        return lax.ppermute(value, "fsdp", [(j, j ^ bit) for j in range(sections)])

    def swapped(value):
        return lax.ppermute(value, "dp", [(0, 1), (1, 0)])

    def shared(value):
        return lax.all_to_all(value, "fsdp", 0, 0, tiled=True, axis_index_groups=groups)

    def own(vector):
        return lax.dynamic_index_in_dim(vector.reshape(-1, chunks, group, piece), place, 2, False).reshape(-1, width)

    def halves_turned(vector):
        low, high = vector[..., : features // 2], vector[..., features // 2 :]
        return jnp.concatenate([jnp.where(first_half, low, high), jnp.where(first_half, high, low)], axis=-1)

    def dealt(value, waits=()):
        if aligned:
            return deal(value, group, waits)
        n, wide = value.shape
        return value.reshape(n, wide // chunk, group, piece).transpose(2, 0, 1, 3).reshape(group, n, wide // group)

    def collected(pieces, dtype, waits=()):
        if aligned:
            return collect(pieces, dtype, waits)
        wide = pieces[0].shape[2]
        back = lambda v: v.reshape(group, -1, wide // piece, piece).transpose(1, 2, 0, 3).reshape(-1, wide * group)
        return jnp.concatenate([back(v) for v in pieces]).astype(dtype)

    mine = shared(dealt(weight))
    theirs = across(mine)
    beside = swapped(mine) if paired else mine
    blocks = {0: stats(inputs, (1 - resets).astype(f32)[:, None, :], (mine,))}
    for bit in bits[::-1]:
        blocks |= {d | bit: flipped(value, bit) for d, value in blocks.items()}
    blocks = {d: fence(value, (theirs, beside)) for d, value in blocks.items()}
    blocks |= {d | 1: flipped(value, 1) for d, value in blocks.items()}
    blocks = [blocks[d] for d in range(group)]
    early_rows = features // 2
    if paired:
        early, late = [mine, beside], [theirs, swapped(theirs)]
    else:
        early, late = (
            [lax.all_gather(v.reshape(-1, columns), "dp", axis=1, tiled=True)] for v in (mine, theirs)
        )
    hfv, hrv = 0.5 * own(forget_vec), 0.5 * own(reset_vec)
    bias = jnp.concatenate([jnp.zeros((1, width), f32), own(forget_bias), own(reset_bias)]).reshape(-1, 1, LANES)
    gain_row, shift_row = halves_turned(gain)[None], halves_turned(shift)[None]
    vector_rows = [*bf16_parts(gain_row), *bf16_parts(shift_row)]
    vector_rows = jnp.pad(jnp.concatenate(vector_rows), ((0, 10), (0, 0)))
    g_own = shared(dealt(grad_out.reshape(-1, features)).reshape(group, rows, block_len, width))
    normed, token_stats, keep, *x_own = norm(where, blocks, gain_row, shift_row, aligned, (g_own,))
    if aligned:
        x_own = x_own[0]
    else:
        in_order = jnp.stack(blocks)[place ^ jnp.arange(group)][:, :, :block_len].swapaxes(0, 1)
        x_own = own(in_order.reshape(rows * tokens, features)).reshape(rows, tokens, tiles, LANES).swapaxes(1, 2)
    some, some_vectors, early_weight = project(where, normed, vector_rows, early, early_rows, slots)
    p, seg, lead, end, lead_end, vectors, late_weight = blocks_forward(
        where, normed, vector_rows, some, some_vectors, bias, keep, hfv, own(initial)[:, None, :], late,
        features - early_rows,
    )
    weights = (early_weight, late_weight)
    start = across(end)
    lead = lead_forward(p, keep, hfv, lead_end, lead)
    first, back = entry(p, keep, seg, x_own, g_own, hfv, hrv, start, ())
    carry = jnp.where(first_half, across(back), 0.0)
    gp, hidden_own, high_own, sums, final, means = backward(
        where, p, keep, seg, lead, first, x_own, g_own, hfv, hrv, carry, vectors
    )

    mask = (jnp.arange(group) == place)[:, None]

    splits = 2 if paired else 1
    by_feature_other, *away = weight_back(normed, gp, sums, weights, 1, group, [(row_block,)] * splits, (), SPARE * paired)
    away_got = swapped(away[1]) if paired else None

    sent, kept = norm_back(
        where, blocks, orders, token_stats, means, gp, weights, gain_row, high_own, hidden_own, aligned,
        (by_feature_other,),
    )
    if not aligned:
        spread = high_own.swapaxes(1, 2).reshape(rows, group, block_len, chunks, 1, piece).swapaxes(0, 1)
        spread = jnp.where(mask, spread.astype(f32), 0.0).reshape(group, rows, block_len, features)
        spread = halves_turned(spread)[place ^ jnp.arange(group)]
        halves = (spread[..., : features // 2], spread[..., features // 2 :])
        n = group // 4

        def with_high(arrays, odd):
            add = [half[d | odd] for half, order in zip(halves, orders) for d in order]
            return [(v.astype(f32) + jnp.stack(add[i * n : (i + 1) * n])).astype(bf16) for i, v in enumerate(arrays)]

        sent, kept = with_high(sent, 1), with_high(kept, 0)
    got = [flipped(value, 1) for value in sent]
    if paired:
        away = added(away[0], away_got, kept[:1])
    else:
        away = lax.psum_scatter(away[0], "dp", scatter_dimension=2, tiled=True)
    z_got = across(away)
    kept, sent = halve(kept, got, features // 2)
    bit_pairs = list(zip(*(w[::-1] for w in ways)))
    got = [flipped(value, bit) for value, bit in zip(sent, bit_pairs.pop(0))]
    cuts = [(row_block,), (row_block // 2,) * 2][:splits]
    by_feature_own, *here = weight_back(normed, gp, sums, weights, 0, group, cuts, (away,))
    if paired:
        here_got = [swapped(value) for value in here[1:]]
    else:
        here = lax.psum_scatter(here[0], "dp", scatter_dimension=2, tiled=True)
    if aligned:
        totals = call(
            functools.partial(totals_kernel, chunk=chunk), [((8, features), f32)],
            (sums, by_feature_own, by_feature_other, gain_row, shift_row), (where,), name="totals",
        )[0]
    else:
        spread = jnp.where(mask, sums[:4, :width].reshape(4, chunks, 1, piece), 0.0).reshape(4, features)
        product, shift_sum = jnp.concatenate([by_feature_own, by_feature_other], axis=1)
        gain_sum = (product - shift_row[0] * shift_sum) / gain_row[0]
        totals = jnp.concatenate([spread, halves_turned(jnp.stack([gain_sum, shift_sum]))], axis=0)
    for way in bit_pairs:
        kept, sent = halve(kept, got, features // 2)
        got = [flipped(value, bit) for value, bit in zip(sent, way)]
    sources = []
    for way in ways:
        sources.append([0])
        for bit in (1, *way[::-1]):
            sources[-1] += [d | bit for d in sources[-1]]
    grad_inputs, *hidden = finish(where, kept, got, features, sources)
    if aligned:
        hidden = hidden[0]
    else:
        hidden = collected([shared(hidden_own).reshape(group, -1, width)], bf16).reshape(rows, block_len, features)
    for bit in [1 << b for b in range(group.bit_length() - 1)]:
        totals = added(totals, flipped(totals, bit))
    waits = (*got, totals)
    value = merge(here[0], here_got, z_got, waits) if paired else added(here, z_got, waits)
    grad_weight = collected([shared(value)], f32)
    totals = added(totals, swapped(totals)) if ranks == 2 else lax.psum(totals, "dp")
    totals = added(totals, across(totals), (grad_inputs,))

    own_width = features // sections
    if piece == own_width and chunks == 2:
        final = final[:, 0]
        low_part = lax.ppermute(final[:, :piece], "fsdp", [(j + group, j) for j in range(group)])
        final_state = jnp.where(first_half, low_part, final[:, piece:])
    else:
        spread = jnp.where(mask, final.reshape(rows, chunks, 1, piece), 0.0).reshape(rows, features)
        spread = lax.psum(jnp.where(first_half, 0.0, spread), "fsdp")
        final_state = lax.dynamic_slice_in_dim(spread, index * own_width, own_width, 1)

    return (hidden, grad_inputs, final_state, grad_weight, *[totals[i] for i in range(6)])


def solution(mesh):
    in_specs = (
        P("dp", "fsdp", None), P("fsdp", "dp"), P(), P(), P(), P(), P(), P(),
        P("dp", None), P("dp", "fsdp"), P("dp", "fsdp", None),
    )
    out_specs = (
        P("dp", "fsdp", None), P("dp", "fsdp", None), P("dp", "fsdp"), P("fsdp", "dp"), P(), P(), P(), P(), P(), P(),
    )
    return jax.shard_map(local, mesh=mesh, in_specs=in_specs, out_specs=out_specs, check_vma=False)
```

```python
import functools
import math

import jax
import jax.numpy as jnp
from jax import lax
from jax.experimental import pallas as pl
from jax.experimental.pallas import tpu as pltpu
from jax.sharding import PartitionSpec as P

SENT = 128
LEAD = 768
REACH = 192
EPSILON = 1e-05
LANES = 128
BLOCK = 128
SPACED = 136
EARLY = REACH - BLOCK
COVERED = EARLY + 2 * BLOCK
STATS = 16
SPARE = 16
UNROLL = 8
TOGETHER = 8
f32 = jnp.float32
bf16 = jnp.bfloat16


def spaced(token):
    return token + (SPACED - BLOCK) * (token // BLOCK)


def tiles_of(ref, count):
    return [ref[:, LANES * i : LANES * (i + 1)] for i in range(count)]


def call(kernel, out_shape, operands, scalars=(), waits=(), scratch=(), mebibytes=14, name=None):
    in_vmem, in_smem = pl.BlockSpec(memory_space=pltpu.VMEM), pl.BlockSpec(memory_space=pltpu.SMEM)
    before = len(scalars) + len(operands)

    def body(*refs):
        kernel(*refs[:before], *refs[before + len(waits) :])

    return pl.pallas_call(
        body,
        in_specs=[in_smem] * len(scalars) + [in_vmem] * len(operands) + [pl.BlockSpec(memory_space=pl.ANY)] * len(waits),
        out_specs=[in_vmem] * len(out_shape),
        out_shape=[jax.ShapeDtypeStruct(*shape) for shape in out_shape],
        scratch_shapes=[pltpu.VMEM(*shape) for shape in scratch],
        compiler_params=pltpu.CompilerParams(vmem_limit_bytes=mebibytes << 20),
        name=name,
    )(*scalars, *operands, *waits)


def fence(value, waits):
    return pl.pallas_call(
        lambda *refs: None,
        in_specs=[pl.BlockSpec(memory_space=pl.ANY)] * (1 + len(waits)),
        out_specs=pl.BlockSpec(memory_space=pl.ANY),
        out_shape=jax.ShapeDtypeStruct(value.shape, value.dtype),
        input_output_aliases={0: 0},
        name="fence",
    )(value, *waits)


def deal_kernel(in_ref, out_ref, *, chunks):
    group = out_ref.shape[0]
    for q in range(group):
        for c in range(chunks):
            lane = (c * group + q) * LANES
            out_ref[q, :, LANES * c : LANES * (c + 1)] = in_ref[:, lane : lane + LANES]


def deal(value, group, waits=()):
    n, features = value.shape
    kernel = functools.partial(deal_kernel, chunks=features // group // LANES)
    return call(kernel, [((group, n, features // group), value.dtype)], (value,), waits=waits, name="deal")[0]


def collect_kernel(*refs):
    *in_refs, out_ref = refs
    row = 0
    for ref in in_refs:
        group, n, width = ref.shape
        for q in range(group):
            for c in range(width // LANES):
                lane = (c * group + q) * LANES
                value = ref[q, :, LANES * c : LANES * (c + 1)]
                out_ref[row : row + n, lane : lane + LANES] = value.astype(out_ref.dtype)
        row += n


def collect(pieces, dtype, waits=()):
    group, _, width = pieces[0].shape
    shape = (sum(value.shape[1] for value in pieces), group * width)
    return call(collect_kernel, [(shape, dtype)], pieces, waits=waits, name="collect")[0]


def add_kernel(a_ref, b_ref, out_ref):
    b = b_ref[...] if b_ref.shape == a_ref.shape else b_ref[:, : a_ref.shape[1]]
    out_ref[...] = (a_ref[...].astype(f32) + b.astype(f32)).astype(out_ref.dtype)


def added(a, b, waits=()):
    return call(add_kernel, [(a.shape, a.dtype)], (a, b), waits=waits, name="added")[0]


def blocks_of(refs):
    return [ref.at[i] for ref in refs for i in range(ref.shape[0])]


def halve_kernel(*refs, width):
    *in_refs, first_stays, first_goes, second_stays, second_goes = refs
    n = len(in_refs) // 4
    parts = [blocks_of(in_refs[n * i : n * (i + 1)]) for i in range(4)]
    for part, (stays, goes) in enumerate(((first_stays, first_goes), (second_stays, second_goes))):
        out = blocks_of([stays, goes])
        for out_ref, a_ref, b_ref in zip(out, parts[part], parts[2 + part]):
            out_ref[:, :, :width] = (a_ref[:, :, :width].astype(f32) + b_ref[:, :, :width].astype(f32)).astype(bf16)
            there = a_ref.shape[2]
            if there > width:
                out_ref[:, :, width:there] = a_ref[:, :, width:]
                out_ref[:, :, there:] = b_ref[:, :, width:]


def halve(kept, got, width, waits=()):
    n = sum(value.shape[0] for value in kept) // 4
    *shape, there = kept[0].shape[1:]
    out = call(
        functools.partial(halve_kernel, width=width), [((n, *shape, 2 * there - width), bf16)] * 4, (*kept, *got),
        waits=waits, name="halve",
    )
    return out[0::2], out[1::2]


def merge_kernel(own_ref, away_ref, *refs):
    *got_refs, out_ref = refs
    start = 0
    for ref in got_refs:
        rows = slice(start, start + ref.shape[1])
        value = own_ref[:, rows, :].astype(f32) + ref[...].astype(f32) + away_ref[:, rows, :].astype(f32)
        out_ref[:, rows, :] = value.astype(bf16)
        start = rows.stop


def merge(own, got, away, waits=()):
    return call(merge_kernel, [(own.shape, bf16)], (own, away, *got), waits=waits, name="merge")[0]


def finish_kernel(where_ref, *refs, sources):
    in_refs, (out_ref, *hidden_ref) = refs[:4], refs[4:]
    half_width = out_ref.shape[2] // 2
    for part in range(2):
        kept_ref, got_ref = in_refs[part], in_refs[2 + part]
        value = kept_ref[0, :, :, :half_width].astype(f32) + got_ref[0, :, :, :half_width].astype(f32)
        lane = pl.multiple_of((where_ref[0] ^ part) * half_width, LANES)
        out_ref[:, :, pl.ds(lane, half_width)] = value.astype(bf16)
        if hidden_ref:
            tiles = [ref[0, :, :, at : at + LANES] for ref in (kept_ref, got_ref) for at in range(half_width, ref.shape[3], LANES)]
            for value, source in zip(tiles, sources[part]):
                lane = pl.multiple_of(part * half_width + (where_ref[3] ^ source) * LANES, LANES)
                hidden_ref[0][:, :, pl.ds(lane, LANES)] = value


def finish(where, kept, got, features, sources, waits=()):
    _, rows, block, there = kept[0].shape
    out_shape = [((rows, block, features), bf16)] * (1 + (there > features // 2))
    kernel = functools.partial(finish_kernel, sources=sources)
    return call(kernel, out_shape, (*kept, *got), (where,), waits, name="finish")


def stats_kernel(x_ref, keep_ref, out_ref):
    total, block, features = x_ref.shape

    def row(column):
        return jnp.transpose(jnp.broadcast_to(column, (block, LANES)))[0:1, :]

    for r in range(total):
        out_ref[r, :block, :] = x_ref[r]
        x = x_ref[r].astype(f32)
        mean = jnp.sum(x, axis=-1, keepdims=True) * (1.0 / features)
        centred = x - mean
        inv = lax.rsqrt(jnp.sum(centred * centred, axis=-1, keepdims=True) * (1.0 / features) + EPSILON)
        rows = [keep_ref[r]]
        for value in (row(mean), row(inv)):
            for _ in range(3):
                upper = value.astype(bf16).astype(f32)
                rows.append(upper)
                value = value - upper
        rows = jnp.concatenate(rows + [jnp.zeros_like(rows[0])] * (STATS - len(rows)), axis=0)
        if block < LANES:
            rows = jnp.concatenate([rows, jnp.zeros((STATS, LANES - block), f32)], axis=1)
        out_ref[r, block:, :LANES] = rows.astype(bf16)
        out_ref[r, block:, LANES:] = jnp.zeros((STATS, features - LANES), bf16)


def stats(inputs, keep, waits):
    rows, block, features = inputs.shape
    return call(stats_kernel, [((rows, block + STATS, features), bf16)], (inputs, keep), waits=waits, name="stats")[0]


def norm_kernel(where_ref, gain_ref, shift_ref, *refs, count):
    block_refs, (normed_ref, stats_ref, keep_ref, *own_refs) = refs[:count], refs[count:]
    total, block, features = block_refs[0].shape
    block -= STATS
    half_width = features // 2
    per_block = BLOCK // block

    def device(r, x_ref, q):
        at = pl.ds(pl.multiple_of(q * block, block), block)
        spaced_at = pl.ds(pl.multiple_of(q // per_block * SPACED + q % per_block * block, 8), block)
        rows = x_ref[r, block:, :block].astype(f32)

        def column(*of):
            row = functools.reduce(jnp.add, [rows[k : k + 1, :] for k in of])
            return jnp.transpose(jnp.broadcast_to(row, (LANES, block)))

        keep_ref[r, spaced_at, :] = column(0)
        mean, inv = column(1, 2, 3), column(4, 5, 6)
        stats_ref[r, 0, at, :] = mean
        stats_ref[r, 1, at, :] = inv
        for part in range(2):
            lane = pl.multiple_of((where_ref[0] ^ part) * half_width, LANES)
            for j in range(half_width // LANES):
                x = x_ref[r, :block, pl.ds(lane + j * LANES, LANES)].astype(f32)
                out = slice(part * half_width + j * LANES, part * half_width + (j + 1) * LANES)
                normed_ref[r, at, out] = ((x - mean) * inv * gain_ref[:, out] + shift_ref[:, out]).astype(bf16)
        for ref in own_refs:
            for i in range(2):
                lane = pl.ds(pl.multiple_of(i * half_width + where_ref[3] * LANES, LANES), LANES)
                ref[r, i, at, :] = x_ref[r, :block, lane]

    for r in range(total):
        for d, ref in enumerate(block_refs):
            device(r, ref, where_ref[3] ^ d)


def norm(where, blocks, gain, shift, aligned, waits):
    rows, block, features = blocks[0].shape
    tokens = len(blocks) * (block - STATS)
    out_shape = [
        ((rows, tokens, features), bf16),
        ((rows, 2, tokens, LANES), f32),
        ((rows, tokens // BLOCK * SPACED, LANES), f32),
    ]
    if aligned:
        out_shape.append(((rows, 2, tokens, LANES), bf16))
    kernel = functools.partial(norm_kernel, count=len(blocks))
    return call(kernel, out_shape, (gain, shift, *blocks), (where,), waits, name="norm")


def weight_into(w_ref, parts):
    if len(parts) == 1:
        w_ref[...] = parts[0][...]
        return
    pieces = len(parts) // 2
    group, _, columns = parts[0].shape
    block = sum(part.shape[1] for part in parts[:pieces])
    for rank in range(2):
        start = 0
        for part in parts[rank * pieces : (rank + 1) * pieces]:
            rows = part.shape[1]
            for q in range(group):
                row = q * block + start
                w_ref[row : row + rows, rank * columns : (rank + 1) * columns] = part[q]
            start += rows


def slot_of(where_ref, s, slots):
    return lax.rem(where_ref[4] + s, slots)


def project_kernel(where_ref, normed_ref, rows_ref, *refs):
    *parts, sum_ref, vectors_ref, w_ref = refs
    weight_into(w_ref, parts)
    depth = w_ref.shape[0]
    total, slots = sum_ref.shape[:2]
    step = 2 * BLOCK
    vectors_ref[...] = jnp.dot(rows_ref[:, :depth], w_ref[...], preferred_element_type=f32)
    for r in range(total):

        @pl.loop(0, normed_ref.shape[1] // step)
        def _(j):
            at = pl.ds(pl.multiple_of(j * step, step), step)
            p = jnp.dot(normed_ref[r, at, :depth], w_ref[...], preferred_element_type=f32)
            for s in range(slots):
                sum_ref[r, s, at, :] = p[:, LANES * s : LANES * (s + 1)]


def project(where, normed, vector_rows, parts, depth, slots):
    rows, tokens, _ = normed.shape
    out_shape = [
        ((rows, slots, tokens, LANES), f32), ((vector_rows.shape[0], slots * LANES), f32), ((depth, slots * LANES), bf16),
    ]
    return call(project_kernel, out_shape, (normed, vector_rows, *parts), (where,), name="project")


def blocks_kernel(where_ref, normed_ref, rows_ref, sum_ref, some_ref, bias_ref, keep_ref, hfv_ref, init_ref, *refs):
    *parts, p_ref, seg_ref, lead_ref, end_ref, lead_end_ref, vectors_ref, w_ref = refs
    weight_into(w_ref, parts)
    depth = w_ref.shape[0]
    total, slots = p_ref.shape[:2]
    tiles = slots // 3
    step = 2 * BLOCK
    features = normed_ref.shape[2]
    by_column = some_ref[...] + jnp.dot(rows_ref[:, features - depth :], w_ref[...], preferred_element_type=f32)
    for s in range(slots):
        slot = slot_of(where_ref, s, slots)
        lanes = slice(LANES * s, LANES * (s + 1))
        vectors_ref[slot, 0:1, :] = jnp.sum(by_column[0:3, lanes], axis=0, keepdims=True)
        vectors_ref[slot, 1:2, :] = jnp.sum(by_column[3:6, lanes], axis=0, keepdims=True) + bias_ref[slot]
    for r in range(total):

        @pl.loop(0, normed_ref.shape[1] // step)
        def _(j):
            at = pl.ds(pl.multiple_of(j * step, step), step)
            p = jnp.dot(normed_ref[r, at, features - depth :], w_ref[...], preferred_element_type=f32)
            for s in range(slots):
                slot = slot_of(where_ref, s, slots)
                scale = jnp.where(slot < tiles, 1.0, 0.5)
                value = scale * (p[:, LANES * s : LANES * (s + 1)] + sum_ref[r, s, at, :] + bias_ref[slot])
                for k in range(2):
                    to = pl.ds(pl.multiple_of((2 * j + k) * SPACED, 8), BLOCK)
                    p_ref[r, slot, to, :] = value[BLOCK * k : BLOCK * (k + 1)]

        row_blocks(
            p_ref.at[r], keep_ref.at[r], hfv_ref, init_ref.at[r], seg_ref.at[r], lead_ref.at[r], end_ref.at[r],
            lead_end_ref.at[r],
        )


def blocks_forward(where, normed, vector_rows, some, some_vectors, bias, keep, hfv, init, parts, depth):
    rows, tokens, _ = normed.shape
    slots = bias.shape[0]
    tiles = slots // 3
    state = ((rows, 1, tiles * LANES), f32)
    length = tokens // BLOCK * SPACED
    out_shape = [
        ((rows, slots, length, LANES), f32), ((rows, tiles, length, LANES), f32),
        ((rows, tiles, spaced(COVERED), LANES), f32), state, state, ((slots, 2, LANES), f32), ((depth, slots * LANES), bf16),
    ]
    return call(
        blocks_kernel, out_shape, (normed, vector_rows, some, some_vectors, bias, keep, hfv, init, *parts), (where,),
        name="blocks_forward",
    )


def chain_step(p_ref, kb_ref, prev_ref, hfv, carried, row, next_row):
    tiles = len(hfv)
    keep = kb_ref[next_row, :]
    out = []
    for i, (y, prev) in enumerate(carried):
        tau = jnp.tanh(y)
        half = 0.5 * p_ref[i, row, :]
        mid, gap = 0.5 * prev + half, 0.5 * prev - half
        prev_ref[i, row, :] = prev
        reach = hfv[i] * keep
        out.append(
            ((p_ref[tiles + i, next_row, :] + reach * mid) + (reach * gap) * tau, (keep * mid) + (keep * gap) * tau)
        )
    return out


def begin(p_ref, hfv, previous, row):
    return [(p_ref[len(hfv) + i, row, :] + hfv[i] * prev, prev) for i, prev in enumerate(previous)]


def rows_of(token):
    return pl.ds(spaced(token), 1)


def run_chain(p_ref, kb_ref, prev_ref, hfv, carried, first, count):
    def body(j, now):
        for u in range(UNROLL):
            token = first + j * UNROLL + u
            now = chain_step(p_ref, kb_ref, prev_ref, hfv, now, rows_of(token), rows_of(token + 1))
        return now

    return lax.fori_loop(0, count // UNROLL, body, carried)


def row_blocks(p_ref, kb_ref, hfv_ref, init_ref, seg_ref, lead_ref, end_ref, lead_end_ref):
    tiles = seg_ref.shape[0]
    blocks = p_ref.shape[1] // SPACED
    hfv = tiles_of(hfv_ref, tiles)

    def seg_step(cells, step, store):
        row = pl.ds(step, blocks, stride=SPACED)
        keep = kb_ref[row, :]
        out = []
        for i, cell in enumerate(cells):
            prev = keep * cell
            tau = jnp.tanh(p_ref[tiles + i, row, :] + (hfv[i] * keep) * cell)
            half = 0.5 * p_ref[i, row, :]
            if store:
                seg_ref[i, row, :] = prev
            out.append((0.5 * prev + half) + (0.5 * prev - half) * tau)
        return out

    def run(cells, lead, first, token, count, store):
        def body(j, carried):
            cells, lead = carried
            for u in range(UNROLL):
                at = j * UNROLL + u
                cells = seg_step(cells, first + at, store)
                lead = chain_step(p_ref, kb_ref, lead_ref, hfv, lead, rows_of(token + at), rows_of(token + at + 1))
            return cells, lead

        return lax.fori_loop(0, count // UNROLL, body, (cells, lead))

    def moved(cells):
        return [jnp.concatenate([jnp.zeros((1, LANES), f32), cell[:-1]], axis=0) for cell in cells]

    cells = [jnp.zeros((blocks, LANES), f32) for _ in range(tiles)]
    lead = begin(p_ref, hfv, [kb_ref[0:1, :] * v for v in tiles_of(init_ref, tiles)], pl.ds(0, 1))
    cells, lead = run(cells, lead, BLOCK - EARLY, 0, EARLY, False)
    cells, lead = run(moved(cells), lead, 0, EARLY, BLOCK, False)
    cells, lead = run(moved(cells), lead, 0, EARLY + BLOCK, BLOCK, True)
    for i in range(tiles):
        end_ref[:, LANES * i : LANES * (i + 1)] = cells[i][-1:]
        lead_end_ref[:, LANES * i : LANES * (i + 1)] = lead[i][1]


def lead_kernel(p_ref, keep_ref, hfv_ref, start_ref, early_ref, lead_ref):
    rows, tiles = lead_ref.shape[:2]
    hfv = tiles_of(hfv_ref, tiles)
    lead_ref[:, :, : spaced(COVERED), :] = early_ref[...]
    for r in range(rows):
        carried = begin(p_ref.at[r], hfv, tiles_of(start_ref.at[r], tiles), rows_of(COVERED))
        run_chain(p_ref.at[r], keep_ref.at[r], lead_ref.at[r], hfv, carried, COVERED, LEAD - COVERED)


def lead_forward(p, keep, hfv, start, early):
    rows, tiles = early.shape[:2]
    out_shape = [((rows, tiles, spaced(LEAD), LANES), f32)]
    return call(lead_kernel, out_shape, (p, keep, hfv, start, early), name="lead_forward")[0]


def token_terms(prev, c, yf, yr, x, g, keep, hfv, hrv):
    tau_f = jnp.tanh(yf + hfv * prev)
    tau_r = jnp.tanh(yr + hrv * prev)
    f, omf, gate, omg = 0.5 + 0.5 * tau_f, 0.5 - 0.5 * tau_f, 0.5 + 0.5 * tau_r, 0.5 - 0.5 * tau_r
    cell = f * prev + omf * c
    gg = g * gate
    dr = gg * omg * (cell - x)
    e = (prev - c) * f * omf
    slope = f + e * (2.0 * hfv)
    return dict(
        cell=cell, hidden=gate * cell + omg * x, high=g * omg, gg=gg, dr=dr, e=e, omf=omf,
        a=keep * slope, b=keep * (slope * gg + dr * (2.0 * hrv)),
    )


def block_terms(p_ref, keep_ref, prev_ref, x_ref, g_ref, hfv, hrv, r, k, i):
    tiles = len(hfv)
    at = pl.ds(pl.multiple_of(k * SPACED, 8), BLOCK)
    devices = BLOCK // g_ref.shape[2]
    lanes = slice(LANES * i, LANES * (i + 1))
    g = jnp.concatenate([g_ref[k * devices + n, r, :, lanes].astype(f32) for n in range(devices)], axis=0)
    x = x_ref[r, i, pl.ds(pl.multiple_of(k * BLOCK, BLOCK), BLOCK), :].astype(f32)
    c, yf, yr = (p_ref[r, m * tiles + i, at, :] for m in range(3))
    return token_terms(prev_ref[i, at, :], c, yf, yr, x, g, keep_ref[r, at, :], hfv[i], hrv[i])


def composed(a, b):
    p, q = (value.reshape(-1, TOGETHER, LANES) for value in (a, b))
    row = lax.broadcasted_iota(jnp.int32, p.shape, 1)
    step = 1
    while step < TOGETHER:
        there = row < TOGETHER - step
        q += jnp.where(there, p * pltpu.roll(q, TOGETHER - step, 1), 0.0)
        p *= jnp.where(there, pltpu.roll(p, TOGETHER - step, 1), 1.0)
        step *= 2
    return p.reshape(a.shape), q.reshape(a.shape)


def entering(p, q, d):
    left = pltpu.roll((p * d + q).reshape(-1, TOGETHER, LANES), TOGETHER - 1, 1)
    row = lax.broadcasted_iota(jnp.int32, left.shape, 1)
    return jnp.where(row < TOGETHER - 1, left, d.reshape(left.shape)).reshape(d.shape)


def run_back(p_ref, q_ref, d_ref, carried, count):
    carried = [jnp.broadcast_to(d, (TOGETHER, LANES)) for d in carried]

    def body(j, carried):
        base = pl.multiple_of(count - UNROLL * TOGETHER * (j + 1), UNROLL * TOGETHER)
        for u in reversed(range(UNROLL)):
            at = base + u * TOGETHER
            now = []
            for i, d in enumerate(carried):
                if d_ref is not None:
                    d_ref[i, pl.ds(at, TOGETHER), :] = d
                now.append(p_ref[i, pl.ds(at, 1), :] * d + q_ref[i, pl.ds(at, 1), :])
            carried = now
        return carried

    carried = lax.fori_loop(0, count // (UNROLL * TOGETHER), body, carried)
    return [d[0:1] for d in carried]


def entry_kernel(
    p_ref, keep_ref, seg_ref, x_ref, g_ref, hfv_ref, hrv_ref, start_ref, first_ref, back_ref, prev_ref, a_ref, b_ref
):
    rows, slots = p_ref.shape[:2]
    tiles = slots // 3
    hfv, hrv = tiles_of(hfv_ref, tiles), tiles_of(hrv_ref, tiles)
    blocks = -(-REACH // BLOCK)
    for r in range(rows):
        prev_ref[...] = seg_ref[r, :, : blocks * SPACED, :]
        start = [keep_ref[r, 0:1, :] * v for v in tiles_of(start_ref.at[r], tiles)]
        run_chain(p_ref.at[r], keep_ref.at[r], prev_ref, hfv, begin(p_ref.at[r], hfv, start, pl.ds(0, 1)), 0, REACH)
        first_ref[r] = prev_ref[:, : spaced(REACH), :]
        for k in range(blocks):
            for i in range(tiles):
                t = block_terms(p_ref, keep_ref, prev_ref, x_ref, g_ref, hfv, hrv, r, k, i)
                rows_here = slice(BLOCK * k, BLOCK * (k + 1))
                a_ref[i, rows_here, :], b_ref[i, rows_here, :] = composed(t["a"], t["b"])
        carried = run_back(a_ref, b_ref, None, [jnp.zeros((1, LANES), f32)] * tiles, blocks * BLOCK)
        for i in range(tiles):
            back_ref[r, :, LANES * i : LANES * (i + 1)] = carried[i]


def entry(p, keep, seg, x_own, g_own, hfv, hrv, start, waits):
    rows, slots, _, _ = p.shape
    tiles = slots // 3
    blocks = -(-REACH // BLOCK)
    length, count = blocks * SPACED, blocks * BLOCK
    return call(
        entry_kernel,
        [((rows, tiles, spaced(REACH), LANES), f32), ((rows, 1, tiles * LANES), f32)],
        (p, keep, seg, x_own, g_own, hfv, hrv, start),
        waits=waits,
        scratch=[((tiles, length, LANES), f32)] + [((tiles, count, LANES), f32)] * 2,
        name="entry",
    )


def backward_kernel(
    where_ref, p_ref, keep_ref, seg_ref, lead_ref, first_ref, x_ref, g_ref, hfv_ref, hrv_ref, carry_ref, vectors_ref,
    gp_ref, hidden_ref, high_ref, sums_ref, final_ref, means_ref,
    prev_ref, a_ref, b_ref, gg_ref, e_ref, omf_ref, dr_ref, d_ref,
):
    rows, slots = p_ref.shape[:2]
    tiles = slots // 3
    blocks = p_ref.shape[2] // SPACED
    hfv, hrv = tiles_of(hfv_ref, tiles), tiles_of(hrv_ref, tiles)
    devices, block = BLOCK // g_ref.shape[2], g_ref.shape[2]
    sums_ref[...] = jnp.zeros_like(sums_ref)
    for r in range(rows):
        prev_ref[...] = seg_ref[r]

        @pl.when(where_ref[0] == 0)
        def _():
            prev_ref[:, : spaced(LEAD), :] = lead_ref[r]

        @pl.when(where_ref[0] != 0)
        def _():
            prev_ref[:, : spaced(REACH), :] = first_ref[r]

        @pl.loop(0, blocks)
        def _(k):
            out = pl.ds(pl.multiple_of(k * BLOCK, BLOCK), BLOCK)
            for i in range(tiles):
                t = block_terms(p_ref, keep_ref, prev_ref, x_ref, g_ref, hfv, hrv, r, k, i)
                lanes = slice(LANES * i, LANES * (i + 1))
                for n in range(devices):
                    hidden_ref[k * devices + n, r, :, lanes] = t["hidden"][n * block : (n + 1) * block].astype(bf16)
                high_ref[r, i, out, :] = t["high"].astype(bf16)
                a_ref[i, out, :], b_ref[i, out, :] = composed(t["a"], t["b"])
                for ref, name in zip((gg_ref, e_ref, omf_ref, dr_ref), ("gg", "e", "omf", "dr")):
                    ref[i, out, :] = t[name]
                final_ref[r, :, lanes] = t["cell"][-1:]

        run_back(a_ref, b_ref, d_ref, tiles_of(carry_ref.at[r], tiles), blocks * BLOCK)

        @pl.loop(0, blocks)
        def _(k):
            at = pl.ds(pl.multiple_of(k * SPACED, 8), BLOCK)
            out = pl.ds(pl.multiple_of(k * BLOCK, BLOCK), BLOCK)
            first, second = jnp.zeros((BLOCK, LANES), f32), jnp.zeros((BLOCK, LANES), f32)
            for i in range(tiles):
                prev = prev_ref[i, at, :]
                u = entering(a_ref[i, out, :], b_ref[i, out, :], d_ref[i, out, :]) + gg_ref[i, out, :]
                df, dr = u * e_ref[i, out, :], dr_ref[i, out, :]
                dc = u * omf_ref[i, out, :]
                for m, value in enumerate((dc, df, dr)):
                    slot = m * tiles + i
                    lane = lax.rem(slot + slots - where_ref[4], slots) * LANES
                    gp_ref[r, out, pl.ds(pl.multiple_of(lane, LANES), LANES)] = value.astype(bf16)
                    first += value * vectors_ref[slot, 0:1, :]
                    second += value * ((1.0 if m == 0 else 2.0) * p_ref[r, slot, at, :] - vectors_ref[slot, 1:2, :])
                lanes = slice(LANES * i, LANES * (i + 1))
                for m, value in enumerate((df * prev, dr * prev, df, dr)):
                    sums_ref[m : m + 1, lanes] += jnp.sum(value, axis=0, keepdims=True)
                for m, value in enumerate((dc, df, dr)):
                    lane = lax.rem(m * tiles + i + slots - where_ref[4], slots) * LANES
                    at_lane = pl.ds(pl.multiple_of(lane, LANES), LANES)
                    sums_ref[7:8, at_lane] += jnp.sum(value, axis=0, keepdims=True)
            means_ref[r, 0, out, :] = first
            means_ref[r, 1, out, :] = second


def backward(where, p, keep, seg, lead, first, x_own, g_own, hfv, hrv, carry, vectors):
    rows, slots, length, _ = p.shape
    tiles = slots // 3
    tokens = length // SPACED * BLOCK
    width = tiles * LANES
    return call(
        backward_kernel,
        [
            ((rows, tokens, 3 * width), bf16),
            (g_own.shape, bf16),
            ((rows, tiles, tokens, LANES), bf16),
            ((8, 3 * width), f32),
            ((rows, 1, width), f32),
            ((rows, 2, tokens, LANES), f32),
        ],
        (p, keep, seg, lead, first, x_own, g_own, hfv, hrv, carry, vectors),
        (where,),
        scratch=[((tiles, length, LANES), f32)] + [((tiles, tokens, LANES), f32)] * 7,
        name="backward",
    )


def weight_back_kernel(normed_ref, gp_ref, sums_ref, *refs, part, group, cuts):
    count = sum(len(rows) for rows in cuts)
    w_refs, (by_feature_ref, *out_refs) = refs[: len(refs) - count - 1], refs[len(refs) - count - 1 :]
    total, _, features = normed_ref.shape
    row_block = features // 2 // group
    columns = out_refs[0].shape[2]
    span = 2 * LANES
    devices = span // row_block
    lane_tiles = gp_ref.shape[2] // LANES
    for k in range(group // devices):
        lane = slice(part * (features // 2) + k * span, part * (features // 2) + (k + 1) * span)
        p = sum(
            lax.dot_general(normed_ref[r, :, lane], gp_ref[r], (((0,), (0,)), ((), ())), preferred_element_type=f32)
            for r in range(total)
        )
        first = w_refs[0].shape[0]
        w = [w_refs[0][lane.start : min(lane.stop, first), :]] if lane.start < first else []
        if lane.stop > first:
            w.append(w_refs[1][max(lane.start - first, 0) : lane.stop - first, :])
        w = jnp.concatenate(w).astype(f32)
        for m, value in enumerate((p * w, w * sums_ref[7:8, :])):
            value = functools.reduce(jnp.add, [value[:, LANES * j : LANES * (j + 1)] for j in range(lane_tiles)])
            by_feature_ref[m : m + 1, k * span : (k + 1) * span] = jnp.sum(jnp.transpose(value), axis=0, keepdims=True)
        p = p.astype(bf16)
        outs = iter(out_refs)
        for split, rows in enumerate(cuts):
            start = 0
            for step in rows:
                out_ref = next(outs)
                for n in range(devices):
                    row = n * row_block + start
                    out_ref[k * devices + n, :step] = p[row : row + step, split * columns : (split + 1) * columns]
                    if out_ref.shape[1] > step:
                        out_ref[k * devices + n, step:] = jnp.zeros((out_ref.shape[1] - step, columns), bf16)
                start += step


def weight_back(normed, gp, sums, weights, part, group, cuts, waits, spare=0):
    features = normed.shape[2]
    columns = gp.shape[2] // len(cuts)
    kernel = functools.partial(weight_back_kernel, part=part, group=group, cuts=cuts)
    out_shape = [((2, features // 2), f32)] + [((group, step, columns), bf16) for rows in cuts for step in rows]
    (count, step, width), dtype = out_shape[-1]
    out_shape[-1] = ((count, step + spare, width), dtype)
    return call(kernel, out_shape, (normed, gp, sums, *weights), waits=waits, name="weight_back")


def norm_back_kernel(where_ref, stats_ref, means_ref, gp_ref, gain_ref, *refs, orders, with_hidden):
    count = len(orders[0])
    x_refs, refs = refs[: 2 * count], refs[2 * count :]
    *w_refs, high_ref, hidden_ref = refs[:-10]
    all_out_refs, (some_ref, gn_ref) = refs[-10:-2], refs[-2:]
    half_count, total, block, _ = all_out_refs[0].shape
    features = gain_ref.shape[1]
    half_width = features // 2
    together = gn_ref.shape[0] // block
    for odd in (1, 0):
        out_refs = all_out_refs[4 * (1 - odd) : 4 * (2 - odd)]
        for r in range(total):
            for d in range(0, count, together):
                tokens = []
                for n in range(together):
                    place = where_ref[3] ^ (orders[0][d + n] | odd)
                    tokens.append(pl.ds(pl.multiple_of(place * block, 16), block))
                    some_ref[n * block : (n + 1) * block, :] = gp_ref[r, tokens[n], :]
                lane = 0
                for w_ref in w_refs:
                    rows = w_ref.shape[0]
                    gn_ref[:, lane : lane + rows] = lax.dot_general(
                        some_ref[...], w_ref[...], (((1,), (1,)), ((), ())), preferred_element_type=f32
                    )
                    lane += rows
                for n in range(together):
                    x_ref = x_refs[orders[0][d + n] | odd]
                    mean, inv = stats_ref[r, 0, tokens[n], :], stats_ref[r, 1, tokens[n], :]
                    first, second = (
                        jnp.sum(means_ref[r, m, tokens[n], :], axis=-1, keepdims=True) * (1.0 / features)
                        for m in range(2)
                    )
                    slope = inv * inv * second
                    rest = inv * first - slope * mean
                    for part in range(2):
                        at_d = orders[part].index(orders[0][d + n])
                        out_ref = out_refs[2 * part + at_d // half_count]
                        start = pl.multiple_of((where_ref[0] ^ part) * half_width, LANES)
                        if with_hidden:
                            high = high_ref[r, where_ref[0] ^ part, tokens[n], :].astype(f32)
                        for j in range(half_width // LANES):
                            at = slice(part * half_width + LANES * j, part * half_width + LANES * (j + 1))
                            value = inv * (gn_ref[n * block : (n + 1) * block, at] * gain_ref[:, at])
                            x = x_ref[r, :block, pl.ds(start + LANES * j, LANES)].astype(f32)
                            value -= slope * x + rest
                            if with_hidden:
                                value += jnp.where(where_ref[3] == j, high, 0.0)
                            out_ref[at_d % half_count, r, :, LANES * j : LANES * (j + 1)] = value.astype(bf16)
                        if with_hidden:
                            hidden = hidden_ref[where_ref[3] ^ (orders[0][d + n] | odd), r]
                            out_ref[at_d % half_count, r, :, half_width:] = hidden[:, LANES * part : LANES * (part + 1)]


def norm_back(where, blocks, orders, stats, means, gp, weights, gain, high, hidden, with_hidden, waits):
    rows, block, features = blocks[0].shape
    block -= STATS
    together = 2 * LANES // block
    out = call(
        functools.partial(norm_back_kernel, orders=orders, with_hidden=with_hidden),
        [((len(blocks) // 4, rows, block, features // 2 + with_hidden * LANES), bf16)] * 8,
        (stats, means, gp, gain, *blocks, *weights, high, hidden), (where,), waits,
        scratch=[((together * block, gp.shape[2]), bf16), ((together * block, features), f32)],
        name="norm_back",
    )
    return out[:4], out[4:]


def totals_kernel(where_ref, sums_ref, own_ref, other_ref, gain_ref, shift_ref, out_ref, *, chunk):
    half_width = own_ref.shape[1]
    out_ref[...] = jnp.zeros_like(out_ref)
    for i in range(2):
        lane = pl.ds(pl.multiple_of(i * chunk + where_ref[3] * LANES, LANES), LANES)
        out_ref[0:4, lane] = sums_ref[0:4, LANES * i : LANES * (i + 1)]
    for part, ref in enumerate((own_ref, other_ref)):
        lane = pl.ds(pl.multiple_of((where_ref[0] ^ part) * half_width, LANES), half_width)
        at = slice(part * half_width, (part + 1) * half_width)
        out_ref[4:5, lane] = (ref[0:1, :] - shift_ref[:, at] * ref[1:2, :]) / gain_ref[:, at]
        out_ref[5:6, lane] = ref[1:2, :]


def bf16_parts(row):
    rows = []
    for _ in range(3):
        upper = lax.reduce_precision(row, 8, 7)
        rows.append(upper.astype(bf16))
        row = row - upper
    return rows


def local(inputs, weight, gain, shift, forget_vec, reset_vec, forget_bias, reset_bias, initial, resets, grad_out):
    rows, block_len, features = inputs.shape
    row_block, columns_here = weight.shape
    sections = lax.axis_size("fsdp")
    ranks = lax.axis_size("dp")
    group = sections // 2
    tokens = group * block_len
    index = lax.axis_index("fsdp")
    half, place = index // group, index % group
    rank = lax.axis_index("dp")
    first_half = half == 0
    groups = [list(range(group)), list(range(group, sections))]
    chunk = math.gcd(features, columns_here)
    chunks, piece = features // chunk, chunk // group
    width = chunks * piece
    tiles = width // LANES
    slots = 3 * tiles
    parts = columns_here // chunk
    columns = parts * piece
    aligned = piece == LANES and chunks == 2
    paired = ranks == 2 and aligned
    turn = rank * (columns // LANES) if paired else jnp.zeros_like(rank)
    where = jnp.stack([half, rank, index % 2, place, turn]).astype(jnp.int32)
    bits = [1 << b for b in range(1, group.bit_length() - 1)]
    ways = (bits[::-1], bits)
    orders = []
    for way in ways:
        order = [0]
        for bit in way:
            order += [d | bit for d in order]
        orders.append(order)

    def across(value):
        return lax.ppermute(value, "fsdp", [(j, (j + group) % sections) for j in range(sections)])

    def flipped(value, bit):
        return lax.ppermute(value, "fsdp", [(j, j ^ bit) for j in range(sections)])

    def swapped(value):
        return lax.ppermute(value, "dp", [(0, 1), (1, 0)])

    def shared(value):
        return lax.all_to_all(value, "fsdp", 0, 0, tiled=True, axis_index_groups=groups)

    def own(vector):
        return lax.dynamic_index_in_dim(vector.reshape(-1, chunks, group, piece), place, 2, False).reshape(-1, width)

    def halves_turned(vector):
        low, high = vector[..., : features // 2], vector[..., features // 2 :]
        return jnp.concatenate([jnp.where(first_half, low, high), jnp.where(first_half, high, low)], axis=-1)

    def dealt(value, waits=()):
        if aligned:
            return deal(value, group, waits)
        n, wide = value.shape
        return value.reshape(n, wide // chunk, group, piece).transpose(2, 0, 1, 3).reshape(group, n, wide // group)

    def collected(pieces, dtype, waits=()):
        if aligned:
            return collect(pieces, dtype, waits)
        wide = pieces[0].shape[2]
        back = lambda v: v.reshape(group, -1, wide // piece, piece).transpose(1, 2, 0, 3).reshape(-1, wide * group)
        return jnp.concatenate([back(v) for v in pieces]).astype(dtype)

    mine = shared(dealt(weight))
    theirs = across(mine)
    beside = swapped(mine) if paired else mine
    blocks = {0: stats(inputs, (1 - resets).astype(f32)[:, None, :], ())}
    for bit in bits[::-1]:
        blocks |= {d | bit: flipped(fence(value, (beside,)) if d else value, bit) for d, value in blocks.items()}
    blocks = {d: fence(value, (theirs, beside)) for d, value in blocks.items()}
    blocks |= {d | 1: flipped(value, 1) for d, value in blocks.items()}
    blocks = [blocks[d] for d in range(group)]
    early_rows = features // 2
    if paired:
        early, late = [mine, beside], [theirs, swapped(theirs)]
    else:
        early, late = (
            [lax.all_gather(v.reshape(-1, columns), "dp", axis=1, tiled=True)] for v in (mine, theirs)
        )
    hfv, hrv = 0.5 * own(forget_vec), 0.5 * own(reset_vec)
    bias = jnp.concatenate([jnp.zeros((1, width), f32), own(forget_bias), own(reset_bias)]).reshape(-1, 1, LANES)
    gain_row, shift_row = halves_turned(gain)[None], halves_turned(shift)[None]
    vector_rows = [*bf16_parts(gain_row), *bf16_parts(shift_row)]
    vector_rows = jnp.pad(jnp.concatenate(vector_rows), ((0, 10), (0, 0)))
    g_own = shared(dealt(grad_out.reshape(-1, features)).reshape(group, rows, block_len, width))
    normed, token_stats, keep, *x_own = norm(where, blocks, gain_row, shift_row, aligned, (g_own,))
    if aligned:
        x_own = x_own[0]
    else:
        in_order = jnp.stack(blocks)[place ^ jnp.arange(group)][:, :, :block_len].swapaxes(0, 1)
        x_own = own(in_order.reshape(rows * tokens, features)).reshape(rows, tokens, tiles, LANES).swapaxes(1, 2)
    some, some_vectors, early_weight = project(where, normed, vector_rows, early, early_rows, slots)
    p, seg, lead, end, lead_end, vectors, late_weight = blocks_forward(
        where, normed, vector_rows, some, some_vectors, bias, keep, hfv, own(initial)[:, None, :], late,
        features - early_rows,
    )
    weights = (early_weight, late_weight)
    start = across(end)
    lead = lead_forward(p, keep, hfv, lead_end, lead)
    first, back = entry(p, keep, seg, x_own, g_own, hfv, hrv, start, ())
    carry = jnp.where(first_half, across(back), 0.0)
    gp, hidden_own, high_own, sums, final, means = backward(
        where, p, keep, seg, lead, first, x_own, g_own, hfv, hrv, carry, vectors
    )

    mask = (jnp.arange(group) == place)[:, None]

    splits = 2 if paired else 1
    by_feature_other, *away = weight_back(normed, gp, sums, weights, 1, group, [(row_block,)] * splits, (), SPARE * paired)
    away_got = swapped(away[1]) if paired else None

    sent, kept = norm_back(
        where, blocks, orders, token_stats, means, gp, weights, gain_row, high_own, hidden_own, aligned,
        (by_feature_other,),
    )
    if not aligned:
        spread = high_own.swapaxes(1, 2).reshape(rows, group, block_len, chunks, 1, piece).swapaxes(0, 1)
        spread = jnp.where(mask, spread.astype(f32), 0.0).reshape(group, rows, block_len, features)
        spread = halves_turned(spread)[place ^ jnp.arange(group)]
        halves = (spread[..., : features // 2], spread[..., features // 2 :])
        n = group // 4

        def with_high(arrays, odd):
            add = [half[d | odd] for half, order in zip(halves, orders) for d in order]
            return [(v.astype(f32) + jnp.stack(add[i * n : (i + 1) * n])).astype(bf16) for i, v in enumerate(arrays)]

        sent, kept = with_high(sent, 1), with_high(kept, 0)
    got = [flipped(value, 1) for value in sent]
    if paired:
        away = added(away[0], away_got, kept[:1])
    else:
        away = lax.psum_scatter(away[0], "dp", scatter_dimension=2, tiled=True)
    z_got = across(away)
    kept, sent = halve(kept, got, features // 2)
    bit_pairs = list(zip(*(w[::-1] for w in ways)))
    got = [flipped(value, bit) for value, bit in zip(sent, bit_pairs.pop(0))]
    cuts = [(row_block,), (row_block // 2,) * 2][:splits]
    by_feature_own, *here = weight_back(normed, gp, sums, weights, 0, group, cuts, (away,))
    if paired:
        here_got = [swapped(value) for value in here[1:]]
    else:
        here = lax.psum_scatter(here[0], "dp", scatter_dimension=2, tiled=True)
    if aligned:
        totals = call(
            functools.partial(totals_kernel, chunk=chunk), [((8, features), f32)],
            (sums, by_feature_own, by_feature_other, gain_row, shift_row), (where,), name="totals",
        )[0]
    else:
        spread = jnp.where(mask, sums[:4, :width].reshape(4, chunks, 1, piece), 0.0).reshape(4, features)
        product, shift_sum = jnp.concatenate([by_feature_own, by_feature_other], axis=1)
        gain_sum = (product - shift_row[0] * shift_sum) / gain_row[0]
        totals = jnp.concatenate([spread, halves_turned(jnp.stack([gain_sum, shift_sum]))], axis=0)
    for way in bit_pairs:
        kept, sent = halve(kept, got, features // 2)
        got = [flipped(value, bit) for value, bit in zip(sent, way)]
    sources = []
    for way in ways:
        sources.append([0])
        for bit in (1, *way[::-1]):
            sources[-1] += [d | bit for d in sources[-1]]
    grad_inputs, *hidden = finish(where, kept, got, features, sources)
    if aligned:
        hidden = hidden[0]
    else:
        hidden = collected([shared(hidden_own).reshape(group, -1, width)], bf16).reshape(rows, block_len, features)
    for bit in [1 << b for b in range(group.bit_length() - 1)]:
        totals = added(totals, flipped(totals, bit))
    waits = (*got, totals)
    value = merge(here[0], here_got, z_got, waits) if paired else added(here, z_got, waits)
    grad_weight = collected([shared(value)], f32)
    totals = added(totals, swapped(totals)) if ranks == 2 else lax.psum(totals, "dp")
    totals = added(totals, across(totals), (grad_inputs,))

    own_width = features // sections
    if piece == own_width and chunks == 2:
        final = final[:, 0]
        low_part = lax.ppermute(final[:, :piece], "fsdp", [(j + group, j) for j in range(group)])
        final_state = jnp.where(first_half, low_part, final[:, piece:])
    else:
        spread = jnp.where(mask, final.reshape(rows, chunks, 1, piece), 0.0).reshape(rows, features)
        spread = lax.psum(jnp.where(first_half, 0.0, spread), "fsdp")
        final_state = lax.dynamic_slice_in_dim(spread, index * own_width, own_width, 1)

    return (hidden, grad_inputs, final_state, grad_weight, *[totals[i] for i in range(6)])


def solution(mesh):
    in_specs = (
        P("dp", "fsdp", None), P("fsdp", "dp"), P(), P(), P(), P(), P(), P(),
        P("dp", None), P("dp", "fsdp"), P("dp", "fsdp", None),
    )
    out_specs = (
        P("dp", "fsdp", None), P("dp", "fsdp", None), P("dp", "fsdp"), P("fsdp", "dp"), P(), P(), P(), P(), P(), P(),
    )
    return jax.shard_map(local, mesh=mesh, in_specs=in_specs, out_specs=out_specs, check_vma=False)
```

```python
import functools
import math

import jax
import jax.numpy as jnp
from jax import lax
from jax.experimental import pallas as pl
from jax.experimental.pallas import tpu as pltpu
from jax.sharding import PartitionSpec as P

SENT = 128
LEAD = 768
REACH = 192
EPSILON = 1e-05
LANES = 128
BLOCK = 128
SPACED = 136
EARLY = REACH - BLOCK
COVERED = EARLY + 2 * BLOCK
STATS = 16
SPARE = 16
UNROLL = 16
TOGETHER = 8
f32 = jnp.float32
bf16 = jnp.bfloat16


def spaced(token):
    return token + (SPACED - BLOCK) * (token // BLOCK)


def tiles_of(ref, count):
    return [ref[:, LANES * i : LANES * (i + 1)] for i in range(count)]


def call(kernel, out_shape, operands, scalars=(), waits=(), scratch=(), mebibytes=14, name=None):
    in_vmem, in_smem = pl.BlockSpec(memory_space=pltpu.VMEM), pl.BlockSpec(memory_space=pltpu.SMEM)
    before = len(scalars) + len(operands)

    def body(*refs):
        kernel(*refs[:before], *refs[before + len(waits) :])

    return pl.pallas_call(
        body,
        in_specs=[in_smem] * len(scalars) + [in_vmem] * len(operands) + [pl.BlockSpec(memory_space=pl.ANY)] * len(waits),
        out_specs=[in_vmem] * len(out_shape),
        out_shape=[jax.ShapeDtypeStruct(*shape) for shape in out_shape],
        scratch_shapes=[pltpu.VMEM(*shape) for shape in scratch],
        compiler_params=pltpu.CompilerParams(vmem_limit_bytes=mebibytes << 20),
        name=name,
    )(*scalars, *operands, *waits)


def fence(value, waits):
    return pl.pallas_call(
        lambda *refs: None,
        in_specs=[pl.BlockSpec(memory_space=pl.ANY)] * (1 + len(waits)),
        out_specs=pl.BlockSpec(memory_space=pl.ANY),
        out_shape=jax.ShapeDtypeStruct(value.shape, value.dtype),
        input_output_aliases={0: 0},
        name="fence",
    )(value, *waits)


def deal_kernel(in_ref, out_ref, *, chunks):
    group = out_ref.shape[0]
    for q in range(group):
        for c in range(chunks):
            lane = (c * group + q) * LANES
            out_ref[q, :, LANES * c : LANES * (c + 1)] = in_ref[:, lane : lane + LANES]


def deal(value, group, waits=()):
    n, features = value.shape
    kernel = functools.partial(deal_kernel, chunks=features // group // LANES)
    return call(kernel, [((group, n, features // group), value.dtype)], (value,), waits=waits, name="deal")[0]


def collect_kernel(*refs):
    *in_refs, out_ref = refs
    row = 0
    for ref in in_refs:
        group, n, width = ref.shape
        for q in range(group):
            for c in range(width // LANES):
                lane = (c * group + q) * LANES
                value = ref[q, :, LANES * c : LANES * (c + 1)]
                out_ref[row : row + n, lane : lane + LANES] = value.astype(out_ref.dtype)
        row += n


def collect(pieces, dtype, waits=()):
    group, _, width = pieces[0].shape
    shape = (sum(value.shape[1] for value in pieces), group * width)
    return call(collect_kernel, [(shape, dtype)], pieces, waits=waits, name="collect")[0]


def add_kernel(a_ref, b_ref, out_ref):
    b = b_ref[...] if b_ref.shape == a_ref.shape else b_ref[:, : a_ref.shape[1]]
    out_ref[...] = (a_ref[...].astype(f32) + b.astype(f32)).astype(out_ref.dtype)


def added(a, b, waits=()):
    return call(add_kernel, [(a.shape, a.dtype)], (a, b), waits=waits, name="added")[0]


def blocks_of(refs):
    return [ref.at[i] for ref in refs for i in range(ref.shape[0])]


def halve_kernel(*refs, width):
    *in_refs, first_stays, first_goes, second_stays, second_goes = refs
    n = len(in_refs) // 4
    parts = [blocks_of(in_refs[n * i : n * (i + 1)]) for i in range(4)]
    for part, (stays, goes) in enumerate(((first_stays, first_goes), (second_stays, second_goes))):
        out = blocks_of([stays, goes])
        for out_ref, a_ref, b_ref in zip(out, parts[part], parts[2 + part]):
            out_ref[:, :, :width] = (a_ref[:, :, :width].astype(f32) + b_ref[:, :, :width].astype(f32)).astype(bf16)
            there = a_ref.shape[2]
            if there > width:
                out_ref[:, :, width:there] = a_ref[:, :, width:]
                out_ref[:, :, there:] = b_ref[:, :, width:]


def halve(kept, got, width, waits=()):
    n = sum(value.shape[0] for value in kept) // 4
    *shape, there = kept[0].shape[1:]
    out = call(
        functools.partial(halve_kernel, width=width), [((n, *shape, 2 * there - width), bf16)] * 4, (*kept, *got),
        waits=waits, name="halve",
    )
    return out[0::2], out[1::2]


def merge_kernel(own_ref, away_ref, *refs):
    *got_refs, out_ref = refs
    start = 0
    for ref in got_refs:
        rows = slice(start, start + ref.shape[1])
        value = own_ref[:, rows, :].astype(f32) + ref[...].astype(f32) + away_ref[:, rows, :].astype(f32)
        out_ref[:, rows, :] = value.astype(bf16)
        start = rows.stop


def merge(own, got, away, waits=()):
    return call(merge_kernel, [(own.shape, bf16)], (own, away, *got), waits=waits, name="merge")[0]


def finish_kernel(where_ref, *refs, sources):
    in_refs, (out_ref, *hidden_ref) = refs[:4], refs[4:]
    half_width = out_ref.shape[2] // 2
    for part in range(2):
        kept_ref, got_ref = in_refs[part], in_refs[2 + part]
        value = kept_ref[0, :, :, :half_width].astype(f32) + got_ref[0, :, :, :half_width].astype(f32)
        lane = pl.multiple_of((where_ref[0] ^ part) * half_width, LANES)
        out_ref[:, :, pl.ds(lane, half_width)] = value.astype(bf16)
        if hidden_ref:
            tiles = [ref[0, :, :, at : at + LANES] for ref in (kept_ref, got_ref) for at in range(half_width, ref.shape[3], LANES)]
            for value, source in zip(tiles, sources[part]):
                lane = pl.multiple_of(part * half_width + (where_ref[3] ^ source) * LANES, LANES)
                hidden_ref[0][:, :, pl.ds(lane, LANES)] = value


def finish(where, kept, got, features, sources, waits=()):
    _, rows, block, there = kept[0].shape
    out_shape = [((rows, block, features), bf16)] * (1 + (there > features // 2))
    kernel = functools.partial(finish_kernel, sources=sources)
    return call(kernel, out_shape, (*kept, *got), (where,), waits, name="finish")


def stats_kernel(x_ref, keep_ref, out_ref):
    total, block, features = x_ref.shape

    def row(column):
        return jnp.transpose(jnp.broadcast_to(column, (block, LANES)))[0:1, :]

    for r in range(total):
        out_ref[r, :block, :] = x_ref[r]
        x = x_ref[r].astype(f32)
        mean = jnp.sum(x, axis=-1, keepdims=True) * (1.0 / features)
        centred = x - mean
        inv = lax.rsqrt(jnp.sum(centred * centred, axis=-1, keepdims=True) * (1.0 / features) + EPSILON)
        rows = [keep_ref[r]]
        for value in (row(mean), row(inv)):
            for _ in range(3):
                upper = value.astype(bf16).astype(f32)
                rows.append(upper)
                value = value - upper
        rows = jnp.concatenate(rows + [jnp.zeros_like(rows[0])] * (STATS - len(rows)), axis=0)
        if block < LANES:
            rows = jnp.concatenate([rows, jnp.zeros((STATS, LANES - block), f32)], axis=1)
        out_ref[r, block:, :LANES] = rows.astype(bf16)
        out_ref[r, block:, LANES:] = jnp.zeros((STATS, features - LANES), bf16)


def stats(inputs, keep, waits):
    rows, block, features = inputs.shape
    return call(stats_kernel, [((rows, block + STATS, features), bf16)], (inputs, keep), waits=waits, name="stats")[0]


def norm_kernel(where_ref, gain_ref, shift_ref, *refs, count):
    block_refs, (normed_ref, stats_ref, keep_ref, *own_refs) = refs[:count], refs[count:]
    total, block, features = block_refs[0].shape
    block -= STATS
    half_width = features // 2
    per_block = BLOCK // block

    def device(r, x_ref, q):
        at = pl.ds(pl.multiple_of(q * block, block), block)
        spaced_at = pl.ds(pl.multiple_of(q // per_block * SPACED + q % per_block * block, 8), block)
        rows = x_ref[r, block:, :block].astype(f32)

        def column(*of):
            row = functools.reduce(jnp.add, [rows[k : k + 1, :] for k in of])
            return jnp.transpose(jnp.broadcast_to(row, (LANES, block)))

        keep_ref[r, spaced_at, :] = column(0)
        mean, inv = column(1, 2, 3), column(4, 5, 6)
        stats_ref[r, 0, at, :] = mean
        stats_ref[r, 1, at, :] = inv
        for part in range(2):
            lane = pl.multiple_of((where_ref[0] ^ part) * half_width, LANES)
            for j in range(half_width // LANES):
                x = x_ref[r, :block, pl.ds(lane + j * LANES, LANES)].astype(f32)
                out = slice(part * half_width + j * LANES, part * half_width + (j + 1) * LANES)
                normed_ref[r, at, out] = ((x - mean) * inv * gain_ref[:, out] + shift_ref[:, out]).astype(bf16)
        for ref in own_refs:
            for i in range(2):
                lane = pl.ds(pl.multiple_of(i * half_width + where_ref[3] * LANES, LANES), LANES)
                ref[r, i, at, :] = x_ref[r, :block, lane]

    for r in range(total):
        for d, ref in enumerate(block_refs):
            device(r, ref, where_ref[3] ^ d)


def norm(where, blocks, gain, shift, aligned, waits):
    rows, block, features = blocks[0].shape
    tokens = len(blocks) * (block - STATS)
    out_shape = [
        ((rows, tokens, features), bf16),
        ((rows, 2, tokens, LANES), f32),
        ((rows, tokens // BLOCK * SPACED, LANES), f32),
    ]
    if aligned:
        out_shape.append(((rows, 2, tokens, LANES), bf16))
    kernel = functools.partial(norm_kernel, count=len(blocks))
    return call(kernel, out_shape, (gain, shift, *blocks), (where,), waits, name="norm")


def weight_into(w_ref, parts):
    if len(parts) == 1:
        w_ref[...] = parts[0][...]
        return
    pieces = len(parts) // 2
    group, _, columns = parts[0].shape
    block = sum(part.shape[1] for part in parts[:pieces])
    for rank in range(2):
        start = 0
        for part in parts[rank * pieces : (rank + 1) * pieces]:
            rows = part.shape[1]
            for q in range(group):
                row = q * block + start
                w_ref[row : row + rows, rank * columns : (rank + 1) * columns] = part[q]
            start += rows


def slot_of(where_ref, s, slots):
    return lax.rem(where_ref[4] + s, slots)


def project_kernel(where_ref, normed_ref, rows_ref, *refs):
    *parts, sum_ref, vectors_ref, w_ref = refs
    weight_into(w_ref, parts)
    depth = w_ref.shape[0]
    total, slots = sum_ref.shape[:2]
    step = 2 * BLOCK
    vectors_ref[...] = jnp.dot(rows_ref[:, :depth], w_ref[...], preferred_element_type=f32)
    for r in range(total):

        @pl.loop(0, normed_ref.shape[1] // step)
        def _(j):
            at = pl.ds(pl.multiple_of(j * step, step), step)
            p = jnp.dot(normed_ref[r, at, :depth], w_ref[...], preferred_element_type=f32)
            for s in range(slots):
                sum_ref[r, s, at, :] = p[:, LANES * s : LANES * (s + 1)]


def project(where, normed, vector_rows, parts, depth, slots):
    rows, tokens, _ = normed.shape
    out_shape = [
        ((rows, slots, tokens, LANES), f32), ((vector_rows.shape[0], slots * LANES), f32), ((depth, slots * LANES), bf16),
    ]
    return call(project_kernel, out_shape, (normed, vector_rows, *parts), (where,), name="project")


def blocks_kernel(where_ref, normed_ref, rows_ref, sum_ref, some_ref, bias_ref, keep_ref, hfv_ref, init_ref, *refs):
    *parts, p_ref, seg_ref, lead_ref, end_ref, lead_end_ref, vectors_ref, w_ref = refs
    weight_into(w_ref, parts)
    depth = w_ref.shape[0]
    total, slots = p_ref.shape[:2]
    tiles = slots // 3
    step = 2 * BLOCK
    features = normed_ref.shape[2]
    by_column = some_ref[...] + jnp.dot(rows_ref[:, features - depth :], w_ref[...], preferred_element_type=f32)
    for s in range(slots):
        slot = slot_of(where_ref, s, slots)
        lanes = slice(LANES * s, LANES * (s + 1))
        vectors_ref[slot, 0:1, :] = jnp.sum(by_column[0:3, lanes], axis=0, keepdims=True)
        vectors_ref[slot, 1:2, :] = jnp.sum(by_column[3:6, lanes], axis=0, keepdims=True) + bias_ref[slot]
    for r in range(total):

        @pl.loop(0, normed_ref.shape[1] // step)
        def _(j):
            at = pl.ds(pl.multiple_of(j * step, step), step)
            p = jnp.dot(normed_ref[r, at, features - depth :], w_ref[...], preferred_element_type=f32)
            for s in range(slots):
                slot = slot_of(where_ref, s, slots)
                scale = jnp.where(slot < tiles, 1.0, 0.5)
                value = scale * (p[:, LANES * s : LANES * (s + 1)] + sum_ref[r, s, at, :] + bias_ref[slot])
                for k in range(2):
                    to = pl.ds(pl.multiple_of((2 * j + k) * SPACED, 8), BLOCK)
                    p_ref[r, slot, to, :] = value[BLOCK * k : BLOCK * (k + 1)]

        row_blocks(
            p_ref.at[r], keep_ref.at[r], hfv_ref, init_ref.at[r], seg_ref.at[r], lead_ref.at[r], end_ref.at[r],
            lead_end_ref.at[r],
        )


def blocks_forward(where, normed, vector_rows, some, some_vectors, bias, keep, hfv, init, parts, depth):
    rows, tokens, _ = normed.shape
    slots = bias.shape[0]
    tiles = slots // 3
    state = ((rows, 1, tiles * LANES), f32)
    length = tokens // BLOCK * SPACED
    out_shape = [
        ((rows, slots, length, LANES), f32), ((rows, tiles, length, LANES), f32),
        ((rows, tiles, spaced(COVERED), LANES), f32), state, state, ((slots, 2, LANES), f32), ((depth, slots * LANES), bf16),
    ]
    return call(
        blocks_kernel, out_shape, (normed, vector_rows, some, some_vectors, bias, keep, hfv, init, *parts), (where,),
        name="blocks_forward",
    )


def chain_step(p_ref, kb_ref, prev_ref, hfv, carried, row, next_row):
    tiles = len(hfv)
    keep = kb_ref[next_row, :]
    out = []
    for i, (y, prev) in enumerate(carried):
        tau = jnp.tanh(y)
        half = 0.5 * p_ref[i, row, :]
        mid, gap = 0.5 * prev + half, 0.5 * prev - half
        prev_ref[i, row, :] = prev
        reach = hfv[i] * keep
        out.append(
            ((p_ref[tiles + i, next_row, :] + reach * mid) + (reach * gap) * tau, (keep * mid) + (keep * gap) * tau)
        )
    return out


def begin(p_ref, hfv, previous, row):
    return [(p_ref[len(hfv) + i, row, :] + hfv[i] * prev, prev) for i, prev in enumerate(previous)]


def rows_of(token):
    return pl.ds(spaced(token), 1)


def run_chain(p_ref, kb_ref, prev_ref, hfv, carried, first, count):
    def body(j, now):
        for u in range(UNROLL):
            token = first + j * UNROLL + u
            now = chain_step(p_ref, kb_ref, prev_ref, hfv, now, rows_of(token), rows_of(token + 1))
        return now

    return lax.fori_loop(0, count // UNROLL, body, carried)


def row_blocks(p_ref, kb_ref, hfv_ref, init_ref, seg_ref, lead_ref, end_ref, lead_end_ref):
    tiles = seg_ref.shape[0]
    blocks = p_ref.shape[1] // SPACED
    hfv = tiles_of(hfv_ref, tiles)

    def seg_step(cells, step, store):
        row = pl.ds(step, blocks, stride=SPACED)
        keep = kb_ref[row, :]
        out = []
        for i, cell in enumerate(cells):
            prev = keep * cell
            tau = jnp.tanh(p_ref[tiles + i, row, :] + (hfv[i] * keep) * cell)
            half = 0.5 * p_ref[i, row, :]
            if store:
                seg_ref[i, row, :] = prev
            out.append((0.5 * prev + half) + (0.5 * prev - half) * tau)
        return out

    def run(cells, lead, first, token, count, store):
        def body(j, carried):
            cells, lead = carried
            for u in range(UNROLL):
                at = j * UNROLL + u
                cells = seg_step(cells, first + at, store)
                lead = chain_step(p_ref, kb_ref, lead_ref, hfv, lead, rows_of(token + at), rows_of(token + at + 1))
            return cells, lead

        return lax.fori_loop(0, count // UNROLL, body, (cells, lead))

    def moved(cells):
        return [jnp.concatenate([jnp.zeros((1, LANES), f32), cell[:-1]], axis=0) for cell in cells]

    cells = [jnp.zeros((blocks, LANES), f32) for _ in range(tiles)]
    lead = begin(p_ref, hfv, [kb_ref[0:1, :] * v for v in tiles_of(init_ref, tiles)], pl.ds(0, 1))
    cells, lead = run(cells, lead, BLOCK - EARLY, 0, EARLY, False)
    cells, lead = run(moved(cells), lead, 0, EARLY, BLOCK, False)
    cells, lead = run(moved(cells), lead, 0, EARLY + BLOCK, BLOCK, True)
    for i in range(tiles):
        end_ref[:, LANES * i : LANES * (i + 1)] = cells[i][-1:]
        lead_end_ref[:, LANES * i : LANES * (i + 1)] = lead[i][1]


def lead_kernel(p_ref, keep_ref, hfv_ref, start_ref, early_ref, lead_ref):
    rows, tiles = lead_ref.shape[:2]
    hfv = tiles_of(hfv_ref, tiles)
    lead_ref[:, :, : spaced(COVERED), :] = early_ref[...]
    for r in range(rows):
        carried = begin(p_ref.at[r], hfv, tiles_of(start_ref.at[r], tiles), rows_of(COVERED))
        run_chain(p_ref.at[r], keep_ref.at[r], lead_ref.at[r], hfv, carried, COVERED, LEAD - COVERED)


def lead_forward(p, keep, hfv, start, early):
    rows, tiles = early.shape[:2]
    out_shape = [((rows, tiles, spaced(LEAD), LANES), f32)]
    return call(lead_kernel, out_shape, (p, keep, hfv, start, early), name="lead_forward")[0]


def token_terms(prev, c, yf, yr, x, g, keep, hfv, hrv):
    tau_f = jnp.tanh(yf + hfv * prev)
    tau_r = jnp.tanh(yr + hrv * prev)
    f, omf, gate, omg = 0.5 + 0.5 * tau_f, 0.5 - 0.5 * tau_f, 0.5 + 0.5 * tau_r, 0.5 - 0.5 * tau_r
    cell = f * prev + omf * c
    gg = g * gate
    dr = gg * omg * (cell - x)
    e = (prev - c) * f * omf
    slope = f + e * (2.0 * hfv)
    return dict(
        cell=cell, hidden=gate * cell + omg * x, high=g * omg, gg=gg, dr=dr, e=e, omf=omf,
        a=keep * slope, b=keep * (slope * gg + dr * (2.0 * hrv)),
    )


def block_terms(p_ref, keep_ref, prev_ref, x_ref, g_ref, hfv, hrv, r, k, i):
    tiles = len(hfv)
    at = pl.ds(pl.multiple_of(k * SPACED, 8), BLOCK)
    devices = BLOCK // g_ref.shape[2]
    lanes = slice(LANES * i, LANES * (i + 1))
    g = jnp.concatenate([g_ref[k * devices + n, r, :, lanes].astype(f32) for n in range(devices)], axis=0)
    x = x_ref[r, i, pl.ds(pl.multiple_of(k * BLOCK, BLOCK), BLOCK), :].astype(f32)
    c, yf, yr = (p_ref[r, m * tiles + i, at, :] for m in range(3))
    return token_terms(prev_ref[i, at, :], c, yf, yr, x, g, keep_ref[r, at, :], hfv[i], hrv[i])


def composed(a, b):
    p, q = (value.reshape(-1, TOGETHER, LANES) for value in (a, b))
    row = lax.broadcasted_iota(jnp.int32, p.shape, 1)
    step = 1
    while step < TOGETHER:
        there = row < TOGETHER - step
        q += jnp.where(there, p * pltpu.roll(q, TOGETHER - step, 1), 0.0)
        p *= jnp.where(there, pltpu.roll(p, TOGETHER - step, 1), 1.0)
        step *= 2
    return p.reshape(a.shape), q.reshape(a.shape)


def entering(p, q, d):
    left = pltpu.roll((p * d + q).reshape(-1, TOGETHER, LANES), TOGETHER - 1, 1)
    row = lax.broadcasted_iota(jnp.int32, left.shape, 1)
    return jnp.where(row < TOGETHER - 1, left, d.reshape(left.shape)).reshape(d.shape)


def run_back(p_ref, q_ref, d_ref, carried, count):
    carried = [jnp.broadcast_to(d, (TOGETHER, LANES)) for d in carried]

    def body(j, carried):
        base = pl.multiple_of(count - UNROLL * TOGETHER * (j + 1), UNROLL * TOGETHER)
        for u in reversed(range(UNROLL)):
            at = base + u * TOGETHER
            now = []
            for i, d in enumerate(carried):
                if d_ref is not None:
                    d_ref[i, pl.ds(at, TOGETHER), :] = d
                now.append(p_ref[i, pl.ds(at, 1), :] * d + q_ref[i, pl.ds(at, 1), :])
            carried = now
        return carried

    carried = lax.fori_loop(0, count // (UNROLL * TOGETHER), body, carried)
    return [d[0:1] for d in carried]


def entry_kernel(
    p_ref, keep_ref, seg_ref, x_ref, g_ref, hfv_ref, hrv_ref, start_ref, first_ref, back_ref, prev_ref, a_ref, b_ref
):
    rows, slots = p_ref.shape[:2]
    tiles = slots // 3
    hfv, hrv = tiles_of(hfv_ref, tiles), tiles_of(hrv_ref, tiles)
    blocks = -(-REACH // BLOCK)
    for r in range(rows):
        prev_ref[...] = seg_ref[r, :, : blocks * SPACED, :]
        start = [keep_ref[r, 0:1, :] * v for v in tiles_of(start_ref.at[r], tiles)]
        run_chain(p_ref.at[r], keep_ref.at[r], prev_ref, hfv, begin(p_ref.at[r], hfv, start, pl.ds(0, 1)), 0, REACH)
        first_ref[r] = prev_ref[:, : spaced(REACH), :]
        for k in range(blocks):
            for i in range(tiles):
                t = block_terms(p_ref, keep_ref, prev_ref, x_ref, g_ref, hfv, hrv, r, k, i)
                rows_here = slice(BLOCK * k, BLOCK * (k + 1))
                a_ref[i, rows_here, :], b_ref[i, rows_here, :] = composed(t["a"], t["b"])
        carried = run_back(a_ref, b_ref, None, [jnp.zeros((1, LANES), f32)] * tiles, blocks * BLOCK)
        for i in range(tiles):
            back_ref[r, :, LANES * i : LANES * (i + 1)] = carried[i]


def entry(p, keep, seg, x_own, g_own, hfv, hrv, start, waits):
    rows, slots, _, _ = p.shape
    tiles = slots // 3
    blocks = -(-REACH // BLOCK)
    length, count = blocks * SPACED, blocks * BLOCK
    return call(
        entry_kernel,
        [((rows, tiles, spaced(REACH), LANES), f32), ((rows, 1, tiles * LANES), f32)],
        (p, keep, seg, x_own, g_own, hfv, hrv, start),
        waits=waits,
        scratch=[((tiles, length, LANES), f32)] + [((tiles, count, LANES), f32)] * 2,
        name="entry",
    )


def backward_kernel(
    where_ref, p_ref, keep_ref, seg_ref, lead_ref, first_ref, x_ref, g_ref, hfv_ref, hrv_ref, carry_ref, vectors_ref,
    gp_ref, hidden_ref, high_ref, sums_ref, final_ref, means_ref,
    prev_ref, a_ref, b_ref, gg_ref, e_ref, omf_ref, dr_ref, d_ref,
):
    rows, slots = p_ref.shape[:2]
    tiles = slots // 3
    blocks = p_ref.shape[2] // SPACED
    hfv, hrv = tiles_of(hfv_ref, tiles), tiles_of(hrv_ref, tiles)
    devices, block = BLOCK // g_ref.shape[2], g_ref.shape[2]
    sums_ref[...] = jnp.zeros_like(sums_ref)
    for r in range(rows):
        prev_ref[...] = seg_ref[r]

        @pl.when(where_ref[0] == 0)
        def _():
            prev_ref[:, : spaced(LEAD), :] = lead_ref[r]

        @pl.when(where_ref[0] != 0)
        def _():
            prev_ref[:, : spaced(REACH), :] = first_ref[r]

        @pl.loop(0, blocks)
        def _(k):
            out = pl.ds(pl.multiple_of(k * BLOCK, BLOCK), BLOCK)
            for i in range(tiles):
                t = block_terms(p_ref, keep_ref, prev_ref, x_ref, g_ref, hfv, hrv, r, k, i)
                lanes = slice(LANES * i, LANES * (i + 1))
                for n in range(devices):
                    hidden_ref[k * devices + n, r, :, lanes] = t["hidden"][n * block : (n + 1) * block].astype(bf16)
                high_ref[r, i, out, :] = t["high"].astype(bf16)
                a_ref[i, out, :], b_ref[i, out, :] = composed(t["a"], t["b"])
                for ref, name in zip((gg_ref, e_ref, omf_ref, dr_ref), ("gg", "e", "omf", "dr")):
                    ref[i, out, :] = t[name]
                final_ref[r, :, lanes] = t["cell"][-1:]

        run_back(a_ref, b_ref, d_ref, tiles_of(carry_ref.at[r], tiles), blocks * BLOCK)

        @pl.loop(0, blocks)
        def _(k):
            at = pl.ds(pl.multiple_of(k * SPACED, 8), BLOCK)
            out = pl.ds(pl.multiple_of(k * BLOCK, BLOCK), BLOCK)
            first, second = jnp.zeros((BLOCK, LANES), f32), jnp.zeros((BLOCK, LANES), f32)
            for i in range(tiles):
                prev = prev_ref[i, at, :]
                u = entering(a_ref[i, out, :], b_ref[i, out, :], d_ref[i, out, :]) + gg_ref[i, out, :]
                df, dr = u * e_ref[i, out, :], dr_ref[i, out, :]
                dc = u * omf_ref[i, out, :]
                for m, value in enumerate((dc, df, dr)):
                    slot = m * tiles + i
                    lane = lax.rem(slot + slots - where_ref[4], slots) * LANES
                    gp_ref[r, out, pl.ds(pl.multiple_of(lane, LANES), LANES)] = value.astype(bf16)
                    first += value * vectors_ref[slot, 0:1, :]
                    second += value * ((1.0 if m == 0 else 2.0) * p_ref[r, slot, at, :] - vectors_ref[slot, 1:2, :])
                lanes = slice(LANES * i, LANES * (i + 1))
                for m, value in enumerate((df * prev, dr * prev, df, dr)):
                    sums_ref[m : m + 1, lanes] += jnp.sum(value, axis=0, keepdims=True)
                for m, value in enumerate((dc, df, dr)):
                    lane = lax.rem(m * tiles + i + slots - where_ref[4], slots) * LANES
                    at_lane = pl.ds(pl.multiple_of(lane, LANES), LANES)
                    sums_ref[7:8, at_lane] += jnp.sum(value, axis=0, keepdims=True)
            means_ref[r, 0, out, :] = first
            means_ref[r, 1, out, :] = second


def backward(where, p, keep, seg, lead, first, x_own, g_own, hfv, hrv, carry, vectors):
    rows, slots, length, _ = p.shape
    tiles = slots // 3
    tokens = length // SPACED * BLOCK
    width = tiles * LANES
    return call(
        backward_kernel,
        [
            ((rows, tokens, 3 * width), bf16),
            (g_own.shape, bf16),
            ((rows, tiles, tokens, LANES), bf16),
            ((8, 3 * width), f32),
            ((rows, 1, width), f32),
            ((rows, 2, tokens, LANES), f32),
        ],
        (p, keep, seg, lead, first, x_own, g_own, hfv, hrv, carry, vectors),
        (where,),
        scratch=[((tiles, length, LANES), f32)] + [((tiles, tokens, LANES), f32)] * 7,
        name="backward",
    )


def weight_back_kernel(normed_ref, gp_ref, sums_ref, *refs, part, group, cuts):
    count = sum(len(rows) for rows in cuts)
    w_refs, (by_feature_ref, *out_refs) = refs[: len(refs) - count - 1], refs[len(refs) - count - 1 :]
    total, _, features = normed_ref.shape
    row_block = features // 2 // group
    columns = out_refs[0].shape[2]
    span = 2 * LANES
    devices = span // row_block
    lane_tiles = gp_ref.shape[2] // LANES
    for k in range(group // devices):
        lane = slice(part * (features // 2) + k * span, part * (features // 2) + (k + 1) * span)
        p = sum(
            lax.dot_general(normed_ref[r, :, lane], gp_ref[r], (((0,), (0,)), ((), ())), preferred_element_type=f32)
            for r in range(total)
        )
        first = w_refs[0].shape[0]
        w = [w_refs[0][lane.start : min(lane.stop, first), :]] if lane.start < first else []
        if lane.stop > first:
            w.append(w_refs[1][max(lane.start - first, 0) : lane.stop - first, :])
        w = jnp.concatenate(w).astype(f32)
        for m, value in enumerate((p * w, w * sums_ref[7:8, :])):
            value = functools.reduce(jnp.add, [value[:, LANES * j : LANES * (j + 1)] for j in range(lane_tiles)])
            by_feature_ref[m : m + 1, k * span : (k + 1) * span] = jnp.sum(jnp.transpose(value), axis=0, keepdims=True)
        p = p.astype(bf16)
        outs = iter(out_refs)
        for split, rows in enumerate(cuts):
            start = 0
            for step in rows:
                out_ref = next(outs)
                for n in range(devices):
                    row = n * row_block + start
                    out_ref[k * devices + n, :step] = p[row : row + step, split * columns : (split + 1) * columns]
                    if out_ref.shape[1] > step:
                        out_ref[k * devices + n, step:] = jnp.zeros((out_ref.shape[1] - step, columns), bf16)
                start += step


def weight_back(normed, gp, sums, weights, part, group, cuts, waits, spare=0):
    features = normed.shape[2]
    columns = gp.shape[2] // len(cuts)
    kernel = functools.partial(weight_back_kernel, part=part, group=group, cuts=cuts)
    out_shape = [((2, features // 2), f32)] + [((group, step, columns), bf16) for rows in cuts for step in rows]
    (count, step, width), dtype = out_shape[-1]
    out_shape[-1] = ((count, step + spare, width), dtype)
    return call(kernel, out_shape, (normed, gp, sums, *weights), waits=waits, name="weight_back")


def norm_back_kernel(where_ref, stats_ref, means_ref, gp_ref, gain_ref, *refs, orders, with_hidden):
    count = len(orders[0])
    x_refs, refs = refs[: 2 * count], refs[2 * count :]
    *w_refs, high_ref, hidden_ref = refs[:-10]
    all_out_refs, (some_ref, gn_ref) = refs[-10:-2], refs[-2:]
    half_count, total, block, _ = all_out_refs[0].shape
    features = gain_ref.shape[1]
    half_width = features // 2
    together = gn_ref.shape[0] // block
    for odd in (1, 0):
        out_refs = all_out_refs[4 * (1 - odd) : 4 * (2 - odd)]
        for r in range(total):
            for d in range(0, count, together):
                tokens = []
                for n in range(together):
                    place = where_ref[3] ^ (orders[0][d + n] | odd)
                    tokens.append(pl.ds(pl.multiple_of(place * block, 16), block))
                    some_ref[n * block : (n + 1) * block, :] = gp_ref[r, tokens[n], :]
                lane = 0
                for w_ref in w_refs:
                    rows = w_ref.shape[0]
                    gn_ref[:, lane : lane + rows] = lax.dot_general(
                        some_ref[...], w_ref[...], (((1,), (1,)), ((), ())), preferred_element_type=f32
                    )
                    lane += rows
                for n in range(together):
                    x_ref = x_refs[orders[0][d + n] | odd]
                    mean, inv = stats_ref[r, 0, tokens[n], :], stats_ref[r, 1, tokens[n], :]
                    first, second = (
                        jnp.sum(means_ref[r, m, tokens[n], :], axis=-1, keepdims=True) * (1.0 / features)
                        for m in range(2)
                    )
                    slope = inv * inv * second
                    rest = inv * first - slope * mean
                    for part in range(2):
                        at_d = orders[part].index(orders[0][d + n])
                        out_ref = out_refs[2 * part + at_d // half_count]
                        start = pl.multiple_of((where_ref[0] ^ part) * half_width, LANES)
                        if with_hidden:
                            high = high_ref[r, where_ref[0] ^ part, tokens[n], :].astype(f32)
                        for j in range(half_width // LANES):
                            at = slice(part * half_width + LANES * j, part * half_width + LANES * (j + 1))
                            value = inv * (gn_ref[n * block : (n + 1) * block, at] * gain_ref[:, at])
                            x = x_ref[r, :block, pl.ds(start + LANES * j, LANES)].astype(f32)
                            value -= slope * x + rest
                            if with_hidden:
                                value += jnp.where(where_ref[3] == j, high, 0.0)
                            out_ref[at_d % half_count, r, :, LANES * j : LANES * (j + 1)] = value.astype(bf16)
                        if with_hidden:
                            hidden = hidden_ref[where_ref[3] ^ (orders[0][d + n] | odd), r]
                            out_ref[at_d % half_count, r, :, half_width:] = hidden[:, LANES * part : LANES * (part + 1)]


def norm_back(where, blocks, orders, stats, means, gp, weights, gain, high, hidden, with_hidden, waits):
    rows, block, features = blocks[0].shape
    block -= STATS
    together = 2 * LANES // block
    out = call(
        functools.partial(norm_back_kernel, orders=orders, with_hidden=with_hidden),
        [((len(blocks) // 4, rows, block, features // 2 + with_hidden * LANES), bf16)] * 8,
        (stats, means, gp, gain, *blocks, *weights, high, hidden), (where,), waits,
        scratch=[((together * block, gp.shape[2]), bf16), ((together * block, features), f32)],
        name="norm_back",
    )
    return out[:4], out[4:]


def totals_kernel(where_ref, sums_ref, own_ref, other_ref, gain_ref, shift_ref, out_ref, *, chunk):
    half_width = own_ref.shape[1]
    out_ref[...] = jnp.zeros_like(out_ref)
    for i in range(2):
        lane = pl.ds(pl.multiple_of(i * chunk + where_ref[3] * LANES, LANES), LANES)
        out_ref[0:4, lane] = sums_ref[0:4, LANES * i : LANES * (i + 1)]
    for part, ref in enumerate((own_ref, other_ref)):
        lane = pl.ds(pl.multiple_of((where_ref[0] ^ part) * half_width, LANES), half_width)
        at = slice(part * half_width, (part + 1) * half_width)
        out_ref[4:5, lane] = (ref[0:1, :] - shift_ref[:, at] * ref[1:2, :]) / gain_ref[:, at]
        out_ref[5:6, lane] = ref[1:2, :]


def bf16_parts(row):
    rows = []
    for _ in range(3):
        upper = lax.reduce_precision(row, 8, 7)
        rows.append(upper.astype(bf16))
        row = row - upper
    return rows


def local(inputs, weight, gain, shift, forget_vec, reset_vec, forget_bias, reset_bias, initial, resets, grad_out):
    rows, block_len, features = inputs.shape
    row_block, columns_here = weight.shape
    sections = lax.axis_size("fsdp")
    ranks = lax.axis_size("dp")
    group = sections // 2
    tokens = group * block_len
    index = lax.axis_index("fsdp")
    half, place = index // group, index % group
    rank = lax.axis_index("dp")
    first_half = half == 0
    groups = [list(range(group)), list(range(group, sections))]
    chunk = math.gcd(features, columns_here)
    chunks, piece = features // chunk, chunk // group
    width = chunks * piece
    tiles = width // LANES
    slots = 3 * tiles
    parts = columns_here // chunk
    columns = parts * piece
    aligned = piece == LANES and chunks == 2
    paired = ranks == 2 and aligned
    turn = rank * (columns // LANES) if paired else jnp.zeros_like(rank)
    where = jnp.stack([half, rank, index % 2, place, turn]).astype(jnp.int32)
    bits = [1 << b for b in range(1, group.bit_length() - 1)]
    ways = (bits[::-1], bits)
    orders = []
    for way in ways:
        order = [0]
        for bit in way:
            order += [d | bit for d in order]
        orders.append(order)

    def across(value):
        return lax.ppermute(value, "fsdp", [(j, (j + group) % sections) for j in range(sections)])

    def flipped(value, bit):
        return lax.ppermute(value, "fsdp", [(j, j ^ bit) for j in range(sections)])

    def swapped(value):
        return lax.ppermute(value, "dp", [(0, 1), (1, 0)])

    def shared(value):
        return lax.all_to_all(value, "fsdp", 0, 0, tiled=True, axis_index_groups=groups)

    def own(vector):
        return lax.dynamic_index_in_dim(vector.reshape(-1, chunks, group, piece), place, 2, False).reshape(-1, width)

    def halves_turned(vector):
        low, high = vector[..., : features // 2], vector[..., features // 2 :]
        return jnp.concatenate([jnp.where(first_half, low, high), jnp.where(first_half, high, low)], axis=-1)

    def dealt(value, waits=()):
        if aligned:
            return deal(value, group, waits)
        n, wide = value.shape
        return value.reshape(n, wide // chunk, group, piece).transpose(2, 0, 1, 3).reshape(group, n, wide // group)

    def collected(pieces, dtype, waits=()):
        if aligned:
            return collect(pieces, dtype, waits)
        wide = pieces[0].shape[2]
        back = lambda v: v.reshape(group, -1, wide // piece, piece).transpose(1, 2, 0, 3).reshape(-1, wide * group)
        return jnp.concatenate([back(v) for v in pieces]).astype(dtype)

    mine = shared(dealt(weight))
    theirs = across(mine)
    beside = swapped(mine) if paired else mine
    blocks = {0: stats(inputs, (1 - resets).astype(f32)[:, None, :], ())}
    for bit in bits[::-1]:
        blocks |= {d | bit: flipped(fence(value, (beside,)) if d else value, bit) for d, value in blocks.items()}
    blocks = {d: fence(value, (theirs, beside)) for d, value in blocks.items()}
    blocks |= {d | 1: flipped(value, 1) for d, value in blocks.items()}
    blocks = [blocks[d] for d in range(group)]
    early_rows = features // 2
    if paired:
        early, late = [mine, beside], [theirs, swapped(theirs)]
    else:
        early, late = (
            [lax.all_gather(v.reshape(-1, columns), "dp", axis=1, tiled=True)] for v in (mine, theirs)
        )
    hfv, hrv = 0.5 * own(forget_vec), 0.5 * own(reset_vec)
    bias = jnp.concatenate([jnp.zeros((1, width), f32), own(forget_bias), own(reset_bias)]).reshape(-1, 1, LANES)
    gain_row, shift_row = halves_turned(gain)[None], halves_turned(shift)[None]
    vector_rows = [*bf16_parts(gain_row), *bf16_parts(shift_row)]
    vector_rows = jnp.pad(jnp.concatenate(vector_rows), ((0, 10), (0, 0)))
    g_own = shared(dealt(grad_out.reshape(-1, features)).reshape(group, rows, block_len, width))
    normed, token_stats, keep, *x_own = norm(where, blocks, gain_row, shift_row, aligned, (g_own,))
    if aligned:
        x_own = x_own[0]
    else:
        in_order = jnp.stack(blocks)[place ^ jnp.arange(group)][:, :, :block_len].swapaxes(0, 1)
        x_own = own(in_order.reshape(rows * tokens, features)).reshape(rows, tokens, tiles, LANES).swapaxes(1, 2)
    some, some_vectors, early_weight = project(where, normed, vector_rows, early, early_rows, slots)
    p, seg, lead, end, lead_end, vectors, late_weight = blocks_forward(
        where, normed, vector_rows, some, some_vectors, bias, keep, hfv, own(initial)[:, None, :], late,
        features - early_rows,
    )
    weights = (early_weight, late_weight)
    start = across(end)
    lead = lead_forward(p, keep, hfv, lead_end, lead)
    first, back = entry(p, keep, seg, x_own, g_own, hfv, hrv, start, ())
    carry = jnp.where(first_half, across(back), 0.0)
    gp, hidden_own, high_own, sums, final, means = backward(
        where, p, keep, seg, lead, first, x_own, g_own, hfv, hrv, carry, vectors
    )

    mask = (jnp.arange(group) == place)[:, None]

    splits = 2 if paired else 1
    by_feature_other, *away = weight_back(normed, gp, sums, weights, 1, group, [(row_block,)] * splits, (), SPARE * paired)
    away_got = swapped(away[1]) if paired else None

    sent, kept = norm_back(
        where, blocks, orders, token_stats, means, gp, weights, gain_row, high_own, hidden_own, aligned,
        (by_feature_other,),
    )
    if not aligned:
        spread = high_own.swapaxes(1, 2).reshape(rows, group, block_len, chunks, 1, piece).swapaxes(0, 1)
        spread = jnp.where(mask, spread.astype(f32), 0.0).reshape(group, rows, block_len, features)
        spread = halves_turned(spread)[place ^ jnp.arange(group)]
        halves = (spread[..., : features // 2], spread[..., features // 2 :])
        n = group // 4

        def with_high(arrays, odd):
            add = [half[d | odd] for half, order in zip(halves, orders) for d in order]
            return [(v.astype(f32) + jnp.stack(add[i * n : (i + 1) * n])).astype(bf16) for i, v in enumerate(arrays)]

        sent, kept = with_high(sent, 1), with_high(kept, 0)
    got = [flipped(value, 1) for value in sent]
    if paired:
        away = added(away[0], away_got, kept[:1])
    else:
        away = lax.psum_scatter(away[0], "dp", scatter_dimension=2, tiled=True)
    z_got = across(away)
    kept, sent = halve(kept, got, features // 2)
    bit_pairs = list(zip(*(w[::-1] for w in ways)))
    got = [flipped(value, bit) for value, bit in zip(sent, bit_pairs.pop(0))]
    cuts = [(row_block,), (row_block // 2,) * 2][:splits]
    by_feature_own, *here = weight_back(normed, gp, sums, weights, 0, group, cuts, (away,))
    if paired:
        here_got = [swapped(value) for value in here[1:]]
    else:
        here = lax.psum_scatter(here[0], "dp", scatter_dimension=2, tiled=True)
    if aligned:
        totals = call(
            functools.partial(totals_kernel, chunk=chunk), [((8, features), f32)],
            (sums, by_feature_own, by_feature_other, gain_row, shift_row), (where,), name="totals",
        )[0]
    else:
        spread = jnp.where(mask, sums[:4, :width].reshape(4, chunks, 1, piece), 0.0).reshape(4, features)
        product, shift_sum = jnp.concatenate([by_feature_own, by_feature_other], axis=1)
        gain_sum = (product - shift_row[0] * shift_sum) / gain_row[0]
        totals = jnp.concatenate([spread, halves_turned(jnp.stack([gain_sum, shift_sum]))], axis=0)
    for way in bit_pairs:
        kept, sent = halve(kept, got, features // 2)
        got = [flipped(value, bit) for value, bit in zip(sent, way)]
    sources = []
    for way in ways:
        sources.append([0])
        for bit in (1, *way[::-1]):
            sources[-1] += [d | bit for d in sources[-1]]
    grad_inputs, *hidden = finish(where, kept, got, features, sources)
    if aligned:
        hidden = hidden[0]
    else:
        hidden = collected([shared(hidden_own).reshape(group, -1, width)], bf16).reshape(rows, block_len, features)
    for bit in [1 << b for b in range(group.bit_length() - 1)]:
        totals = added(totals, flipped(totals, bit))
    waits = (*got, totals)
    value = merge(here[0], here_got, z_got, waits) if paired else added(here, z_got, waits)
    grad_weight = collected([shared(value)], f32)
    totals = added(totals, swapped(totals)) if ranks == 2 else lax.psum(totals, "dp")
    totals = added(totals, across(totals), (grad_inputs,))

    own_width = features // sections
    if piece == own_width and chunks == 2:
        final = final[:, 0]
        low_part = lax.ppermute(final[:, :piece], "fsdp", [(j + group, j) for j in range(group)])
        final_state = jnp.where(first_half, low_part, final[:, piece:])
    else:
        spread = jnp.where(mask, final.reshape(rows, chunks, 1, piece), 0.0).reshape(rows, features)
        spread = lax.psum(jnp.where(first_half, 0.0, spread), "fsdp")
        final_state = lax.dynamic_slice_in_dim(spread, index * own_width, own_width, 1)

    return (hidden, grad_inputs, final_state, grad_weight, *[totals[i] for i in range(6)])


def solution(mesh):
    in_specs = (
        P("dp", "fsdp", None), P("fsdp", "dp"), P(), P(), P(), P(), P(), P(),
        P("dp", None), P("dp", "fsdp"), P("dp", "fsdp", None),
    )
    out_specs = (
        P("dp", "fsdp", None), P("dp", "fsdp", None), P("dp", "fsdp"), P("fsdp", "dp"), P(), P(), P(), P(), P(), P(),
    )
    return jax.shard_map(local, mesh=mesh, in_specs=in_specs, out_specs=out_specs, check_vma=False)
```
